32 devices in a mesh: sec: 2 (over y), dp: 4 (over x, core), tp: 4 (over z).
Axes of the slice: x: 2, y: 2, z: 4, core: 2. Of those that a mesh axis runs over, the one named last changes fastest.
Arguments:
- latents: bfloat16 [32, 64, 1280], P(('dp', 'tp')), may hold values from -6 to 6
- timesteps: int32 [32], P(('dp', 'tp')), may hold values from 0 to 24
- prompt_ids: int32 [32], P(('dp', 'tp')), may hold values from 0 to 63
- prompt_table: bfloat16 [64, 1280], replicated, may hold values from -6 to 6
- gains: float32 [2, 1280], replicated, may hold values from 0.5 to 1.5
- w_in: bfloat16 [2, 1280, 5120], P('sec', None, 'tp'), may hold values from -0.15625 to 0.15625
- w_out: bfloat16 [2, 1280, 5120], P('sec', None, 'tp'), may hold values from -0.078125 to 0.078125
Outputs:
- grad_in: float32 [1280, 5120], P(('sec', 'dp'), 'tp')
- grad_out: float32 [1280, 5120], P(('sec', 'dp'), 'tp')
The draws below stay inside these ranges and needn't reach their ends.
All inputs are finite; a program needn't handle non-finite values.
Results may differ from the reference program's by a relative error of at most 0.03.
Values may be sent and summed in bfloat16 or wider, within the bound.
No kernel may reach another device: no remote copies, remote signals or barrier semaphores. Data moves between devices by JAX's collectives and lax.ppermute only.
A program may use at most 64 MiB of HBM per device.

```python
import math
import jax
import jax.numpy as jnp
from jax import lax

D = 1280
H = 5120
TOK = 64
STEPS = 50
PROMPTS = 64
IMAGES = 32
N_TP = 4


def touch_ends(drawn, stream_key, smallest, largest):
    shape = drawn.shape
    index_at = [jax.random.randint(jax.random.fold_in(stream_key, axis), (), 0, shape[axis]) for axis in range(len(shape))]
    drawn = drawn.at[tuple(index_at)].set(smallest)
    longest = shape.index(max(shape))
    index_at[longest] = (index_at[longest] + 1) % shape[longest]
    return drawn.at[tuple(index_at)].set(largest)


def levels(rng, shape, pieces, low, largest):
    loudness, own = 1.0, jax.random.fold_in(rng, 6)
    for position, shards_of in pieces:
        heights = jnp.exp(jax.random.uniform(jax.random.fold_in(own, position), (shards_of,), jnp.float32, low / len(pieces), largest / len(pieces)))
        loudness = loudness * jnp.repeat(heights, shape[position] // shards_of).reshape([-1 if axis == position else 1 for axis in range(len(shape))])
    return loudness


def bell_draw(own_key, extent, width, bound, cuts=(), kind=jnp.bfloat16):
    factor_of = levels(own_key, extent, cuts, -0.22, 0.18) if cuts else 1.0
    entries = jax.random.normal(own_key, extent, jnp.float32) * width * factor_of
    return jnp.minimum(jnp.maximum(entries, -bound), bound).astype(kind)


def setup_inputs(seed: int = 0) -> dict:
    key_of = jax.random.split(jax.random.key(seed), 8)
    latents = bell_draw(key_of[0], (IMAGES, TOK, D), 1.0, 6.0, ((0, 16),))
    timesteps = touch_ends(jax.random.randint(key_of[1], (IMAGES,), 0, STEPS // 2), jax.random.fold_in(key_of[1], 1), 0, (STEPS // 2) - 1).astype(jnp.int32)
    prompt_ids = touch_ends(jax.random.randint(key_of[2], (IMAGES,), 0, PROMPTS), jax.random.fold_in(key_of[2], 1), 0, PROMPTS - 1).astype(jnp.int32)
    prompt_table = bell_draw(key_of[3], (PROMPTS, D), 1.0, 6.0)
    gains = jnp.clip(1.0 + 0.1 * jax.random.normal(key_of[4], (2, D), jnp.float32), 0.5, 1.5)
    w_in = bell_draw(key_of[5], (2, D, H), D ** -0.5, 0.15625, ((0, 2), (2, 4)))
    w_out = bell_draw(key_of[6], (2, D, H), H ** -0.5, 0.078125, ((0, 2), (2, 4)))
    return {"latents": latents, "timesteps": timesteps, "prompt_ids": prompt_ids, "prompt_table": prompt_table, "gains": gains, "w_in": w_in, "w_out": w_out}


EPS = 1e-06

def gelu_slope(value):
    return 0.5 * (1.0 + lax.erf(value / math.sqrt(2.0))) + value * jnp.exp(-0.5 * value * value) / math.sqrt(2.0 * math.pi)

def normed(rows, gain):
    scale = lax.rsqrt(lax.optimization_barrier(jnp.mean(rows * rows, axis=-1, keepdims=True)) + EPS)
    return ((rows * scale * gain).astype(jnp.bfloat16), scale)

def blocked_sum(left, right):
    share = left.shape[1] // N_TP
    total = jnp.zeros((left.shape[0], right.shape[0]), jnp.float32)
    for part in range(N_TP):
        piece = lax.dot_general(left[:, part * share:(part + 1) * share], right[:, part * share:(part + 1) * share], (((1,), (1,)), ((), ())), preferred_element_type=jnp.float32)
        rounded = lax.optimization_barrier(piece.astype(jnp.bfloat16))
        total = total + rounded.astype(jnp.float32)
    return total

def forward(rows, gain, weight_in, weight_out):
    base = rows.astype(jnp.float32)
    xn, scale = normed(base, gain)
    hp = jnp.dot(xn, weight_in, preferred_element_type=jnp.float32)
    act = jax.nn.gelu(hp, approximate=False).astype(jnp.bfloat16)
    return (base + blocked_sum(act, weight_out), xn, hp, act, scale)

def score_of(pooled, text):
    unit_img = pooled * lax.rsqrt(lax.optimization_barrier(jnp.mean(pooled * pooled, axis=-1, keepdims=True)) + EPS)
    unit_txt = text * lax.rsqrt(lax.optimization_barrier(jnp.mean(text * text, axis=-1, keepdims=True)) + EPS)
    return 100.0 * lax.optimization_barrier(jnp.sum(unit_img * unit_txt, axis=-1)) / pooled.shape[-1]

def reference(latents, timesteps, prompt_ids, prompt_table, gains, w_in, w_out):
    rows = latents.reshape(IMAGES * TOK, D)
    theta = math.pi / 2.0 * (timesteps.astype(jnp.float32) + 1.0) / (STEPS + 1.0)
    alpha = jnp.repeat(jnp.cos(theta), TOK)[:, None]
    sigma = jnp.repeat(jnp.sin(theta), TOK)[:, None]
    eps, xn0, hp0, act0, unused = forward(rows, gains[0], w_in[0], w_out[0])
    images = ((rows.astype(jnp.float32) - sigma * eps) / alpha).astype(jnp.bfloat16)
    seen, xn1, hp1, act1, scale1 = forward(images, gains[1], w_in[1], w_out[1])
    pooled = lax.optimization_barrier(jnp.mean(seen.reshape(IMAGES, TOK, D), axis=1))
    text = prompt_table[prompt_ids].astype(jnp.float32)
    g_pooled = jax.grad(lambda p: -jnp.sum(score_of(p, text)))(pooled)
    g_mean = g_pooled / TOK
    g_tok = g_mean.astype(jnp.bfloat16)
    g_h1 = jnp.dot(g_tok, w_out[1], preferred_element_type=jnp.float32)
    g_hp1 = (jnp.repeat(g_h1, TOK, axis=0) * gelu_slope(hp1)).astype(jnp.bfloat16)
    g_xn1 = blocked_sum(g_hp1, w_in[1])
    base1 = images.astype(jnp.float32)
    weighted = gains[1] * g_xn1
    g_norm = scale1 * weighted - base1 * scale1 ** 3 * lax.optimization_barrier(jnp.mean(base1 * weighted, axis=-1, keepdims=True))
    g_images = (jnp.repeat(g_mean, TOK, axis=0) + g_norm).astype(jnp.bfloat16)
    g_eps = (-(sigma / alpha) * g_images.astype(jnp.float32)).astype(jnp.bfloat16)
    grad_out = lax.dot_general(g_eps, act0, (((0,), (0,)), ((), ())), preferred_element_type=jnp.float32)
    g_hp0 = (jnp.dot(g_eps, w_out[0], preferred_element_type=jnp.float32) * gelu_slope(hp0)).astype(jnp.bfloat16)
    grad_in = lax.dot_general(xn0, g_hp0, (((0,), (0,)), ((), ())), preferred_element_type=jnp.float32)
    return (grad_in, grad_out)
```

```python
import math

import jax
import jax.numpy as jnp
from jax import lax
from jax.sharding import PartitionSpec as P

STEPS = 50


EPS = 1e-06


def rotated(value, axis, steps):
    count = lax.axis_size(axis)
    return lax.ppermute(value, axis, [(i, (i + steps) % count) for i in range(count)])


def sibling(value):
    count = lax.axis_size("dp")
    return lax.ppermute(value, "dp", [(i, i ^ 1) for i in range(count)])


def gelu_slope(value):
    return 0.5 * (1.0 + lax.erf(value / math.sqrt(2.0))) + value * jnp.exp(
        -0.5 * value * value
    ) / math.sqrt(2.0 * math.pi)


def normed(rows, gain):
    scale = lax.rsqrt(jnp.mean(rows * rows, axis=-1, keepdims=True) + EPS)
    return ((rows * scale * gain).astype(jnp.bfloat16), scale)


def score_of(pooled, text):
    unit_img = pooled * lax.rsqrt(jnp.mean(pooled * pooled, axis=-1, keepdims=True) + EPS)
    unit_txt = text * lax.rsqrt(jnp.mean(text * text, axis=-1, keepdims=True) + EPS)
    return 100.0 * jnp.sum(unit_img * unit_txt, axis=-1) / pooled.shape[-1]


def dot_nn(a, b):
    return jnp.dot(a, b, preferred_element_type=jnp.float32)


def dot_nt(a, b):
    return lax.dot_general(a, b, (((1,), (1,)), ((), ())), preferred_element_type=jnp.float32)


def dot_tn(a, b):
    return lax.dot_general(a, b, (((0,), (0,)), ((), ())), preferred_element_type=jnp.float32)


def gather_parts(piece):
    return [piece] + [rotated(piece, "tp", k) for k in range(1, lax.axis_size("tp"))]


def reduce_parts(parts):
    total = parts[0].astype(jnp.float32)
    for k in range(1, len(parts)):
        total = total + rotated(parts[k].astype(jnp.bfloat16), "tp", -k).astype(jnp.float32)
    return total


def from_other_section(weight, core):
    half = weight.shape[0] // 2
    piece = lax.dynamic_slice_in_dim(weight, core * half, half, 0)
    got = lax.ppermute(piece, "sec", [(0, 1), (1, 0)])
    beside = sibling(got)
    return jnp.where(
        core == 0, jnp.concatenate([got, beside], 0), jnp.concatenate([beside, got], 0)
    )


def sum_over_dp(partial, core):
    groups = lax.axis_size("dp") // 2
    rows = partial.shape[0] // (2 * groups)
    place = lax.axis_index("dp") // 2
    cut = partial.astype(jnp.bfloat16).reshape(groups, 2, rows, -1)
    away = lax.dynamic_index_in_dim(cut, 1 - core, 1, keepdims=False)
    keep = lax.dynamic_index_in_dim(cut, core, 1, keepdims=False)
    chip = keep.astype(jnp.float32) + sibling(away).astype(jnp.float32)
    total = lax.dynamic_index_in_dim(chip, place, 0, keepdims=False)
    sent = chip.astype(jnp.bfloat16)
    count = 2 * groups
    for k in range(1, groups):
        part = lax.dynamic_index_in_dim(sent, (place + k) % groups, 0, keepdims=False)
        total = total + rotated(part, "dp", 2 * k).astype(jnp.float32)
    return total


def on_device(latents, timesteps, prompt_ids, prompt_table, gains, w_in, w_out):
    count, tokens, width = latents.shape
    half = count // 2
    segment = lax.axis_index("sec")
    first = segment == 0
    core = lax.axis_index("dp") % 2
    own_in = w_in[0]
    own_out = w_out[0]
    theta = math.pi / 2.0 * (timesteps.astype(jnp.float32) + 1.0) / (STEPS + 1.0)
    alpha = jnp.cos(theta)[:, None, None]
    sigma = jnp.sin(theta)[:, None, None]

    flat = latents.reshape(count * tokens, width)
    lat_parts = gather_parts(flat)
    other_in = from_other_section(own_in, core)
    other_out = from_other_section(own_out, core)

    onehot = (
        prompt_ids[:, None] == jnp.arange(prompt_table.shape[0], dtype=jnp.int32)[None, :]
    ).astype(jnp.bfloat16)
    text = dot_nn(onehot, prompt_table).astype(jnp.bfloat16)
    text_mine = jnp.where(first, text[half:], text[:half])
    text_all = jnp.concatenate(gather_parts(text_mine), 0).astype(jnp.float32)

    eps_parts = []
    for part in lat_parts:
        xn, unused = normed(part.astype(jnp.float32), gains[0])
        act = jax.nn.gelu(dot_nn(xn, own_in), approximate=False).astype(jnp.bfloat16)
        eps_parts.append(dot_nt(act, own_out))
    eps_mix = reduce_parts(eps_parts).reshape(count, tokens, width)
    base = latents.astype(jnp.float32)
    images = ((base - sigma * (base + eps_mix)) / alpha).astype(jnp.bfloat16)

    arrived = lax.ppermute(images[:half], "sec", [(0, 1)])
    mine = jnp.where(first, images[half:], arrived)
    ratio = jnp.where(first, (sigma / alpha)[half:], (sigma / alpha)[:half])
    w1_in = jnp.where(first, other_in, own_in)
    w1_out = jnp.where(first, other_out, own_out)
    mine_rows = mine.reshape(half * tokens, width)
    seen_all = jnp.concatenate(gather_parts(mine_rows), 0).astype(jnp.float32)
    n_img = seen_all.shape[0] // tokens
    xn1, unused = normed(seen_all, gains[1])
    hp1 = dot_nn(xn1, w1_in)
    hidden = hp1.shape[1]
    act1 = jax.nn.gelu(hp1, approximate=False)
    slope1 = gelu_slope(hp1)
    act_mean = jnp.mean(act1.reshape(n_img, tokens, hidden), axis=1).astype(jnp.bfloat16)
    pool_part = dot_nt(act_mean, w1_out)
    pool = pool_part
    n_tp = lax.axis_size("tp")
    by_owner = pool_part.reshape(n_tp, half, width)
    for k in range(1, n_tp):
        theirs = rotated(by_owner, "tp", k)
        pool = pool + jnp.roll(theirs, k, axis=0).reshape(n_img, width)
    pooled = pool + jnp.mean(seen_all.reshape(n_img, tokens, width), axis=1)
    g_pooled = jax.grad(lambda p: -jnp.sum(score_of(p, text_all)))(pooled)
    g_mean = g_pooled / tokens
    g_h = dot_nn(g_mean.astype(jnp.bfloat16), w1_out)
    g_hp1 = (
        (g_h[:, None, :] * slope1.reshape(n_img, tokens, hidden))
        .reshape(n_img * tokens, hidden)
        .astype(jnp.bfloat16)
    )
    g_parts = dot_nt(g_hp1, w1_in).reshape(n_tp, half * tokens, width)
    g_xn = reduce_parts([g_parts[k] for k in range(n_tp)])
    seen = mine_rows.astype(jnp.float32)
    scale1 = lax.rsqrt(jnp.mean(seen * seen, axis=-1, keepdims=True) + EPS)
    weighted = gains[1] * g_xn
    g_norm = scale1 * weighted - seen * scale1**3 * jnp.mean(
        seen * weighted, axis=-1, keepdims=True
    )
    g_images = (g_mean[:half, None, :] + g_norm.reshape(half, tokens, width)).astype(jnp.bfloat16)
    g_eps = (-ratio * g_images.astype(jnp.float32)).astype(jnp.bfloat16)

    g_mine = gather_parts(g_eps.reshape(half * tokens, width))
    g_theirs = [lax.ppermute(part, "sec", [(0, 1), (1, 0)]) for part in g_mine]
    g_rows = jnp.concatenate(g_mine + g_theirs, 0)

    w0_in = jnp.where(first, own_in, other_in)
    w0_out = jnp.where(first, own_out, other_out)
    late = half * tokens
    lat_b = jnp.concatenate([part[late:] for part in lat_parts], 0)
    lat_a = jnp.concatenate([part[:late] for part in lat_parts], 0)
    lat_rows = jnp.concatenate(
        [jnp.where(first, lat_b, lat_a), jnp.where(first, lat_a, lat_b)], 0
    )
    xn0, unused = normed(lat_rows.astype(jnp.float32), gains[0])
    hp0 = dot_nn(xn0, w0_in)
    act0 = jax.nn.gelu(hp0, approximate=False).astype(jnp.bfloat16)
    slope0 = gelu_slope(hp0)

    share = width // 2
    g_cols = lax.dynamic_slice_in_dim(g_rows, segment * share, share, 1)
    xn_cols = lax.dynamic_slice_in_dim(xn0, segment * share, share, 1)
    grad_out = sum_over_dp(dot_tn(g_cols, act0), core)
    g_hp0 = (dot_nn(g_rows, w0_out) * slope0).astype(jnp.bfloat16)
    grad_in = sum_over_dp(dot_tn(xn_cols, g_hp0), core)
    return (grad_in, grad_out)


def solution(mesh):
    in_specs = (
        P(("dp", "tp"), None, None),
        P(("dp", "tp")),
        P(("dp", "tp")),
        P(),
        P(),
        P("sec", None, "tp"),
        P("sec", None, "tp"),
    )
    out_specs = (P(("sec", "dp"), "tp"), P(("sec", "dp"), "tp"))
    return jax.shard_map(
        on_device, mesh=mesh, in_specs=in_specs, out_specs=out_specs, check_vma=False
    )
```

```python
import functools
import math

import jax
import jax.numpy as jnp
from jax import lax
from jax.experimental import pallas as pl
from jax.experimental.pallas import tpu as pltpu
from jax.sharding import PartitionSpec as P

STEPS = 50


EPS = 1e-06
VMEM_BYTES = 48 * 1024 * 1024
POOL_ROWS = 8


def rotated(value, axis, steps):
    count = lax.axis_size(axis)
    return lax.ppermute(value, axis, [(i, (i + steps) % count) for i in range(count)])


def swapped(value, axis, bit):
    count = lax.axis_size(axis)
    return lax.ppermute(value, axis, [(i, i ^ bit) for i in range(count)])


def gather_parts(piece):
    return [piece] + [rotated(piece, "tp", k) for k in range(1, lax.axis_size("tp"))]


def reduce_parts(parts):
    total = parts[0].astype(jnp.float32)
    for k in range(1, len(parts)):
        total = total + rotated(parts[k], "tp", -k).astype(jnp.float32)
    return total


def assemble_body(place_ref, *refs):
    pieces, out, sems = refs[:4], refs[4], refs[5]
    rows = pieces[0].shape[0]
    copies = []
    for q, piece in enumerate(pieces):
        start = pl.multiple_of((place_ref[0] ^ q) * rows, rows)
        copies.append(pltpu.make_async_copy(piece, out.at[pl.ds(start, rows), :], sems.at[q]))
    for copy in copies:
        copy.start()
    for copy in copies:
        copy.wait()


def from_other_section(weight):
    place = lax.axis_index("dp") % 4
    rows = weight.shape[0] // 4
    piece = lax.dynamic_slice_in_dim(weight, place * rows, rows, 0)
    got = swapped(piece, "sec", 1)
    beside = swapped(got, "dp", 1)
    across = swapped(got, "dp", 2)
    diagonal = swapped(across, "dp", 1)
    return pl.pallas_call(
        assemble_body,
        grid_spec=pltpu.PrefetchScalarGridSpec(
            num_scalar_prefetch=1,
            grid=(1,),
            in_specs=[pl.BlockSpec(memory_space=pl.ANY)] * 4,
            out_specs=pl.BlockSpec(memory_space=pl.ANY),
            scratch_shapes=[pltpu.SemaphoreType.DMA((4,))],
        ),
        out_shape=jax.ShapeDtypeStruct(weight.shape, weight.dtype),
        name="assemble",
    )(place.astype(jnp.int32)[None], got, beside, across, diagonal)


def gelu_pair(value):
    cdf = 0.5 * (1.0 + lax.erf(value * (1.0 / math.sqrt(2.0))))
    density = jnp.exp(-0.5 * value * value) * (1.0 / math.sqrt(2.0 * math.pi))
    return (value * cdf, cdf + value * density)


def normed(rows, gain):
    scale = lax.rsqrt(jnp.mean(rows * rows, axis=-1, keepdims=True) + EPS)
    return (rows * scale * gain).astype(jnp.bfloat16)


def dot_nn(a, b):
    return jnp.dot(a, b, preferred_element_type=jnp.float32)


def dot_nt(a, b):
    return lax.dot_general(a, b, (((1,), (1,)), ((), ())), preferred_element_type=jnp.float32)


def tile_of(hidden):
    for tile in (256, 128):
        if hidden % tile == 0:
            return tile
    return hidden


def whole(shape):
    return pl.BlockSpec(shape, lambda h, sel: (0,) * len(shape))


def columns(rows, tile):
    return pl.BlockSpec((rows, tile), lambda h, sel: (0, h))


def chosen(rows, tile, section):
    return pl.BlockSpec((rows, tile), lambda h, sel: (0, jnp.where(sel[0] == section, h, 0)))


def run(body, name, steps, sel, operands, in_specs, outs, out_specs, scratch, flops, elements=0):
    read = sum(x.size * x.dtype.itemsize for x in operands)
    written = sum(math.prod(o.shape) * o.dtype.itemsize for o in outs)
    return pl.pallas_call(
        body,
        grid_spec=pltpu.PrefetchScalarGridSpec(
            num_scalar_prefetch=1,
            grid=(steps,),
            in_specs=in_specs,
            out_specs=out_specs,
            scratch_shapes=scratch,
        ),
        out_shape=outs,
        compiler_params=pltpu.CompilerParams(
            dimension_semantics=("arbitrary",), vmem_limit_bytes=VMEM_BYTES
        ),
        cost_estimate=pl.CostEstimate(
            flops=flops, bytes_accessed=read + written, transcendentals=elements
        ),
        name=name,
    )(sel, *operands)


def bf16(*shape):
    return jax.ShapeDtypeStruct(shape, jnp.bfloat16)


def partial_body(count, sel_ref, *refs):
    parts, (gain, w_in, w_out) = refs[:count], refs[count : count + 3]
    outs, (xn, acc) = refs[count + 3 : 2 * count + 3], refs[2 * count + 3 :]
    h = pl.program_id(0)
    rows = parts[0].shape[0]

    @pl.when(h == 0)
    def _():
        for i, part in enumerate(parts):
            xn[i * rows : (i + 1) * rows, :] = normed(part[...].astype(jnp.float32), gain[...])
        acc[...] = jnp.zeros_like(acc)

    act, unused = gelu_pair(dot_nn(xn[...], w_in[...]))
    acc[...] += dot_nt(act.astype(jnp.bfloat16), w_out[...])

    @pl.when(h == pl.num_programs(0) - 1)
    def _():
        for i, out in enumerate(outs):
            out[...] = acc[i * rows : (i + 1) * rows, :].astype(jnp.bfloat16)


def block0_partials(parts, gain, w_in, w_out, sel):
    rows, width = parts[0].shape
    hidden = w_in.shape[1]
    tile, n = tile_of(hidden), len(parts)
    return run(
        functools.partial(partial_body, n),
        "block0_partial",
        hidden // tile,
        sel,
        [*parts, gain, w_in, w_out],
        [whole((rows, width))] * n
        + [whole((1, width)), columns(width, tile), columns(width, tile)],
        [bf16(rows, width)] * n,
        [whole((rows, width))] * n,
        [
            pltpu.VMEM((n * rows, width), jnp.bfloat16),
            pltpu.VMEM((n * rows, width), jnp.float32),
        ],
        4 * n * rows * width * hidden,
        n * rows * hidden,
    )


def state_body(sel_ref, part, gain, own_in, other_in, act, slope, xn_cols, xn):
    h = pl.program_id(0)
    rows = part.shape[0]
    late = rows // 2
    share = xn_cols.shape[0]
    first = sel_ref[0] == 0

    @pl.when(h == 0)
    def _():
        mine = pl.multiple_of(jnp.where(first, late, 0), late)
        theirs = pl.multiple_of(jnp.where(first, 0, late), late)
        for i, start in enumerate((mine, theirs)):
            xn[i * late : (i + 1) * late, :] = normed(
                part[pl.ds(start, late), :].astype(jnp.float32), gain[...]
            )
        cols = xn[:, pl.ds(pl.multiple_of(sel_ref[0] * share, share), share)]
        xn_cols[...] = cols.T

    def work(weight):
        value, grad = gelu_pair(dot_nn(xn[...], weight[...]))
        act[...] = value.astype(jnp.bfloat16)
        slope[...] = grad.astype(jnp.bfloat16)

    @pl.when(first)
    def _():
        work(own_in)

    @pl.when(jnp.logical_not(first))
    def _():
        work(other_in)


def block0_state(part, gain, own_in, other_in, sel):
    rows, width = part.shape
    hidden = own_in.shape[1]
    tile = tile_of(hidden)
    return run(
        state_body,
        "block0_state",
        hidden // tile,
        sel,
        [part, gain, own_in, other_in],
        [whole((rows, width)), whole((1, width)), chosen(width, tile, 0), chosen(width, tile, 1)],
        [bf16(rows, hidden), bf16(rows, hidden), bf16(width // 2, rows)],
        [columns(rows, tile), columns(rows, tile), whole((width // 2, rows))],
        [pltpu.VMEM((rows, width), jnp.bfloat16)],
        2 * rows * width * hidden,
        2 * rows * hidden,
    )


def reward_body(count, tokens, sel_ref, *refs):
    parts = refs[:count]
    gain, own_in, own_out, other_in, other_out = refs[count : count + 5]
    slopes = refs[count + 5 : 2 * count + 5]
    pools = refs[2 * count + 5 : 3 * count + 5]
    xn = refs[3 * count + 5]
    h = pl.program_id(0)
    rows = parts[0].shape[0]

    @pl.when(h == 0)
    def _():
        for i, part in enumerate(parts):
            xn[i * rows : (i + 1) * rows, :] = normed(part[...].astype(jnp.float32), gain[...])
            pools[i][...] = jnp.zeros_like(pools[i])

    def work(w_in, w_out):
        act, grad = gelu_pair(dot_nn(xn[...], w_in[...]))
        for i in range(count):
            slopes[i][...] = grad[i * rows : (i + 1) * rows, :].astype(jnp.bfloat16)
            row = lax.broadcasted_iota(jnp.int32, (POOL_ROWS, act.shape[1]), 0)
            means = jnp.zeros((POOL_ROWS, act.shape[1]), jnp.float32)
            for image in range(rows // tokens):
                start = i * rows + image * tokens
                mean = jnp.mean(act[start : start + tokens, :], axis=0, keepdims=True)
                means = jnp.where(row == image, mean, means)
            pools[i][...] += dot_nt(means.astype(jnp.bfloat16), w_out[...])

    @pl.when(sel_ref[0] == 1)
    def _():
        work(own_in, own_out)

    @pl.when(sel_ref[0] == 0)
    def _():
        work(other_in, other_out)


def reward_forward(parts, tokens, gain, own, other, sel):
    rows, width = parts[0].shape
    hidden = own[0].shape[1]
    tile, n = tile_of(hidden), len(parts)
    outs = run(
        functools.partial(reward_body, n, tokens),
        "reward_forward",
        hidden // tile,
        sel,
        [*parts, gain, *own, *other],
        [whole((rows, width))] * n
        + [whole((1, width))]
        + [chosen(width, tile, 1)] * 2
        + [chosen(width, tile, 0)] * 2,
        [bf16(rows, hidden)] * n + [jax.ShapeDtypeStruct((POOL_ROWS, width), jnp.float32)] * n,
        [columns(rows, tile)] * n + [whole((POOL_ROWS, width))] * n,
        [pltpu.VMEM((n * rows, width), jnp.bfloat16)],
        2 * n * rows * width * hidden,
        2 * n * rows * hidden,
    )
    return outs[:n], outs[n:]


def back_body(count, tokens, sel_ref, *refs):
    g_tok = refs[0]
    slopes = refs[1 : count + 1]
    own_in, own_out, other_in, other_out = refs[count + 1 : count + 5]
    outs = refs[count + 5 : 2 * count + 5]
    acc = refs[2 * count + 5]
    h = pl.program_id(0)
    rows = slopes[0].shape[0]
    per = rows // tokens

    @pl.when(h == 0)
    def _():
        acc[...] = jnp.zeros_like(acc)

    def work(w_in, w_out):
        g_h = dot_nn(g_tok[...], w_out[...])
        terms = []
        for i in range(count):
            for image in range(per):
                at = i * per + image
                slope = slopes[i][image * tokens : (image + 1) * tokens, :].astype(jnp.float32)
                terms.append((slope * g_h[at : at + 1, :]).astype(jnp.bfloat16))
        acc[...] += dot_nt(jnp.concatenate(terms, axis=0), w_in[...])

    @pl.when(sel_ref[0] == 1)
    def _():
        work(own_in, own_out)

    @pl.when(sel_ref[0] == 0)
    def _():
        work(other_in, other_out)

    @pl.when(h == pl.num_programs(0) - 1)
    def _():
        for i, out in enumerate(outs):
            out[...] = acc[i * rows : (i + 1) * rows, :].astype(jnp.bfloat16)


def reward_back(g_tok, slopes, tokens, own, other, sel):
    rows, hidden = slopes[0].shape
    width = own[0].shape[0]
    tile, n = tile_of(hidden), len(slopes)
    return run(
        functools.partial(back_body, n, tokens),
        "reward_back",
        hidden // tile,
        sel,
        [g_tok, *slopes, *own, *other],
        [whole(g_tok.shape)]
        + [columns(rows, tile)] * n
        + [chosen(width, tile, 1)] * 2
        + [chosen(width, tile, 0)] * 2,
        [bf16(rows, width)] * n,
        [whole((rows, width))] * n,
        [pltpu.VMEM((n * rows, width), jnp.float32)],
        2 * n * rows * width * hidden,
    )


def put_rows(result, core, keep, away):
    groups, rows, unused = keep.shape
    for g in range(groups):
        even = result[2 * g * rows : (2 * g + 1) * rows, :]
        odd = result[(2 * g + 1) * rows : (2 * g + 2) * rows, :]
        keep[g] = jnp.where(core == 0, even, odd).astype(jnp.bfloat16)
        away[g] = jnp.where(core == 0, odd, even).astype(jnp.bfloat16)


def grad_out_body(count, sel_ref, *refs):
    pieces, acts = refs[: 2 * count], refs[2 * count : 3 * count]
    keep, away, turned = refs[3 * count :]
    share = turned.shape[0]

    @pl.when(pl.program_id(0) == 0)
    def _():
        start = pl.multiple_of(sel_ref[0] * share, share)
        cols = jnp.concatenate([piece[:, pl.ds(start, share)] for piece in pieces], axis=0)
        turned[...] = cols.T

    act = jnp.concatenate([part[...] for part in acts], axis=0)
    put_rows(dot_nn(turned[...], act), sel_ref[1], keep, away)


def grad_in_body(count, sel_ref, *refs):
    pieces, slopes = refs[: 2 * count], refs[2 * count : 3 * count]
    xn_cols = refs[3 * count : 4 * count]
    own_out, other_out, keep, away, g_all, turned, g_hidden = refs[4 * count :]
    rows = pieces[0].shape[0]
    wide = xn_cols[0].shape[1]

    @pl.when(pl.program_id(0) == 0)
    def _():
        for i, piece in enumerate(pieces):
            g_all[i * rows : (i + 1) * rows, :] = piece[...]
        for i, part in enumerate(xn_cols):
            turned[:, i * wide : (i + 1) * wide] = part[...]

    def work(weight):
        g_h = dot_nn(g_all[...], weight[...])
        slope = jnp.concatenate([part[...] for part in slopes], axis=0).astype(jnp.float32)
        g_hidden[...] = (g_h * slope).astype(jnp.bfloat16)

    @pl.when(sel_ref[0] == 0)
    def _():
        work(own_out)

    @pl.when(sel_ref[0] == 1)
    def _():
        work(other_out)

    put_rows(dot_nn(turned[...], g_hidden[...]), sel_ref[1], keep, away)


def gradient_call(body, name, pieces, states, extra, extra_specs, scratch, sel, flops):
    rows, width = pieces[0].shape
    hidden = states[0].shape[1]
    tile = tile_of(hidden)
    groups = lax.axis_size("dp") // 2
    cut = (groups, width // 2 // (2 * groups))
    return run(
        body,
        name,
        hidden // tile,
        sel,
        [*pieces, *states, *extra],
        [whole((rows, width))] * len(pieces)
        + [columns(states[0].shape[0], tile)] * len(states)
        + extra_specs,
        [bf16(*cut, hidden)] * 2,
        [pl.BlockSpec((*cut, tile), lambda h, sel: (0, 0, h))] * 2,
        scratch,
        flops,
    )


def grad_out_parts(pieces, acts, sel):
    rows, width = pieces[0].shape
    total = rows * len(pieces)
    return gradient_call(
        functools.partial(grad_out_body, len(acts)),
        "grad_out",
        pieces,
        acts,
        [],
        [],
        [pltpu.VMEM((width // 2, total), jnp.bfloat16)],
        sel,
        total * width * acts[0].shape[1],
    )


def grad_in_parts(pieces, slopes, xn_cols, own_out, other_out, sel):
    rows, width = pieces[0].shape
    total = rows * len(pieces)
    hidden = slopes[0].shape[1]
    tile = tile_of(hidden)
    return gradient_call(
        functools.partial(grad_in_body, len(slopes)),
        "grad_in",
        pieces,
        slopes,
        [*xn_cols, own_out, other_out],
        [whole(xn_cols[0].shape)] * len(xn_cols)
        + [chosen(width, tile, 0), chosen(width, tile, 1)],
        [
            pltpu.VMEM((total, width), jnp.bfloat16),
            pltpu.VMEM((width // 2, total), jnp.bfloat16),
            pltpu.VMEM((total, tile), jnp.bfloat16),
        ],
        sel,
        3 * total * width * hidden,
    )


def sum_over_dp(keep, away):
    groups = keep.shape[0]
    place = lax.axis_index("dp") // 2
    chip = keep.astype(jnp.float32) + swapped(away, "dp", 1).astype(jnp.float32)
    total = lax.dynamic_index_in_dim(chip, place, 0, keepdims=False)
    sent = chip.astype(jnp.bfloat16)
    for k in range(1, groups):
        part = lax.dynamic_index_in_dim(sent, (place + k) % groups, 0, keepdims=False)
        total = total + rotated(part, "dp", 2 * k).astype(jnp.float32)
    return total


def score_of(pooled, text):
    unit_img = pooled * lax.rsqrt(jnp.mean(pooled * pooled, axis=-1, keepdims=True) + EPS)
    unit_txt = text * lax.rsqrt(jnp.mean(text * text, axis=-1, keepdims=True) + EPS)
    return 100.0 * jnp.sum(unit_img * unit_txt, axis=-1) / pooled.shape[-1]


def on_device(latents, timesteps, prompt_ids, prompt_table, gains, w_in, w_out):
    count, tokens, width = latents.shape
    half = count // 2
    n_tp = lax.axis_size("tp")
    segment = lax.axis_index("sec")
    first = segment == 0
    core = lax.axis_index("dp") % 2
    sel = jnp.stack([segment, core]).astype(jnp.int32)
    own = (w_in[0], w_out[0])
    theta = math.pi / 2.0 * (timesteps.astype(jnp.float32) + 1.0) / (STEPS + 1.0)
    alpha = jnp.cos(theta)[:, None, None]
    sigma = jnp.sin(theta)[:, None, None]

    flat = latents.reshape(count * tokens, width)
    lat_parts = gather_parts(flat)
    other = (from_other_section(own[0]), from_other_section(own[1]))

    onehot = (
        prompt_ids[:, None] == jnp.arange(prompt_table.shape[0], dtype=jnp.int32)[None, :]
    ).astype(jnp.bfloat16)
    text = dot_nn(onehot, prompt_table).astype(jnp.bfloat16)
    text_mine = jnp.where(first, text[half:], text[:half])
    text_all = jnp.concatenate(gather_parts(text_mine), 0).astype(jnp.float32)

    near = [k for k in range(1, n_tp) if 2 * k != n_tp]
    far = [k for k in range(1, n_tp) if 2 * k == n_tp]
    eps_parts = [None] * n_tp
    for ks in ([0], near, far):
        if ks:
            results = block0_partials([lat_parts[k] for k in ks], gains[:1], *own, sel)
            for k, result in zip(ks, results):
                eps_parts[k] = result
    eps_mix = reduce_parts(eps_parts).reshape(count, tokens, width)
    base = latents.astype(jnp.float32)
    images = ((base - sigma * (base + eps_mix)) / alpha).astype(jnp.bfloat16)

    arrived = lax.ppermute(images[:half], "sec", [(0, 1)])
    mine = jnp.where(first, images[half:], arrived)
    ratio = jnp.where(first, (sigma / alpha)[half:], (sigma / alpha)[:half])
    mine_rows = mine.reshape(half * tokens, width)
    seen_parts = gather_parts(mine_rows)
    slopes1, pool_parts = [None] * n_tp, [None] * n_tp
    for ks in ([0] + near, far):
        if ks:
            some_slopes, some_pools = reward_forward(
                [seen_parts[k] for k in ks], tokens, gains[1:], own, other, sel
            )
            for k, slope, pool in zip(ks, some_slopes, some_pools):
                slopes1[k], pool_parts[k] = slope, pool[:half]
    pool_part = jnp.stack(pool_parts)
    pool = pool_part
    for k in range(1, n_tp):
        pool = pool + jnp.roll(rotated(pool_part, "tp", k), k, axis=0)
    seen_mean = jnp.stack(
        [
            jnp.mean(part.astype(jnp.float32).reshape(half, tokens, width), axis=1)
            for part in seen_parts
        ]
    )
    pooled = (pool + seen_mean).reshape(n_tp * half, width)
    g_pooled = jax.grad(lambda p: -jnp.sum(score_of(p, text_all)))(pooled)
    g_mean = g_pooled / tokens
    padded = -(-n_tp * half // 16) * 16
    g_tok = jnp.pad(g_mean.astype(jnp.bfloat16), ((0, padded - n_tp * half), (0, 0)))
    g_xn = reduce_parts(reward_back(g_tok, slopes1, tokens, own, other, sel))
    seen = mine_rows.astype(jnp.float32)
    scale1 = lax.rsqrt(jnp.mean(seen * seen, axis=-1, keepdims=True) + EPS)
    weighted = gains[1] * g_xn
    g_norm = scale1 * weighted - seen * scale1**3 * jnp.mean(
        seen * weighted, axis=-1, keepdims=True
    )
    g_images = (g_mean[:half, None, :] + g_norm.reshape(half, tokens, width)).astype(jnp.bfloat16)
    g_eps = (-ratio * g_images.astype(jnp.float32)).astype(jnp.bfloat16)

    acts, slopes0, xn_cols = [], [], []
    for part in lat_parts:
        act, slope, cols = block0_state(part, gains[:1], own[0], other[0], sel)
        acts.append(act)
        slopes0.append(slope)
        xn_cols.append(cols)

    pieces = []
    for part in gather_parts(g_eps.reshape(half * tokens, width)):
        pieces += [part, swapped(part, "sec", 1)]
    grad_out = sum_over_dp(*grad_out_parts(pieces, acts, sel))
    grad_in = sum_over_dp(*grad_in_parts(pieces, slopes0, xn_cols, own[1], other[1], sel))
    return (grad_in, grad_out)


def solution(mesh):
    in_specs = (
        P(("dp", "tp"), None, None),
        P(("dp", "tp")),
        P(("dp", "tp")),
        P(),
        P(),
        P("sec", None, "tp"),
        P("sec", None, "tp"),
    )
    out_specs = (P(("sec", "dp"), "tp"), P(("sec", "dp"), "tp"))
    return jax.shard_map(
        on_device, mesh=mesh, in_specs=in_specs, out_specs=out_specs, check_vma=False
    )
```

```python
import functools
import math

import jax
import jax.numpy as jnp
from jax import lax
from jax.experimental import pallas as pl
from jax.experimental.pallas import tpu as pltpu
from jax.sharding import PartitionSpec as P

STEPS = 50


EPS = 1e-06
VMEM_BYTES = 32 * 1024 * 1024
POOL_ROWS = 8


def rotated(value, axis, steps):
    count = lax.axis_size(axis)
    return lax.ppermute(value, axis, [(i, (i + steps) % count) for i in range(count)])


def swapped(value, axis, bit):
    count = lax.axis_size(axis)
    return lax.ppermute(value, axis, [(i, i ^ bit) for i in range(count)])


def gather_parts(piece):
    return [piece] + [rotated(piece, "tp", k) for k in range(1, lax.axis_size("tp"))]


def reduce_parts(parts):
    total = parts[0].astype(jnp.float32)
    for k in range(1, len(parts)):
        total = total + rotated(parts[k], "tp", -k).astype(jnp.float32)
    return total


def quarter(weight, place):
    rows = weight.shape[0] // 4
    return lax.dynamic_slice_in_dim(weight, place * rows, rows, 0)


def quarters(got, across):
    return (got, swapped(got, "dp", 1), across, swapped(across, "dp", 1))


def gelu_pair(value):
    cdf = 0.5 * (1.0 + lax.erf(value * (1.0 / math.sqrt(2.0))))
    density = jnp.exp(-0.5 * value * value) * (1.0 / math.sqrt(2.0 * math.pi))
    return (value * cdf, cdf + value * density)


def normed(rows, gain):
    scale = lax.rsqrt(jnp.mean(rows * rows, axis=-1, keepdims=True) + EPS)
    return (rows * scale * gain).astype(jnp.bfloat16)


def dot_nn(a, b):
    return jnp.dot(a, b, preferred_element_type=jnp.float32)


def dot_nt(a, b):
    return lax.dot_general(a, b, (((1,), (1,)), ((), ())), preferred_element_type=jnp.float32)


def tile_of(hidden):
    for tile in (256, 128):
        if hidden % tile == 0:
            return tile
    return hidden


def whole(shape):
    return pl.BlockSpec(shape, lambda h, sel: (0,) * len(shape))


def columns(rows, tile):
    return pl.BlockSpec((rows, tile), lambda h, sel: (0, h))


IN_HBM = pl.BlockSpec(memory_space=pltpu.HBM)


def weight_buffers(width, hidden, tile):
    steps = hidden // tile
    return [pltpu.VMEM((steps, width, tile), jnp.bfloat16), pltpu.SemaphoreType.DMA((steps,))]


def fetch_own(own, buffer, sems):
    steps, unused, tile = buffer.shape
    for t in range(steps):
        pltpu.make_async_copy(own.at[:, pl.ds(t * tile, tile)], buffer.at[t], sems.at[t]).start()


def fetch(sel_ref, section, own, pieces, buffer, sems):
    steps, unused, tile = buffer.shape

    @pl.when(sel_ref[0] == section)
    def _():
        fetch_own(own, buffer, sems)

    @pl.when(sel_ref[0] != section)
    def _():
        for t in range(steps):
            for q, piece in enumerate(pieces):
                rows = piece.shape[0]
                start = pl.multiple_of((sel_ref[2] ^ q) * rows, rows)
                pltpu.make_async_copy(
                    piece.at[:, pl.ds(t * tile, tile)],
                    buffer.at[t, pl.ds(start, rows), :],
                    sems.at[t],
                ).start()


def fetched(own, buffer, sems, h):
    tile = buffer.shape[2]
    pltpu.make_async_copy(own.at[:, pl.ds(0, tile)], buffer.at[h], sems.at[h]).wait()
    return buffer[h]


def run(body, name, steps, sel, operands, in_specs, outs, out_specs, scratch, flops, elements=0):
    read = sum(x.size * x.dtype.itemsize for x in operands)
    written = sum(math.prod(o.shape) * o.dtype.itemsize for o in outs)
    return pl.pallas_call(
        body,
        grid_spec=pltpu.PrefetchScalarGridSpec(
            num_scalar_prefetch=1,
            grid=(steps,),
            in_specs=in_specs,
            out_specs=out_specs,
            scratch_shapes=scratch,
        ),
        out_shape=outs,
        compiler_params=pltpu.CompilerParams(
            dimension_semantics=("arbitrary",), vmem_limit_bytes=VMEM_BYTES
        ),
        cost_estimate=pl.CostEstimate(
            flops=flops, bytes_accessed=read + written, transcendentals=elements
        ),
        name=name,
    )(sel, *operands)


def bf16(*shape):
    return jax.ShapeDtypeStruct(shape, jnp.bfloat16)


def partial_body(count, sel_ref, *refs):
    parts, (gain, w_in, w_out) = refs[:count], refs[count : count + 3]
    outs = refs[count + 3 : 2 * count + 3]
    xn, acc, in_buffer, in_sems, out_buffer, out_sems = refs[2 * count + 3 :]
    h = pl.program_id(0)
    rows = parts[0].shape[0]

    @pl.when(h == 0)
    def _():
        fetch_own(w_in, in_buffer, in_sems)
        fetch_own(w_out, out_buffer, out_sems)
        for i, part in enumerate(parts):
            xn[i * rows : (i + 1) * rows, :] = normed(part[...].astype(jnp.float32), gain[...])
        acc[...] = jnp.zeros_like(acc)

    act, unused = gelu_pair(dot_nn(xn[...], fetched(w_in, in_buffer, in_sems, h)))
    acc[...] += dot_nt(act.astype(jnp.bfloat16), fetched(w_out, out_buffer, out_sems, h))

    @pl.when(h == pl.num_programs(0) - 1)
    def _():
        for i, out in enumerate(outs):
            out[...] = acc[i * rows : (i + 1) * rows, :].astype(jnp.bfloat16)


def block0_partials(parts, gain, w_in, w_out, sel):
    rows, width = parts[0].shape
    hidden = w_in.shape[1]
    tile, n = tile_of(hidden), len(parts)
    return run(
        functools.partial(partial_body, n),
        "block0_partial",
        hidden // tile,
        sel,
        [*parts, gain, w_in, w_out],
        [whole((rows, width))] * n
        + [whole((1, width)), IN_HBM, IN_HBM],
        [bf16(rows, width)] * n,
        [whole((rows, width))] * n,
        [
            pltpu.VMEM((n * rows, width), jnp.bfloat16),
            pltpu.VMEM((n * rows, width), jnp.float32),
            *weight_buffers(width, hidden, tile),
            *weight_buffers(width, hidden, tile),
        ],
        4 * n * rows * width * hidden,
        n * rows * hidden,
    )


def state_body(sel_ref, part, gain, own, p0, p1, p2, p3, act, slope, xn_cols, xn, buffer, sems):
    h = pl.program_id(0)
    rows = part.shape[0]
    late = rows // 2
    share = xn_cols.shape[0]

    @pl.when(h == 0)
    def _():
        fetch(sel_ref, 0, own, (p0, p1, p2, p3), buffer, sems)
        mine = pl.multiple_of((1 - sel_ref[0]) * late, late)
        theirs = pl.multiple_of(sel_ref[0] * late, late)
        for i, start in enumerate((mine, theirs)):
            xn[i * late : (i + 1) * late, :] = normed(
                part[pl.ds(start, late), :].astype(jnp.float32), gain[...]
            )
        cols = xn[:, pl.ds(pl.multiple_of(sel_ref[0] * share, share), share)]
        xn_cols[...] = cols.T

    value, grad = gelu_pair(dot_nn(xn[...], fetched(own, buffer, sems, h)))
    act[...] = value.astype(jnp.bfloat16)
    slope[...] = grad.astype(jnp.bfloat16)


def block0_state(part, gain, own, pieces, sel):
    rows, width = part.shape
    hidden = own.shape[1]
    tile = tile_of(hidden)
    return run(
        state_body,
        "block0_state",
        hidden // tile,
        sel,
        [part, gain, own, *pieces],
        [whole((rows, width)), whole((1, width))] + [IN_HBM] * 5,
        [bf16(rows, hidden), bf16(rows, hidden), bf16(width // 2, rows)],
        [columns(rows, tile), columns(rows, tile), whole((width // 2, rows))],
        [pltpu.VMEM((rows, width), jnp.bfloat16), *weight_buffers(width, hidden, tile)],
        2 * rows * width * hidden,
        2 * rows * hidden,
    )


def reward_body(count, tokens, sel_ref, *refs):
    parts, gain = refs[:count], refs[count]
    own_in, own_out, *pieces = refs[count + 1 : count + 11]
    slopes = refs[count + 11 : 2 * count + 11]
    pools = refs[2 * count + 11 : 3 * count + 11]
    xn, in_buffer, in_sems, out_buffer, out_sems = refs[3 * count + 11 :]
    h = pl.program_id(0)
    rows = parts[0].shape[0]

    @pl.when(h == 0)
    def _():
        fetch(sel_ref, 1, own_in, pieces[:4], in_buffer, in_sems)
        fetch(sel_ref, 1, own_out, pieces[4:], out_buffer, out_sems)
        for i, part in enumerate(parts):
            xn[i * rows : (i + 1) * rows, :] = normed(part[...].astype(jnp.float32), gain[...])
            pools[i][...] = jnp.zeros_like(pools[i])

    act, grad = gelu_pair(dot_nn(xn[...], fetched(own_in, in_buffer, in_sems, h)))
    weight = fetched(own_out, out_buffer, out_sems, h)
    row = lax.broadcasted_iota(jnp.int32, (POOL_ROWS, act.shape[1]), 0)
    for i in range(count):
        slopes[i][...] = grad[i * rows : (i + 1) * rows, :].astype(jnp.bfloat16)
        means = jnp.zeros((POOL_ROWS, act.shape[1]), jnp.float32)
        for image in range(rows // tokens):
            start = i * rows + image * tokens
            mean = jnp.mean(act[start : start + tokens, :], axis=0, keepdims=True)
            means = jnp.where(row == image, mean, means)
        pools[i][...] += dot_nt(means.astype(jnp.bfloat16), weight)


def reward_forward(parts, tokens, gain, own, pieces, sel):
    rows, width = parts[0].shape
    hidden = own[0].shape[1]
    tile, n = tile_of(hidden), len(parts)
    outs = run(
        functools.partial(reward_body, n, tokens),
        "reward_forward",
        hidden // tile,
        sel,
        [*parts, gain, *own, *pieces[0], *pieces[1]],
        [whole((rows, width))] * n + [whole((1, width))] + [IN_HBM] * 10,
        [bf16(rows, hidden)] * n + [jax.ShapeDtypeStruct((POOL_ROWS, width), jnp.float32)] * n,
        [columns(rows, tile)] * n + [whole((POOL_ROWS, width))] * n,
        [
            pltpu.VMEM((n * rows, width), jnp.bfloat16),
            *weight_buffers(width, hidden, tile),
            *weight_buffers(width, hidden, tile),
        ],
        2 * n * rows * width * hidden,
        2 * n * rows * hidden,
    )
    return outs[:n], outs[n:]


def back_body(count, tokens, sel_ref, *refs):
    g_tok = refs[0]
    slopes = refs[1 : count + 1]
    own_in, own_out, *pieces = refs[count + 1 : count + 11]
    outs = refs[count + 11 : 2 * count + 11]
    acc, in_buffer, in_sems, out_buffer, out_sems = refs[2 * count + 11 :]
    h = pl.program_id(0)
    rows = slopes[0].shape[0]
    per = rows // tokens

    @pl.when(h == 0)
    def _():
        fetch(sel_ref, 1, own_out, pieces[4:], out_buffer, out_sems)
        fetch(sel_ref, 1, own_in, pieces[:4], in_buffer, in_sems)
        acc[...] = jnp.zeros_like(acc)

    g_h = dot_nn(g_tok[...], fetched(own_out, out_buffer, out_sems, h))
    terms = []
    for i in range(count):
        for image in range(per):
            at = i * per + image
            slope = slopes[i][image * tokens : (image + 1) * tokens, :].astype(jnp.float32)
            terms.append((slope * g_h[at : at + 1, :]).astype(jnp.bfloat16))
    weight = fetched(own_in, in_buffer, in_sems, h)
    acc[...] += dot_nt(jnp.concatenate(terms, axis=0), weight)

    @pl.when(h == pl.num_programs(0) - 1)
    def _():
        for i, out in enumerate(outs):
            out[...] = acc[i * rows : (i + 1) * rows, :].astype(jnp.bfloat16)


def reward_back(g_tok, slopes, tokens, own, pieces, sel):
    rows, hidden = slopes[0].shape
    width = own[0].shape[0]
    tile, n = tile_of(hidden), len(slopes)
    return run(
        functools.partial(back_body, n, tokens),
        "reward_back",
        hidden // tile,
        sel,
        [g_tok, *slopes, *own, *pieces[0], *pieces[1]],
        [whole(g_tok.shape)] + [columns(rows, tile)] * n + [IN_HBM] * 10,
        [bf16(rows, width)] * n,
        [whole((rows, width))] * n,
        [
            pltpu.VMEM((n * rows, width), jnp.float32),
            *weight_buffers(width, hidden, tile),
            *weight_buffers(width, hidden, tile),
        ],
        2 * n * rows * width * hidden,
    )


def put_rows(result, core, keep, away):
    groups, rows, unused = keep.shape
    for g in range(groups):
        even = result[2 * g * rows : (2 * g + 1) * rows, :]
        odd = result[(2 * g + 1) * rows : (2 * g + 2) * rows, :]
        keep[g] = jnp.where(core == 0, even, odd).astype(jnp.bfloat16)
        away[g] = jnp.where(core == 0, odd, even).astype(jnp.bfloat16)


def grad_out_body(count, sel_ref, *refs):
    pieces, acts = refs[: 2 * count], refs[2 * count : 3 * count]
    keep, away, turned = refs[3 * count :]
    share = turned.shape[0]

    @pl.when(pl.program_id(0) == 0)
    def _():
        start = pl.multiple_of(sel_ref[0] * share, share)
        cols = jnp.concatenate([piece[:, pl.ds(start, share)] for piece in pieces], axis=0)
        turned[...] = cols.T

    act = jnp.concatenate([part[...] for part in acts], axis=0)
    put_rows(dot_nn(turned[...], act), sel_ref[1], keep, away)


def grad_in_body(count, sel_ref, *refs):
    pieces, slopes = refs[: 2 * count], refs[2 * count : 3 * count]
    xn_cols = refs[3 * count : 4 * count]
    own, *quarters = refs[4 * count : 4 * count + 5]
    keep, away, g_all, turned, buffer, sems = refs[4 * count + 5 :]
    rows = pieces[0].shape[0]
    wide = xn_cols[0].shape[1]
    h = pl.program_id(0)

    @pl.when(h == 0)
    def _():
        fetch(sel_ref, 0, own, quarters, buffer, sems)
        for i, piece in enumerate(pieces):
            g_all[i * rows : (i + 1) * rows, :] = piece[...]
        for i, part in enumerate(xn_cols):
            turned[:, i * wide : (i + 1) * wide] = part[...]

    g_h = dot_nn(g_all[...], fetched(own, buffer, sems, h))
    slope = jnp.concatenate([part[...] for part in slopes], axis=0).astype(jnp.float32)
    g_hidden = (g_h * slope).astype(jnp.bfloat16)
    put_rows(dot_nn(turned[...], g_hidden), sel_ref[1], keep, away)


def gradient_call(body, name, pieces, states, extra, extra_specs, scratch, sel, flops):
    rows, width = pieces[0].shape
    hidden = states[0].shape[1]
    tile = tile_of(hidden)
    groups = lax.axis_size("dp") // 2
    cut = (groups, width // 2 // (2 * groups))
    return run(
        body,
        name,
        hidden // tile,
        sel,
        [*pieces, *states, *extra],
        [whole((rows, width))] * len(pieces)
        + [columns(states[0].shape[0], tile)] * len(states)
        + extra_specs,
        [bf16(*cut, hidden)] * 2,
        [pl.BlockSpec((*cut, tile), lambda h, sel: (0, 0, h))] * 2,
        scratch,
        flops,
    )


def grad_out_parts(pieces, acts, sel):
    rows, width = pieces[0].shape
    total = rows * len(pieces)
    return gradient_call(
        functools.partial(grad_out_body, len(acts)),
        "grad_out",
        pieces,
        acts,
        [],
        [],
        [pltpu.VMEM((width // 2, total), jnp.bfloat16)],
        sel,
        total * width * acts[0].shape[1],
    )


def grad_in_parts(pieces, slopes, xn_cols, own, quarters, sel):
    rows, width = pieces[0].shape
    total = rows * len(pieces)
    hidden = slopes[0].shape[1]
    return gradient_call(
        functools.partial(grad_in_body, len(slopes)),
        "grad_in",
        pieces,
        slopes,
        [*xn_cols, own, *quarters],
        [whole(xn_cols[0].shape)] * len(xn_cols) + [IN_HBM] * 5,
        [
            pltpu.VMEM((total, width), jnp.bfloat16),
            pltpu.VMEM((width // 2, total), jnp.bfloat16),
            *weight_buffers(width, hidden, tile_of(hidden)),
        ],
        sel,
        3 * total * width * hidden,
    )


def sum_over_dp(keep, away):
    groups = keep.shape[0]
    place = lax.axis_index("dp") // 2
    chip = keep.astype(jnp.float32) + swapped(away, "dp", 1).astype(jnp.float32)
    total = lax.dynamic_index_in_dim(chip, place, 0, keepdims=False)
    sent = chip.astype(jnp.bfloat16)
    for k in range(1, groups):
        part = lax.dynamic_index_in_dim(sent, (place + k) % groups, 0, keepdims=False)
        total = total + rotated(part, "dp", 2 * k).astype(jnp.float32)
    return total


def score_of(pooled, text):
    unit_img = pooled * lax.rsqrt(jnp.mean(pooled * pooled, axis=-1, keepdims=True) + EPS)
    unit_txt = text * lax.rsqrt(jnp.mean(text * text, axis=-1, keepdims=True) + EPS)
    return 100.0 * jnp.sum(unit_img * unit_txt, axis=-1) / pooled.shape[-1]


def on_device(latents, timesteps, prompt_ids, prompt_table, gains, w_in, w_out):
    count, tokens, width = latents.shape
    half = count // 2
    n_tp = lax.axis_size("tp")
    segment = lax.axis_index("sec")
    first = segment == 0
    core = lax.axis_index("dp") % 2
    place = lax.axis_index("dp") % 4
    sel = jnp.stack([segment, core, place]).astype(jnp.int32)
    own = (w_in[0], w_out[0])
    theta = math.pi / 2.0 * (timesteps.astype(jnp.float32) + 1.0) / (STEPS + 1.0)
    alpha = jnp.cos(theta)[:, None, None]
    sigma = jnp.sin(theta)[:, None, None]

    flat = latents.reshape(count * tokens, width)
    got_in = swapped(quarter(own[0], place), "sec", 1)
    lat_parts = gather_parts(flat)
    got_out = swapped(quarter(own[1], place), "sec", 1)
    across_in = swapped(got_in, "dp", 2)
    across_out = swapped(got_out, "dp", 2)

    onehot = (
        prompt_ids[:, None] == jnp.arange(prompt_table.shape[0], dtype=jnp.int32)[None, :]
    ).astype(jnp.bfloat16)
    text = dot_nn(onehot, prompt_table).astype(jnp.bfloat16)
    text_mine = jnp.where(first, text[half:], text[:half])
    text_all = jnp.concatenate(gather_parts(text_mine), 0).astype(jnp.float32)

    near = [k for k in range(1, n_tp) if 2 * k != n_tp]
    far = [k for k in range(1, n_tp) if 2 * k == n_tp]
    eps_parts = [None] * n_tp
    arrivals = ([], [got_in, text_all], [got_out, across_in])
    for ks, arrived in zip(([0], near, far), arrivals):
        if ks:
            operands, unused = lax.optimization_barrier(([lat_parts[k] for k in ks], arrived))
            results = block0_partials(operands, gains[:1], *own, sel)
            for k, result in zip(ks, results):
                eps_parts[k] = result
    eps_mix, across_out = lax.optimization_barrier((reduce_parts(eps_parts), across_out))
    eps_mix = eps_mix.reshape(count, tokens, width)
    other = (quarters(got_in, across_in), quarters(got_out, across_out))
    base = latents.astype(jnp.float32)
    images = ((base - sigma * (base + eps_mix)) / alpha).astype(jnp.bfloat16)

    arrived = lax.ppermute(images[:half], "sec", [(0, 1)])
    mine = jnp.where(first, images[half:], arrived)
    ratio = jnp.where(first, (sigma / alpha)[half:], (sigma / alpha)[:half])
    mine_rows = mine.reshape(half * tokens, width)
    seen_parts = gather_parts(mine_rows)

    states = [block0_state(part, gains[:1], own[0], other[0], sel) for part in lat_parts]
    slopes1, pool_parts = [None] * n_tp, [None] * n_tp
    early = n_tp // 2
    done = (states[: early // 2], states[early // 2 : early])
    for ks, before in zip(([0] + near, far), done):
        if ks:
            operands, unused = lax.optimization_barrier(([seen_parts[k] for k in ks], before))
            some_slopes, some_pools = reward_forward(
                operands, tokens, gains[1:], own, other, sel
            )
            for k, slope, pool in zip(ks, some_slopes, some_pools):
                slopes1[k], pool_parts[k] = slope, pool[:half]
    pool_part = jnp.stack(pool_parts)
    pool = pool_part
    for k in range(1, n_tp):
        pool = pool + jnp.roll(rotated(pool_part, "tp", k), k, axis=0)
    seen_mean = jnp.stack(
        [
            jnp.mean(part.astype(jnp.float32).reshape(half, tokens, width), axis=1)
            for part in seen_parts
        ]
    )
    pooled = (pool + seen_mean).reshape(n_tp * half, width)
    g_pooled = jax.grad(lambda p: -jnp.sum(score_of(p, text_all)))(pooled)
    g_mean = g_pooled / tokens
    padded = -(-n_tp * half // 16) * 16
    g_tok = jnp.pad(g_mean.astype(jnp.bfloat16), ((0, padded - n_tp * half), (0, 0)))
    g_parts = reward_back(g_tok, slopes1, tokens, own, other, sel)
    g_xn, unused = lax.optimization_barrier((reduce_parts(g_parts), states[early:]))
    seen = mine_rows.astype(jnp.float32)
    scale1 = lax.rsqrt(jnp.mean(seen * seen, axis=-1, keepdims=True) + EPS)
    weighted = gains[1] * g_xn
    g_norm = scale1 * weighted - seen * scale1**3 * jnp.mean(
        seen * weighted, axis=-1, keepdims=True
    )
    g_images = (g_mean[:half, None, :] + g_norm.reshape(half, tokens, width)).astype(jnp.bfloat16)
    g_eps = (-ratio * g_images.astype(jnp.float32)).astype(jnp.bfloat16)

    pieces = []
    for part in gather_parts(g_eps.reshape(half * tokens, width)):
        pieces += [part, swapped(part, "sec", 1)]
    grad_out = sum_over_dp(*grad_out_parts(pieces, [state[0] for state in states], sel))
    slopes0, xn_cols = [state[1] for state in states], [state[2] for state in states]
    grad_in = sum_over_dp(*grad_in_parts(pieces, slopes0, xn_cols, own[1], other[1], sel))
    return (grad_in, grad_out)


def solution(mesh):
    in_specs = (
        P(("dp", "tp"), None, None),
        P(("dp", "tp")),
        P(("dp", "tp")),
        P(),
        P(),
        P("sec", None, "tp"),
        P("sec", None, "tp"),
    )
    out_specs = (P(("sec", "dp"), "tp"), P(("sec", "dp"), "tp"))
    return jax.shard_map(
        on_device, mesh=mesh, in_specs=in_specs, out_specs=out_specs, check_vma=False
    )
```

```python
import functools
import math

import jax
import jax.numpy as jnp
from jax import lax
from jax.experimental import pallas as pl
from jax.experimental.pallas import tpu as pltpu
from jax.sharding import PartitionSpec as P

STEPS = 50


EPS = 1e-06
VMEM_BYTES = 16 * 1024 * 1024


def rotated(value, axis, steps):
    count = lax.axis_size(axis)
    return lax.ppermute(value, axis, [(i, (i + steps) % count) for i in range(count)])


def swapped(value, axis, bit):
    count = lax.axis_size(axis)
    return lax.ppermute(value, axis, [(i, i ^ bit) for i in range(count)])


def gather_parts(piece):
    return [piece] + [rotated(piece, "tp", k) for k in range(1, lax.axis_size("tp"))]


def reduce_parts(parts):
    total = parts[0].astype(jnp.float32)
    for k in range(1, len(parts)):
        total = total + rotated(parts[k], "tp", -k).astype(jnp.float32)
    return total


def quarter(weight, place):
    rows = weight.shape[0] // 4
    return lax.dynamic_slice_in_dim(weight, place * rows, rows, 0)


def assembled(got, across, place):
    pieces = (got, swapped(got, "dp", 1), across, swapped(across, "dp", 1))
    rows, columns = got.shape
    full = jnp.zeros((4 * rows, columns), got.dtype)
    for q, piece in enumerate(pieces):
        full = lax.dynamic_update_slice_in_dim(full, piece, (place ^ q) * rows, 0)
    return full


def gelu_pair(value):
    cdf = 0.5 * (1.0 + lax.erf(value * (1.0 / math.sqrt(2.0))))
    density = jnp.exp(-0.5 * value * value) * (1.0 / math.sqrt(2.0 * math.pi))
    return (value * cdf, cdf + value * density)


def normed(rows, gain):
    scale = lax.rsqrt(jnp.mean(rows * rows, axis=-1, keepdims=True) + EPS)
    return (rows * scale * gain).astype(jnp.bfloat16)


def dot_nn(a, b):
    return jnp.dot(a, b, preferred_element_type=jnp.float32)


def dot_nt(a, b):
    return lax.dot_general(a, b, (((1,), (1,)), ((), ())), preferred_element_type=jnp.float32)


def tile_of(hidden):
    for tile in (256, 128):
        if hidden % tile == 0:
            return tile
    return hidden


IN_VMEM = pl.BlockSpec(memory_space=pltpu.VMEM)
IN_SMEM = pl.BlockSpec(memory_space=pltpu.SMEM)


def run(body, name, sel, operands, outs, scratch, flops, elements=0):
    read = sum(x.size * x.dtype.itemsize for x in operands)
    written = sum(math.prod(o.shape) * o.dtype.itemsize for o in outs)
    return pl.pallas_call(
        body,
        in_specs=[IN_SMEM] + [IN_VMEM] * len(operands),
        out_specs=[IN_VMEM] * len(outs),
        scratch_shapes=scratch,
        out_shape=outs,
        compiler_params=pltpu.CompilerParams(vmem_limit_bytes=VMEM_BYTES),
        cost_estimate=pl.CostEstimate(
            flops=flops, bytes_accessed=read + written, transcendentals=elements
        ),
        name=name,
    )(sel, *operands)


def bf16(*shape):
    return jax.ShapeDtypeStruct(shape, jnp.bfloat16)


def tiles(hidden):
    tile = tile_of(hidden)
    return [slice(t, t + tile) for t in range(0, hidden, tile)]


def by_section(sel_ref, section, work, own, other):
    @pl.when(sel_ref[0] == section)
    def _():
        work(*own)

    @pl.when(sel_ref[0] != section)
    def _():
        work(*other)


def partial_body(count, sel_ref, *refs):
    parts, (gain, w_in, w_out) = refs[:count], refs[count : count + 3]
    outs, (xn, acc) = refs[count + 3 : 2 * count + 3], refs[2 * count + 3 :]
    rows = parts[0].shape[0]
    for i, part in enumerate(parts):
        xn[i * rows : (i + 1) * rows, :] = normed(part[...].astype(jnp.float32), gain[...])
    for t, tile in enumerate(tiles(w_in.shape[1])):
        act, unused = gelu_pair(dot_nn(xn[...], w_in[:, tile]))
        term = dot_nt(act.astype(jnp.bfloat16), w_out[:, tile])
        acc[...] = term if t == 0 else acc[...] + term
    for i, out in enumerate(outs):
        out[...] = acc[i * rows : (i + 1) * rows, :].astype(jnp.bfloat16)


def block0_partials(parts, gain, w_in, w_out, sel):
    rows, width = parts[0].shape
    hidden, n = w_in.shape[1], len(parts)
    return run(
        functools.partial(partial_body, n),
        "block0_partial",
        sel,
        [*parts, gain, w_in, w_out],
        [bf16(rows, width)] * n,
        [
            pltpu.VMEM((n * rows, width), jnp.bfloat16),
            pltpu.VMEM((n * rows, width), jnp.float32),
        ],
        4 * n * rows * width * hidden,
        n * rows * hidden,
    )


def state_body(sel_ref, part, gain, own, other, act, slope, xn_cols, xn):
    rows = part.shape[0]
    late = rows // 2
    share = xn_cols.shape[0]
    mine = pl.multiple_of((1 - sel_ref[0]) * late, late)
    theirs = pl.multiple_of(sel_ref[0] * late, late)
    for i, start in enumerate((mine, theirs)):
        xn[i * late : (i + 1) * late, :] = normed(
            part[pl.ds(start, late), :].astype(jnp.float32), gain[...]
        )
    cols = xn[:, pl.ds(pl.multiple_of(sel_ref[0] * share, share), share)]
    xn_cols[...] = cols.T

    def work(weight):
        for tile in tiles(weight.shape[1]):
            value, grad = gelu_pair(dot_nn(xn[...], weight[:, tile]))
            act[:, tile] = value.astype(jnp.bfloat16)
            slope[:, tile] = grad.astype(jnp.bfloat16)

    by_section(sel_ref, 0, work, (own,), (other,))


def block0_state(part, gain, own, other, sel):
    rows, width = part.shape
    hidden = own.shape[1]
    return run(
        state_body,
        "block0_state",
        sel,
        [part, gain, own, other],
        [bf16(rows, hidden), bf16(rows, hidden), bf16(width // 2, rows)],
        [pltpu.VMEM((rows, width), jnp.bfloat16)],
        2 * rows * width * hidden,
        2 * rows * hidden,
    )


def reward_body(count, tokens, sel_ref, *refs):
    parts, gain = refs[:count], refs[count]
    own_in, own_out, other_in, other_out = refs[count + 1 : count + 5]
    slopes, (pool, xn) = refs[count + 5 : 2 * count + 5], refs[2 * count + 5 :]
    rows = parts[0].shape[0]
    for i, part in enumerate(parts):
        xn[i * rows : (i + 1) * rows, :] = normed(part[...].astype(jnp.float32), gain[...])

    def work(w_in, w_out):
        for t, tile in enumerate(tiles(w_in.shape[1])):
            act, grad = gelu_pair(dot_nn(xn[...], w_in[:, tile]))
            for i in range(count):
                slopes[i][:, tile] = grad[i * rows : (i + 1) * rows, :].astype(jnp.bfloat16)
            means = [
                jnp.mean(act[start : start + tokens, :], axis=0, keepdims=True)
                for start in range(0, count * rows, tokens)
            ]
            row = lax.broadcasted_iota(jnp.int32, (pool.shape[0], act.shape[1]), 0)
            stacked = jnp.zeros(row.shape, jnp.float32)
            for i, mean in enumerate(means):
                stacked = jnp.where(row == i, mean, stacked)
            term = dot_nt(stacked.astype(jnp.bfloat16), w_out[:, tile])
            pool[...] = term if t == 0 else pool[...] + term

    by_section(sel_ref, 1, work, (own_in, own_out), (other_in, other_out))


def reward_forward(parts, tokens, gain, own, other, sel):
    rows, width = parts[0].shape
    hidden, n = own[0].shape[1], len(parts)
    images = n * rows // tokens
    outs = run(
        functools.partial(reward_body, n, tokens),
        "reward_forward",
        sel,
        [*parts, gain, *own, *other],
        [bf16(rows, hidden)] * n
        + [jax.ShapeDtypeStruct((-(-images // 8) * 8, width), jnp.float32)],
        [pltpu.VMEM((n * rows, width), jnp.bfloat16)],
        2 * n * rows * width * hidden,
        2 * n * rows * hidden,
    )
    return outs[:n], outs[n][:images]


def back_body(count, tokens, sel_ref, *refs):
    g_tok = refs[0]
    slopes = refs[1 : count + 1]
    own_in, own_out, other_in, other_out = refs[count + 1 : count + 5]
    outs, acc = refs[count + 5 : 2 * count + 5], refs[2 * count + 5]
    rows = slopes[0].shape[0]
    per = rows // tokens

    def work(w_in, w_out):
        for t, tile in enumerate(tiles(w_in.shape[1])):
            g_h = dot_nn(g_tok[...], w_out[:, tile])
            terms = []
            for i in range(count):
                for image in range(per):
                    at = i * per + image
                    slope = slopes[i][image * tokens : (image + 1) * tokens, tile]
                    terms.append(
                        (slope.astype(jnp.float32) * g_h[at : at + 1, :]).astype(jnp.bfloat16)
                    )
            term = dot_nt(jnp.concatenate(terms, axis=0), w_in[:, tile])
            acc[...] = term if t == 0 else acc[...] + term

    by_section(sel_ref, 1, work, (own_in, own_out), (other_in, other_out))
    for i, out in enumerate(outs):
        out[...] = acc[i * rows : (i + 1) * rows, :].astype(jnp.bfloat16)


def reward_back(g_tok, slopes, tokens, own, other, sel):
    rows, hidden = slopes[0].shape
    width, n = own[0].shape[0], len(slopes)
    return run(
        functools.partial(back_body, n, tokens),
        "reward_back",
        sel,
        [g_tok, *slopes, *own, *other],
        [bf16(rows, width)] * n,
        [pltpu.VMEM((n * rows, width), jnp.float32)],
        2 * n * rows * width * hidden,
    )


def put_rows(result, core, keep, away, tile):
    groups, rows, unused = keep.shape
    for g in range(groups):
        even = result[2 * g * rows : (2 * g + 1) * rows, :]
        odd = result[(2 * g + 1) * rows : (2 * g + 2) * rows, :]
        keep[g, :, tile] = jnp.where(core == 0, even, odd).astype(jnp.bfloat16)
        away[g, :, tile] = jnp.where(core == 0, odd, even).astype(jnp.bfloat16)


def grad_out_body(count, sel_ref, *refs):
    pieces, acts = refs[: 2 * count], refs[2 * count : 3 * count]
    keep, away, turned, state = refs[3 * count :]
    share = turned.shape[0]
    rows = acts[0].shape[0]
    start = pl.multiple_of(sel_ref[0] * share, share)
    cols = jnp.concatenate([piece[:, pl.ds(start, share)] for piece in pieces], axis=0)
    turned[...] = cols.T
    for i, part in enumerate(acts):
        state[i * rows : (i + 1) * rows, :] = part[...]
    for tile in tiles(state.shape[1]):
        put_rows(dot_nn(turned[...], state[:, tile]), sel_ref[1], keep, away, tile)


def grad_in_body(count, sel_ref, *refs):
    pieces, slopes = refs[: 2 * count], refs[2 * count : 3 * count]
    xn_cols = refs[3 * count : 4 * count]
    own, other, keep, away, g_all, turned = refs[4 * count :]
    rows = pieces[0].shape[0]
    wide = xn_cols[0].shape[1]
    for i, piece in enumerate(pieces):
        g_all[i * rows : (i + 1) * rows, :] = piece[...]
    for i, part in enumerate(xn_cols):
        turned[:, i * wide : (i + 1) * wide] = part[...]

    def work(weight):
        for tile in tiles(weight.shape[1]):
            g_h = dot_nn(g_all[...], weight[:, tile])
            slope = jnp.concatenate([part[:, tile] for part in slopes], axis=0)
            g_hidden = (g_h * slope.astype(jnp.float32)).astype(jnp.bfloat16)
            put_rows(dot_nn(turned[...], g_hidden), sel_ref[1], keep, away, tile)

    by_section(sel_ref, 0, work, (own,), (other,))


def gradient_outs(width, hidden):
    groups = lax.axis_size("dp") // 2
    return [bf16(groups, width // 2 // (2 * groups), hidden)] * 2


def grad_out_parts(pieces, acts, sel):
    rows, width = pieces[0].shape
    total, hidden = rows * len(pieces), acts[0].shape[1]
    return run(
        functools.partial(grad_out_body, len(acts)),
        "grad_out",
        sel,
        [*pieces, *acts],
        gradient_outs(width, hidden),
        [
            pltpu.VMEM((width // 2, total), jnp.bfloat16),
            pltpu.VMEM((total, hidden), jnp.bfloat16),
        ],
        total * width * hidden,
    )


def grad_in_parts(pieces, slopes, xn_cols, own, other, sel):
    rows, width = pieces[0].shape
    total, hidden = rows * len(pieces), slopes[0].shape[1]
    return run(
        functools.partial(grad_in_body, len(slopes)),
        "grad_in",
        sel,
        [*pieces, *slopes, *xn_cols, own, other],
        gradient_outs(width, hidden),
        [
            pltpu.VMEM((total, width), jnp.bfloat16),
            pltpu.VMEM((width // 2, total), jnp.bfloat16),
        ],
        3 * total * width * hidden,
    )


def sum_over_dp(keep, away):
    groups = keep.shape[0]
    place = lax.axis_index("dp") // 2
    chip = keep.astype(jnp.float32) + swapped(away, "dp", 1).astype(jnp.float32)
    total = lax.dynamic_index_in_dim(chip, place, 0, keepdims=False)
    sent = chip.astype(jnp.bfloat16)
    for k in range(1, groups):
        part = lax.dynamic_index_in_dim(sent, (place + k) % groups, 0, keepdims=False)
        total = total + rotated(part, "dp", 2 * k).astype(jnp.float32)
    return total


def score_of(pooled, text):
    unit_img = pooled * lax.rsqrt(jnp.mean(pooled * pooled, axis=-1, keepdims=True) + EPS)
    unit_txt = text * lax.rsqrt(jnp.mean(text * text, axis=-1, keepdims=True) + EPS)
    return 100.0 * jnp.sum(unit_img * unit_txt, axis=-1) / pooled.shape[-1]


def on_device(latents, timesteps, prompt_ids, prompt_table, gains, w_in, w_out):
    count, tokens, width = latents.shape
    half = count // 2
    n_tp = lax.axis_size("tp")
    segment = lax.axis_index("sec")
    first = segment == 0
    core = lax.axis_index("dp") % 2
    place = lax.axis_index("dp") % 4
    sel = jnp.stack([segment, core, place]).astype(jnp.int32)
    own = (w_in[0], w_out[0])
    theta = math.pi / 2.0 * (timesteps.astype(jnp.float32) + 1.0) / (STEPS + 1.0)
    alpha = jnp.cos(theta)[:, None, None]
    sigma = jnp.sin(theta)[:, None, None]

    flat = latents.reshape(count * tokens, width)
    got_in = swapped(quarter(own[0], place), "sec", 1)
    lat_parts = gather_parts(flat)
    got_out = swapped(quarter(own[1], place), "sec", 1)
    across_in = swapped(got_in, "dp", 2)
    across_out = swapped(got_out, "dp", 2)

    onehot = (
        prompt_ids[:, None] == jnp.arange(prompt_table.shape[0], dtype=jnp.int32)[None, :]
    ).astype(jnp.bfloat16)
    text = dot_nn(onehot, prompt_table)
    text_mine = jnp.where(first, text[half:], text[:half])

    near = [k for k in range(1, n_tp) if 2 * k != n_tp]
    far = [k for k in range(1, n_tp) if 2 * k == n_tp]
    eps_parts = [None] * n_tp
    arrivals = ([], [got_in], [got_out, across_in])
    for ks, arrived in zip(([0], near, far), arrivals):
        if ks:
            operands, unused = lax.optimization_barrier(([lat_parts[k] for k in ks], arrived))
            results = block0_partials(operands, gains[:1], *own, sel)
            for k, result in zip(ks, results):
                eps_parts[k] = result
    eps_mix, across_out = lax.optimization_barrier((reduce_parts(eps_parts), across_out))
    eps_mix = eps_mix.reshape(count, tokens, width)
    other = (assembled(got_in, across_in, place), assembled(got_out, across_out, place))
    base = latents.astype(jnp.float32)
    images = ((base - sigma * (base + eps_mix)) / alpha).astype(jnp.bfloat16)

    arrived = lax.ppermute(images[:half], "sec", [(0, 1)])
    mine = jnp.where(first, images[half:], arrived)
    ratio = jnp.where(first, (sigma / alpha)[half:], (sigma / alpha)[:half])
    mine_rows = mine.reshape(half * tokens, width)
    seen_parts = gather_parts(mine_rows)

    states = [block0_state(part, gains[:1], own[0], other[0], sel) for part in lat_parts]
    slopes1, pool_parts = [None] * n_tp, [None] * n_tp
    for ks in ([0] + near, far):
        if ks:
            operands = [seen_parts[k] for k in ks]
            some_slopes, some_pools = reward_forward(
                operands, tokens, gains[1:], own, other, sel
            )
            for i, k in enumerate(ks):
                slopes1[k] = some_slopes[i]
                pool_parts[k] = some_pools[i * half : (i + 1) * half]
    pool_part = jnp.concatenate(pool_parts, 0)
    with_text = jnp.concatenate([pool_part, text_mine], 0)
    pool, texts = pool_part, [text_mine]
    for k in range(1, n_tp):
        theirs = rotated(with_text, "tp", k)
        pool = pool + jnp.roll(theirs[: n_tp * half], k * half, axis=0)
        texts.append(theirs[n_tp * half :])
    text_all = jnp.concatenate(texts, 0)
    seen_mean = [
        jnp.mean(part.astype(jnp.float32).reshape(half, tokens, width), axis=1)
        for part in seen_parts
    ]
    pooled = pool + jnp.concatenate(seen_mean, 0)
    g_pooled = jax.grad(lambda p: -jnp.sum(score_of(p, text_all)))(pooled)
    g_mean = g_pooled / tokens
    padded = -(-n_tp * half // 16) * 16
    g_tok = jnp.pad(g_mean.astype(jnp.bfloat16), ((0, padded - n_tp * half), (0, 0)))
    g_parts = reward_back(g_tok, slopes1, tokens, own, other, sel)
    g_xn, unused = lax.optimization_barrier((reduce_parts(g_parts), states))
    seen = mine_rows.astype(jnp.float32)
    scale1 = lax.rsqrt(jnp.mean(seen * seen, axis=-1, keepdims=True) + EPS)
    weighted = gains[1] * g_xn
    g_norm = scale1 * weighted - seen * scale1**3 * jnp.mean(
        seen * weighted, axis=-1, keepdims=True
    )
    g_images = (g_mean[:half, None, :] + g_norm.reshape(half, tokens, width)).astype(jnp.bfloat16)
    g_eps = (-ratio * g_images.astype(jnp.float32)).astype(jnp.bfloat16)

    pieces = []
    for part in gather_parts(g_eps.reshape(half * tokens, width)):
        pieces += [part, swapped(part, "sec", 1)]
    out_parts = grad_out_parts(pieces, [state[0] for state in states], sel)
    slopes0, xn_cols = [state[1] for state in states], [state[2] for state in states]
    out_parts, slopes0 = lax.optimization_barrier((out_parts, slopes0))
    in_parts = grad_in_parts(pieces, slopes0, xn_cols, own[1], other[1], sel)
    grad_out, grad_in = sum_over_dp(*out_parts), sum_over_dp(*in_parts)
    return (grad_in, grad_out)


def solution(mesh):
    in_specs = (
        P(("dp", "tp"), None, None),
        P(("dp", "tp")),
        P(("dp", "tp")),
        P(),
        P(),
        P("sec", None, "tp"),
        P("sec", None, "tp"),
    )
    out_specs = (P(("sec", "dp"), "tp"), P(("sec", "dp"), "tp"))
    return jax.shard_map(
        on_device, mesh=mesh, in_specs=in_specs, out_specs=out_specs, check_vma=False
    )
```

```python
import functools
import math

import jax
import jax.numpy as jnp
from jax import lax
from jax.experimental import pallas as pl
from jax.experimental.pallas import tpu as pltpu
from jax.sharding import PartitionSpec as P

STEPS = 50


EPS = 1e-06
VMEM_BYTES = 6 * 1024 * 1024


def rotated(value, axis, steps):
    count = lax.axis_size(axis)
    return lax.ppermute(value, axis, [(i, (i + steps) % count) for i in range(count)])


def swapped(value, axis, bit):
    count = lax.axis_size(axis)
    return lax.ppermute(value, axis, [(i, i ^ bit) for i in range(count)])


def gather_parts(piece):
    return [piece] + [rotated(piece, "tp", k) for k in range(1, lax.axis_size("tp"))]


def gather_chain(piece):
    count, half = lax.axis_size("tp"), piece.shape[0] // 2
    parts = [[piece]] + [None] * (count - 1)
    right, left = piece, piece
    for k in range(1, (count + 1) // 2):
        right, left = rotated(right, "tp", 1), rotated(left, "tp", -1)
        parts[k], parts[count - k] = [right], [left]
    if count % 2 == 0:
        parts[count // 2] = [rotated(right[:half], "tp", 1), rotated(left[half:], "tp", -1)]
    return parts


def reduce_parts(parts):
    total = parts[0].astype(jnp.float32)
    for k in range(1, len(parts)):
        total = total + rotated(parts[k], "tp", -k).astype(jnp.float32)
    return total


def quarter(weight, place):
    rows = weight.shape[0] // 4
    return lax.dynamic_slice_in_dim(weight, place * rows, rows, 0)


def assembled(got, across, place):
    pieces = (got, swapped(got, "dp", 1), across, swapped(across, "dp", 1))
    rows, columns = got.shape
    full = jnp.zeros((4 * rows, columns), got.dtype)
    for q, piece in enumerate(pieces):
        full = lax.dynamic_update_slice_in_dim(full, piece, (place ^ q) * rows, 0)
    return full


def gelu_pair(value):
    cdf = 0.5 * (1.0 + lax.erf(value * (1.0 / math.sqrt(2.0))))
    density = jnp.exp(-0.5 * value * value) * (1.0 / math.sqrt(2.0 * math.pi))
    return (value * cdf, cdf + value * density)


def normed(rows, gain):
    scale = lax.rsqrt(jnp.mean(rows * rows, axis=-1, keepdims=True) + EPS)
    return (rows * scale * gain).astype(jnp.bfloat16)


def dot_nn(a, b):
    return jnp.dot(a, b, preferred_element_type=jnp.float32)


def dot_nt(a, b):
    return lax.dot_general(a, b, (((1,), (1,)), ((), ())), preferred_element_type=jnp.float32)


def tile_of(hidden):
    for tile in (256, 128):
        if hidden % tile == 0:
            return tile
    return hidden


IN_VMEM = pl.BlockSpec(memory_space=pltpu.VMEM)
IN_SMEM = pl.BlockSpec(memory_space=pltpu.SMEM)


def run(body, name, sel, operands, outs, scratch, flops, elements=0):
    read = sum(x.size * x.dtype.itemsize for x in operands)
    written = sum(math.prod(o.shape) * o.dtype.itemsize for o in outs)
    return pl.pallas_call(
        body,
        in_specs=[IN_SMEM] + [IN_VMEM] * len(operands),
        out_specs=[IN_VMEM] * len(outs),
        scratch_shapes=scratch,
        out_shape=outs,
        compiler_params=pltpu.CompilerParams(vmem_limit_bytes=VMEM_BYTES),
        cost_estimate=pl.CostEstimate(
            flops=flops, bytes_accessed=read + written, transcendentals=elements
        ),
        name=name,
    )(sel, *operands)


def bf16(*shape):
    return jax.ShapeDtypeStruct(shape, jnp.bfloat16)


def tiles(hidden):
    tile = tile_of(hidden)
    return [slice(t, t + tile) for t in range(0, hidden, tile)]


def by_section(sel_ref, section, work, own, other):
    @pl.when(sel_ref[0] == section)
    def _():
        work(*own)

    @pl.when(sel_ref[0] != section)
    def _():
        work(*other)


def partial_body(count, sel_ref, *refs):
    pieces, (gain, w_in, w_out) = refs[:count], refs[count : count + 3]
    outs, (xn, acc) = refs[count + 3 : -2], refs[-2:]
    start = 0
    for piece in pieces:
        stop = start + piece.shape[0]
        xn[start:stop, :] = normed(piece[...].astype(jnp.float32), gain[...])
        start = stop
    for t, tile in enumerate(tiles(w_in.shape[1])):
        act, unused = gelu_pair(dot_nn(xn[...], w_in[:, tile]))
        term = dot_nt(act.astype(jnp.bfloat16), w_out[:, tile])
        acc[...] = term if t == 0 else acc[...] + term
    rows = outs[0].shape[0]
    for i, out in enumerate(outs):
        out[...] = acc[i * rows : (i + 1) * rows, :].astype(jnp.bfloat16)


def block0_partials(parts, gain, w_in, w_out, sel):
    pieces = [piece for part in parts for piece in part]
    rows, width = sum(piece.shape[0] for piece in parts[0]), w_in.shape[0]
    hidden, n = w_in.shape[1], len(parts)
    return run(
        functools.partial(partial_body, len(pieces)),
        "block0_partial",
        sel,
        [*pieces, gain, w_in, w_out],
        [bf16(rows, width)] * n,
        [
            pltpu.VMEM((n * rows, width), jnp.bfloat16),
            pltpu.VMEM((n * rows, width), jnp.float32),
        ],
        4 * n * rows * width * hidden,
        n * rows * hidden,
    )


def state_body(sel_ref, part, gain, own, other, act, slope, xn_cols, xn):
    rows = part.shape[0]
    late = rows // 2
    share = xn_cols.shape[0]
    mine = pl.multiple_of((1 - sel_ref[0]) * late, late)
    theirs = pl.multiple_of(sel_ref[0] * late, late)
    for i, start in enumerate((mine, theirs)):
        xn[i * late : (i + 1) * late, :] = normed(
            part[pl.ds(start, late), :].astype(jnp.float32), gain[...]
        )
    cols = xn[:, pl.ds(pl.multiple_of(sel_ref[0] * share, share), share)]
    xn_cols[...] = cols.T

    def work(weight):
        for tile in tiles(weight.shape[1]):
            value, grad = gelu_pair(dot_nn(xn[...], weight[:, tile]))
            act[:, tile] = value.astype(jnp.bfloat16)
            slope[:, tile] = grad.astype(jnp.bfloat16)

    by_section(sel_ref, 0, work, (own,), (other,))


def block0_state(part, gain, own, other, sel):
    rows, width = part.shape
    hidden = own.shape[1]
    return run(
        state_body,
        "block0_state",
        sel,
        [part, gain, own, other],
        [bf16(rows, hidden), bf16(rows, hidden), bf16(width // 2, rows)],
        [pltpu.VMEM((rows, width), jnp.bfloat16)],
        2 * rows * width * hidden,
        2 * rows * hidden,
    )


def reward_body(count, tokens, sel_ref, *refs):
    parts, gain = refs[:count], refs[count]
    own_in, own_out, other_in, other_out = refs[count + 1 : count + 5]
    slopes, (pool, xn) = refs[count + 5 : 2 * count + 5], refs[2 * count + 5 :]
    rows = parts[0].shape[0]
    for i, part in enumerate(parts):
        xn[i * rows : (i + 1) * rows, :] = normed(part[...].astype(jnp.float32), gain[...])

    def work(w_in, w_out):
        for t, tile in enumerate(tiles(w_in.shape[1])):
            act, grad = gelu_pair(dot_nn(xn[...], w_in[:, tile]))
            for i in range(count):
                slopes[i][:, tile] = grad[i * rows : (i + 1) * rows, :].astype(jnp.bfloat16)
            means = [
                jnp.mean(act[start : start + tokens, :], axis=0, keepdims=True)
                for start in range(0, count * rows, tokens)
            ]
            row = lax.broadcasted_iota(jnp.int32, (pool.shape[0], act.shape[1]), 0)
            stacked = jnp.zeros(row.shape, jnp.float32)
            for i, mean in enumerate(means):
                stacked = jnp.where(row == i, mean, stacked)
            term = dot_nt(stacked.astype(jnp.bfloat16), w_out[:, tile])
            pool[...] = term if t == 0 else pool[...] + term

    by_section(sel_ref, 1, work, (own_in, own_out), (other_in, other_out))


def reward_forward(parts, tokens, gain, own, other, sel):
    rows, width = parts[0].shape
    hidden, n = own[0].shape[1], len(parts)
    images = n * rows // tokens
    outs = run(
        functools.partial(reward_body, n, tokens),
        "reward_forward",
        sel,
        [*parts, gain, *own, *other],
        [bf16(rows, hidden)] * n
        + [jax.ShapeDtypeStruct((-(-images // 8) * 8, width), jnp.float32)],
        [pltpu.VMEM((n * rows, width), jnp.bfloat16)],
        2 * n * rows * width * hidden,
        2 * n * rows * hidden,
    )
    return outs[:n], outs[n][:images]


def back_body(count, tokens, sel_ref, *refs):
    g_tok = refs[0]
    slopes = refs[1 : count + 1]
    own_in, own_out, other_in, other_out = refs[count + 1 : count + 5]
    outs, acc = refs[count + 5 : 2 * count + 5], refs[2 * count + 5]
    rows = slopes[0].shape[0]
    per = rows // tokens

    def work(w_in, w_out):
        for t, tile in enumerate(tiles(w_in.shape[1])):
            g_h = dot_nn(g_tok[...], w_out[:, tile])
            terms = []
            for i in range(count):
                for image in range(per):
                    at = i * per + image
                    slope = slopes[i][image * tokens : (image + 1) * tokens, tile]
                    terms.append(
                        (slope.astype(jnp.float32) * g_h[at : at + 1, :]).astype(jnp.bfloat16)
                    )
            term = dot_nt(jnp.concatenate(terms, axis=0), w_in[:, tile])
            acc[...] = term if t == 0 else acc[...] + term

    by_section(sel_ref, 1, work, (own_in, own_out), (other_in, other_out))
    for i, out in enumerate(outs):
        out[...] = acc[i * rows : (i + 1) * rows, :].astype(jnp.bfloat16)


def reward_back(g_tok, slopes, tokens, own, other, sel):
    rows, hidden = slopes[0].shape
    width, n = own[0].shape[0], len(slopes)
    return run(
        functools.partial(back_body, n, tokens),
        "reward_back",
        sel,
        [g_tok, *slopes, *own, *other],
        [bf16(rows, width)] * n,
        [pltpu.VMEM((n * rows, width), jnp.float32)],
        2 * n * rows * width * hidden,
    )


def put_rows(result, core, keep, away, tile):
    groups, rows, unused = keep.shape
    for g in range(groups):
        even = result[2 * g * rows : (2 * g + 1) * rows, :]
        odd = result[(2 * g + 1) * rows : (2 * g + 2) * rows, :]
        keep[g, :, tile] = jnp.where(core == 0, even, odd).astype(jnp.bfloat16)
        away[g, :, tile] = jnp.where(core == 0, odd, even).astype(jnp.bfloat16)


def grad_out_body(count, sel_ref, *refs):
    pieces, acts = refs[: 2 * count], refs[2 * count : 3 * count]
    keep, away, turned, state = refs[3 * count :]
    share = turned.shape[0]
    rows = acts[0].shape[0]
    start = pl.multiple_of(sel_ref[0] * share, share)
    cols = jnp.concatenate([piece[:, pl.ds(start, share)] for piece in pieces], axis=0)
    turned[...] = cols.T
    for i, part in enumerate(acts):
        state[i * rows : (i + 1) * rows, :] = part[...]
    for tile in tiles(state.shape[1]):
        put_rows(dot_nn(turned[...], state[:, tile]), sel_ref[1], keep, away, tile)


def grad_in_body(count, sel_ref, *refs):
    pieces, slopes = refs[: 2 * count], refs[2 * count : 3 * count]
    xn_cols = refs[3 * count : 4 * count]
    own, other, keep, away, g_all, turned = refs[4 * count :]
    rows = pieces[0].shape[0]
    wide = xn_cols[0].shape[1]
    for i, piece in enumerate(pieces):
        g_all[i * rows : (i + 1) * rows, :] = piece[...]
    for i, part in enumerate(xn_cols):
        turned[:, i * wide : (i + 1) * wide] = part[...]

    def work(weight):
        for tile in tiles(weight.shape[1]):
            g_h = dot_nn(g_all[...], weight[:, tile])
            slope = jnp.concatenate([part[:, tile] for part in slopes], axis=0)
            g_hidden = (g_h * slope.astype(jnp.float32)).astype(jnp.bfloat16)
            put_rows(dot_nn(turned[...], g_hidden), sel_ref[1], keep, away, tile)

    by_section(sel_ref, 0, work, (own,), (other,))


def gradient_outs(width, hidden):
    groups = lax.axis_size("dp") // 2
    return [bf16(groups, width // 2 // (2 * groups), hidden)] * 2


def grad_out_parts(pieces, acts, sel):
    rows, width = pieces[0].shape
    total, hidden = rows * len(pieces), acts[0].shape[1]
    return run(
        functools.partial(grad_out_body, len(acts)),
        "grad_out",
        sel,
        [*pieces, *acts],
        gradient_outs(width, hidden),
        [
            pltpu.VMEM((width // 2, total), jnp.bfloat16),
            pltpu.VMEM((total, hidden), jnp.bfloat16),
        ],
        total * width * hidden,
    )


def grad_in_parts(pieces, slopes, xn_cols, own, other, sel):
    rows, width = pieces[0].shape
    total, hidden = rows * len(pieces), slopes[0].shape[1]
    return run(
        functools.partial(grad_in_body, len(slopes)),
        "grad_in",
        sel,
        [*pieces, *slopes, *xn_cols, own, other],
        gradient_outs(width, hidden),
        [
            pltpu.VMEM((total, width), jnp.bfloat16),
            pltpu.VMEM((width // 2, total), jnp.bfloat16),
        ],
        3 * total * width * hidden,
    )


def sum_over_dp(keep, away):
    groups = keep.shape[0]
    place = lax.axis_index("dp") // 2
    chip = keep.astype(jnp.float32) + swapped(away, "dp", 1).astype(jnp.float32)
    total = lax.dynamic_index_in_dim(chip, place, 0, keepdims=False)
    sent = chip.astype(jnp.bfloat16)
    for k in range(1, groups):
        part = lax.dynamic_index_in_dim(sent, (place + k) % groups, 0, keepdims=False)
        total = total + rotated(part, "dp", 2 * k).astype(jnp.float32)
    return total


def score_of(pooled, text):
    unit_img = pooled * lax.rsqrt(jnp.mean(pooled * pooled, axis=-1, keepdims=True) + EPS)
    unit_txt = text * lax.rsqrt(jnp.mean(text * text, axis=-1, keepdims=True) + EPS)
    return 100.0 * jnp.sum(unit_img * unit_txt, axis=-1) / pooled.shape[-1]


def on_device(latents, timesteps, prompt_ids, prompt_table, gains, w_in, w_out):
    count, tokens, width = latents.shape
    half = count // 2
    n_tp = lax.axis_size("tp")
    segment = lax.axis_index("sec")
    first = segment == 0
    core = lax.axis_index("dp") % 2
    place = lax.axis_index("dp") % 4
    sel = jnp.stack([segment, core, place]).astype(jnp.int32)
    own = (w_in[0], w_out[0])
    theta = math.pi / 2.0 * (timesteps.astype(jnp.float32) + 1.0) / (STEPS + 1.0)
    alpha = jnp.cos(theta)[:, None, None]
    sigma = jnp.sin(theta)[:, None, None]

    flat = latents.reshape(count * tokens, width)
    got_in = swapped(quarter(own[0], place), "sec", 1)
    lat_parts = gather_chain(flat)
    out_quarter, got_in = lax.optimization_barrier((quarter(own[1], place), got_in))
    across_in = swapped(got_in, "dp", 2)
    got_out = swapped(out_quarter, "sec", 1)
    across_out = swapped(got_out, "dp", 2)

    onehot = (
        prompt_ids[:, None] == jnp.arange(prompt_table.shape[0], dtype=jnp.int32)[None, :]
    ).astype(jnp.bfloat16)
    text = dot_nn(onehot, prompt_table)
    text_mine = jnp.where(first, text[half:], text[:half])

    near = [k for k in range(1, n_tp) if 2 * k != n_tp]
    far = [k for k in range(1, n_tp) if 2 * k == n_tp]
    eps_parts = [None] * n_tp
    results = []
    for ks, hop in ((near, got_in), (far, None), ([0], got_out)):
        if ks:
            operands, unused = lax.optimization_barrier(
                ([lat_parts[k] for k in ks], (hop, results))
            )
            results = block0_partials(operands, gains[:1], *own, sel)
            for k, result in zip(ks, results):
                eps_parts[k] = result
    eps_mix = reduce_parts(eps_parts).reshape(count, tokens, width)
    other = (assembled(got_in, across_in, place), assembled(got_out, across_out, place))
    base = latents.astype(jnp.float32)
    images = ((base - sigma * (base + eps_mix)) / alpha).astype(jnp.bfloat16)

    arrived = lax.ppermute(images[:half], "sec", [(0, 1)])
    mine = jnp.where(first, images[half:], arrived)
    ratio = jnp.where(first, (sigma / alpha)[half:], (sigma / alpha)[:half])
    mine_rows = mine.reshape(half * tokens, width)
    seen_parts = gather_parts(mine_rows)

    states = [
        block0_state(jnp.concatenate(part, 0), gains[:1], own[0], other[0], sel)
        for part in lat_parts
    ]
    slopes1, pool_parts = [None] * n_tp, [None] * n_tp
    for ks in ([0] + near, far):
        if ks:
            operands = [seen_parts[k] for k in ks]
            some_slopes, some_pools = reward_forward(
                operands, tokens, gains[1:], own, other, sel
            )
            for i, k in enumerate(ks):
                slopes1[k] = some_slopes[i]
                pool_parts[k] = some_pools[i * half : (i + 1) * half]
    pool_part = jnp.concatenate(pool_parts, 0)
    with_text = jnp.concatenate([pool_part, text_mine], 0)
    pool, texts = pool_part, [text_mine]
    for k in range(1, n_tp):
        theirs = rotated(with_text, "tp", k)
        pool = pool + jnp.roll(theirs[: n_tp * half], k * half, axis=0)
        texts.append(theirs[n_tp * half :])
    text_all = jnp.concatenate(texts, 0)
    seen_mean = [
        jnp.mean(part.astype(jnp.float32).reshape(half, tokens, width), axis=1)
        for part in seen_parts
    ]
    pooled = pool + jnp.concatenate(seen_mean, 0)
    g_pooled = jax.grad(lambda p: -jnp.sum(score_of(p, text_all)))(pooled)
    g_mean = g_pooled / tokens
    padded = -(-n_tp * half // 16) * 16
    g_tok = jnp.pad(g_mean.astype(jnp.bfloat16), ((0, padded - n_tp * half), (0, 0)))
    g_parts = reward_back(g_tok, slopes1, tokens, own, other, sel)
    g_xn, unused = lax.optimization_barrier((reduce_parts(g_parts), states))
    seen = mine_rows.astype(jnp.float32)
    scale1 = lax.rsqrt(jnp.mean(seen * seen, axis=-1, keepdims=True) + EPS)
    weighted = gains[1] * g_xn
    g_norm = scale1 * weighted - seen * scale1**3 * jnp.mean(
        seen * weighted, axis=-1, keepdims=True
    )
    g_images = (g_mean[:half, None, :] + g_norm.reshape(half, tokens, width)).astype(jnp.bfloat16)
    g_eps = (-ratio * g_images.astype(jnp.float32)).astype(jnp.bfloat16)

    pieces = []
    for part in gather_parts(g_eps.reshape(half * tokens, width)):
        pieces += [part, swapped(part, "sec", 1)]
    out_parts = grad_out_parts(pieces, [state[0] for state in states], sel)
    slopes0, xn_cols = [state[1] for state in states], [state[2] for state in states]
    out_parts, slopes0 = lax.optimization_barrier((out_parts, slopes0))
    in_parts = grad_in_parts(pieces, slopes0, xn_cols, own[1], other[1], sel)
    grad_out, grad_in = sum_over_dp(*out_parts), sum_over_dp(*in_parts)
    return (grad_in, grad_out)


def solution(mesh):
    in_specs = (
        P(("dp", "tp"), None, None),
        P(("dp", "tp")),
        P(("dp", "tp")),
        P(),
        P(),
        P("sec", None, "tp"),
        P("sec", None, "tp"),
    )
    out_specs = (P(("sec", "dp"), "tp"), P(("sec", "dp"), "tp"))
    return jax.shard_map(
        on_device, mesh=mesh, in_specs=in_specs, out_specs=out_specs, check_vma=False
    )
```

```python
import functools
import math

import jax
import jax.numpy as jnp
from jax import lax
from jax.experimental import pallas as pl
from jax.experimental.pallas import tpu as pltpu
from jax.sharding import PartitionSpec as P

STEPS = 50


EPS = 1e-06
VMEM_BYTES = 8 * 1024 * 1024


def rotated(value, axis, steps):
    count = lax.axis_size(axis)
    return lax.ppermute(value, axis, [(i, (i + steps) % count) for i in range(count)])


def swapped(value, axis, bit):
    count = lax.axis_size(axis)
    return lax.ppermute(value, axis, [(i, i ^ bit) for i in range(count)])


def gather_parts(piece):
    return [piece] + [rotated(piece, "tp", k) for k in range(1, lax.axis_size("tp"))]


def to_second(value, steps):
    count = lax.axis_size("tp")
    return lax.ppermute(
        value, ("sec", "tp"), [(i, count + (i + steps) % count) for i in range(count)]
    )


def reduce_parts(parts):
    total = parts[0].astype(jnp.float32)
    for k in range(1, len(parts)):
        total = total + rotated(parts[k], "tp", -k).astype(jnp.float32)
    return total


def quarter(weight, place):
    rows = weight.shape[0] // 4
    return lax.dynamic_slice_in_dim(weight, place * rows, rows, 0)


def gelu_pair(value):
    cdf = 0.5 * (1.0 + lax.erf(value * (1.0 / math.sqrt(2.0))))
    density = jnp.exp(-0.5 * value * value) * (1.0 / math.sqrt(2.0 * math.pi))
    return (value * cdf, cdf + value * density)


def normed(rows, gain):
    scale = lax.rsqrt(jnp.mean(rows * rows, axis=-1, keepdims=True) + EPS)
    return (rows * scale * gain).astype(jnp.bfloat16)


def dot_nn(a, b):
    return jnp.dot(a, b, preferred_element_type=jnp.float32)


def dot_nt(a, b):
    return lax.dot_general(a, b, (((1,), (1,)), ((), ())), preferred_element_type=jnp.float32)


def tile_of(hidden):
    for tile in (256, 128):
        if hidden % tile == 0:
            return tile
    return hidden


IN_VMEM = pl.BlockSpec(memory_space=pltpu.VMEM)
IN_SMEM = pl.BlockSpec(memory_space=pltpu.SMEM)


def run(body, name, sel, operands, outs, scratch, flops, elements=0):
    read = sum(x.size * x.dtype.itemsize for x in operands)
    written = sum(math.prod(o.shape) * o.dtype.itemsize for o in outs)
    return pl.pallas_call(
        body,
        in_specs=[IN_SMEM] + [IN_VMEM] * len(operands),
        out_specs=[IN_VMEM] * len(outs),
        scratch_shapes=scratch,
        out_shape=outs,
        compiler_params=pltpu.CompilerParams(vmem_limit_bytes=VMEM_BYTES),
        cost_estimate=pl.CostEstimate(
            flops=flops, bytes_accessed=read + written, transcendentals=elements
        ),
        name=name,
    )(sel, *operands)


def bf16(*shape):
    return jax.ShapeDtypeStruct(shape, jnp.bfloat16)


def tiles(hidden):
    tile = tile_of(hidden)
    return [slice(t, t + tile) for t in range(0, hidden, tile)]


def by_section(sel_ref, section, work, own, other):
    @pl.when(sel_ref[0] == section)
    def _():
        work(*own)

    @pl.when(sel_ref[0] != section)
    def _():
        work(*other)


def assemble_body(sel_ref, p0, p1, p2, p3, out):
    rows = p0.shape[0]
    for q, piece in enumerate((p0, p1, p2, p3)):
        out[pl.ds(pl.multiple_of((sel_ref[2] ^ q) * rows, rows), rows), :] = piece[...]


def assembled(got, across, sel):
    pieces = [got, swapped(got, "dp", 1), across, swapped(across, "dp", 1)]
    out = bf16(4 * got.shape[0], got.shape[1])
    return run(assemble_body, "assemble", sel, pieces, [out], [], 0)[0]


def partial_body(count, sel_ref, *refs):
    parts, (gain, w_in, w_out) = refs[:count], refs[count : count + 3]
    outs, (xn, acc) = refs[count + 3 : -2], refs[-2:]
    rows = parts[0].shape[0]
    for i, part in enumerate(parts):
        xn[i * rows : (i + 1) * rows, :] = normed(part[...].astype(jnp.float32), gain[...])
    for t, tile in enumerate(tiles(w_in.shape[1])):
        act, unused = gelu_pair(dot_nn(xn[...], w_in[:, tile]))
        term = dot_nt(act.astype(jnp.bfloat16), w_out[:, tile])
        acc[...] = term if t == 0 else acc[...] + term
    late = rows // 2
    for i, out in enumerate(outs):
        out[...] = acc[i * late : (i + 1) * late, :].astype(jnp.bfloat16)


def block0_partials(parts, gain, w_in, w_out, sel):
    rows, width = parts[0].shape
    hidden, n = w_in.shape[1], len(parts)
    outs = run(
        functools.partial(partial_body, n),
        "block0_partial",
        sel,
        [*parts, gain, w_in, w_out],
        [bf16(rows // 2, width)] * (2 * n),
        [
            pltpu.VMEM((n * rows, width), jnp.bfloat16),
            pltpu.VMEM((n * rows, width), jnp.float32),
        ],
        4 * n * rows * width * hidden,
        n * rows * hidden,
    )
    return [(outs[2 * i], outs[2 * i + 1]) for i in range(n)]


def state_body(count, sel_ref, *refs):
    parts = refs[:count]
    gain, own, other, act, slope, xn_cols, xn = refs[count:]
    rows = parts[0].shape[0]
    late = rows // 2
    share = xn_cols.shape[0]
    mine = pl.multiple_of((1 - sel_ref[0]) * late, late)
    theirs = pl.multiple_of(sel_ref[0] * late, late)
    for i, part in enumerate(parts):
        for j, start in enumerate((mine, theirs)):
            at = i * rows + j * late
            xn[at : at + late, :] = normed(
                part[pl.ds(start, late), :].astype(jnp.float32), gain[...]
            )
    cols = xn[:, pl.ds(pl.multiple_of(sel_ref[0] * share, share), share)]
    xn_cols[...] = cols.T

    def work(weight):
        for tile in tiles(weight.shape[1]):
            value, grad = gelu_pair(dot_nn(xn[...], weight[:, tile]))
            act[:, tile] = value.astype(jnp.bfloat16)
            slope[:, tile] = grad.astype(jnp.bfloat16)

    by_section(sel_ref, 0, work, (own,), (other,))


def block0_state(parts, gain, own, other, sel):
    total, width = sum(part.shape[0] for part in parts), parts[0].shape[1]
    hidden = own.shape[1]
    return run(
        functools.partial(state_body, len(parts)),
        "block0_state",
        sel,
        [*parts, gain, own, other],
        [bf16(total, hidden), bf16(total, hidden), bf16(width // 2, total)],
        [pltpu.VMEM((total, width), jnp.bfloat16)],
        2 * total * width * hidden,
        2 * total * hidden,
    )


def reward_body(count, tokens, sel_ref, *refs):
    parts, gain = refs[:count], refs[count]
    own_in, own_out, other_in, other_out = refs[count + 1 : count + 5]
    slopes, (pool, xn) = refs[count + 5 : 2 * count + 5], refs[2 * count + 5 :]
    rows = parts[0].shape[0]
    for i, part in enumerate(parts):
        xn[i * rows : (i + 1) * rows, :] = normed(part[...].astype(jnp.float32), gain[...])

    def work(w_in, w_out):
        for t, tile in enumerate(tiles(w_in.shape[1])):
            act, grad = gelu_pair(dot_nn(xn[...], w_in[:, tile]))
            for i in range(count):
                slopes[i][:, tile] = grad[i * rows : (i + 1) * rows, :].astype(jnp.bfloat16)
            means = [
                jnp.mean(act[start : start + tokens, :], axis=0, keepdims=True)
                for start in range(0, count * rows, tokens)
            ]
            row = lax.broadcasted_iota(jnp.int32, (pool.shape[0], act.shape[1]), 0)
            stacked = jnp.zeros(row.shape, jnp.float32)
            for i, mean in enumerate(means):
                stacked = jnp.where(row == i, mean, stacked)
            term = dot_nt(stacked.astype(jnp.bfloat16), w_out[:, tile])
            pool[...] = term if t == 0 else pool[...] + term

    by_section(sel_ref, 1, work, (own_in, own_out), (other_in, other_out))


def reward_forward(parts, tokens, gain, own, other, sel):
    rows, width = parts[0].shape
    hidden, n = own[0].shape[1], len(parts)
    images = n * rows // tokens
    outs = run(
        functools.partial(reward_body, n, tokens),
        "reward_forward",
        sel,
        [*parts, gain, *own, *other],
        [bf16(rows, hidden)] * n
        + [jax.ShapeDtypeStruct((-(-images // 8) * 8, width), jnp.float32)],
        [pltpu.VMEM((n * rows, width), jnp.bfloat16)],
        2 * n * rows * width * hidden,
        2 * n * rows * hidden,
    )
    return outs[:n], outs[n][:images]


def back_body(count, tokens, sel_ref, *refs):
    g_tok = refs[0]
    slopes = refs[1 : count + 1]
    own_in, own_out, other_in, other_out = refs[count + 1 : count + 5]
    outs, acc = refs[count + 5 : 2 * count + 5], refs[2 * count + 5]
    rows = slopes[0].shape[0]
    per = rows // tokens

    def work(w_in, w_out):
        for t, tile in enumerate(tiles(w_in.shape[1])):
            g_h = dot_nn(g_tok[...], w_out[:, tile])
            terms = []
            for i in range(count):
                for image in range(per):
                    at = i * per + image
                    slope = slopes[i][image * tokens : (image + 1) * tokens, tile]
                    terms.append(
                        (slope.astype(jnp.float32) * g_h[at : at + 1, :]).astype(jnp.bfloat16)
                    )
            term = dot_nt(jnp.concatenate(terms, axis=0), w_in[:, tile])
            acc[...] = term if t == 0 else acc[...] + term

    by_section(sel_ref, 1, work, (own_in, own_out), (other_in, other_out))
    for i, out in enumerate(outs):
        out[...] = acc[i * rows : (i + 1) * rows, :].astype(jnp.bfloat16)


def reward_back(g_tok, slopes, tokens, own, other, sel):
    rows, hidden = slopes[0].shape
    width, n = own[0].shape[0], len(slopes)
    return run(
        functools.partial(back_body, n, tokens),
        "reward_back",
        sel,
        [g_tok, *slopes, *own, *other],
        [bf16(rows, width)] * n,
        [pltpu.VMEM((n * rows, width), jnp.float32)],
        2 * n * rows * width * hidden,
    )


def put_rows(result, core, keep, away, tile):
    groups, rows, unused = keep.shape
    for g in range(groups):
        even = result[2 * g * rows : (2 * g + 1) * rows, :]
        odd = result[(2 * g + 1) * rows : (2 * g + 2) * rows, :]
        keep[g, :, tile] = jnp.where(core == 0, even, odd).astype(jnp.bfloat16)
        away[g, :, tile] = jnp.where(core == 0, odd, even).astype(jnp.bfloat16)


def gradient_body(count, sel_ref, *refs):
    pieces = refs[:count]
    act, slope, xn_cols, own, other = refs[count : count + 5]
    out_keep, out_away, in_keep, in_away, g_all, turned = refs[count + 5 :]
    rows = pieces[0].shape[0]
    share = turned.shape[0]
    core = sel_ref[1]
    for i, piece in enumerate(pieces):
        g_all[i * rows : (i + 1) * rows, :] = piece[...]
    cols = g_all[:, pl.ds(pl.multiple_of(sel_ref[0] * share, share), share)]
    turned[...] = cols.T

    def work(weight):
        for tile in tiles(weight.shape[1]):
            put_rows(dot_nn(turned[...], act[:, tile]), core, out_keep, out_away, tile)
            g_h = dot_nn(g_all[...], weight[:, tile])
            g_hidden = (g_h * slope[:, tile].astype(jnp.float32)).astype(jnp.bfloat16)
            put_rows(dot_nn(xn_cols[...], g_hidden), core, in_keep, in_away, tile)

    by_section(sel_ref, 0, work, (own,), (other,))


def gradients(pieces, states, own, other, sel):
    rows, width = pieces[0].shape
    total, hidden = rows * len(pieces), own.shape[1]
    groups = lax.axis_size("dp") // 2
    outs = run(
        functools.partial(gradient_body, len(pieces)),
        "gradients",
        sel,
        [*pieces, *states, own, other],
        [bf16(groups, width // 2 // (2 * groups), hidden)] * 4,
        [
            pltpu.VMEM((total, width), jnp.bfloat16),
            pltpu.VMEM((width // 2, total), jnp.bfloat16),
        ],
        4 * total * width * hidden,
    )
    return outs[:2], outs[2:]


def sum_over_dp(keep, away):
    groups = keep.shape[0]
    place = lax.axis_index("dp") // 2
    chip = keep.astype(jnp.float32) + swapped(away, "dp", 1).astype(jnp.float32)
    total = lax.dynamic_index_in_dim(chip, place, 0, keepdims=False)
    sent = chip.astype(jnp.bfloat16)
    for k in range(1, groups):
        part = lax.dynamic_index_in_dim(sent, (place + k) % groups, 0, keepdims=False)
        total = total + rotated(part, "dp", 2 * k).astype(jnp.float32)
    return total


def score_of(pooled, text):
    unit_img = pooled * lax.rsqrt(jnp.mean(pooled * pooled, axis=-1, keepdims=True) + EPS)
    unit_txt = text * lax.rsqrt(jnp.mean(text * text, axis=-1, keepdims=True) + EPS)
    return 100.0 * jnp.sum(unit_img * unit_txt, axis=-1) / pooled.shape[-1]


def on_device(latents, timesteps, prompt_ids, prompt_table, gains, w_in, w_out):
    count, tokens, width = latents.shape
    half = count // 2
    n_tp = lax.axis_size("tp")
    segment = lax.axis_index("sec")
    first = segment == 0
    core = lax.axis_index("dp") % 2
    place = lax.axis_index("dp") % 4
    sel = jnp.stack([segment, core, place]).astype(jnp.int32)
    own = (w_in[0], w_out[0])

    def my_half(value):
        return jnp.where(first, value[half:], value[:half])

    theta = math.pi / 2.0 * (my_half(timesteps).astype(jnp.float32) + 1.0) / (STEPS + 1.0)
    alpha = jnp.cos(theta)[:, None, None]
    sigma = jnp.sin(theta)[:, None, None]

    flat = latents.reshape(count * tokens, width)
    lat_parts = gather_parts(flat)
    got_in = swapped(quarter(own[0], place), "sec", 1)
    out_quarter, lat_parts[1], lat_parts[-1] = lax.optimization_barrier(
        (quarter(own[1], place), lat_parts[1], lat_parts[-1])
    )
    across_in = swapped(got_in, "dp", 2)
    got_out = lax.ppermute(out_quarter, "sec", [(1, 0)])
    across_out = swapped(got_out, "dp", 2)

    onehot = (
        my_half(prompt_ids)[:, None] == jnp.arange(prompt_table.shape[0], dtype=jnp.int32)[None, :]
    ).astype(jnp.bfloat16)
    text_mine = dot_nn(onehot, prompt_table)

    near = [k for k in range(1, n_tp) if 2 * k != n_tp]
    far = [k for k in range(1, n_tp) if 2 * k == n_tp]
    eps_parts = [None] * n_tp
    results = []
    for ks, hop in ((near, got_in), ([0], None), (far, None)):
        if ks:
            operands, unused = lax.optimization_barrier(
                ([lat_parts[k] for k in ks], (hop, results))
            )
            results = block0_partials(operands, gains[:1], *own, sel)
            for k, result in zip(ks, results):
                eps_parts[k] = result
    stay = reduce_parts([part[1] for part in eps_parts])
    leave = [to_second(part[0], -k).astype(jnp.float32) for k, part in enumerate(eps_parts)]
    eps_mix = jnp.where(first, stay, sum(leave)).reshape(half, tokens, width)
    base = my_half(latents).astype(jnp.float32)
    mine = ((base - sigma * (base + eps_mix)) / alpha).astype(jnp.bfloat16)
    mine_rows = mine.reshape(half * tokens, width)

    other = (assembled(got_in, across_in, sel), assembled(got_out, across_out, sel))
    seen_parts = gather_parts(mine_rows)
    slopes1, pool_parts = [None] * n_tp, [None] * n_tp
    for ks in ([0] + near, far):
        if ks:
            operands = [seen_parts[k] for k in ks]
            some_slopes, some_pools = reward_forward(
                operands, tokens, gains[1:], own, other, sel
            )
            for i, k in enumerate(ks):
                slopes1[k] = some_slopes[i]
                pool_parts[k] = some_pools[i * half : (i + 1) * half]
    pool_part = jnp.concatenate(pool_parts, 0)
    with_text = jnp.concatenate([pool_part, text_mine], 0)
    pool, texts = pool_part, [text_mine]
    for k in range(1, n_tp):
        theirs = rotated(with_text, "tp", k)
        pool = pool + jnp.roll(theirs[: n_tp * half], k * half, axis=0)
        texts.append(theirs[n_tp * half :])
    text_all = jnp.concatenate(texts, 0)
    seen_mean = [
        jnp.mean(part.astype(jnp.float32).reshape(half, tokens, width), axis=1)
        for part in seen_parts
    ]
    pooled = pool + jnp.concatenate(seen_mean, 0)
    g_pooled = jax.grad(lambda p: -jnp.sum(score_of(p, text_all)))(pooled)
    g_mean = g_pooled / tokens
    padded = -(-n_tp * half // 16) * 16
    g_tok = jnp.pad(g_mean.astype(jnp.bfloat16), ((0, padded - n_tp * half), (0, 0)))
    g_parts = reward_back(g_tok, slopes1, tokens, own, other, sel)

    states = block0_state(lat_parts, gains[:1], own[0], other[0], sel)
    late_quarter, unused = lax.optimization_barrier((out_quarter, mine_rows))
    got_late = lax.ppermute(late_quarter, "sec", [(0, 1)])

    g_xn, states, got_late = lax.optimization_barrier(
        (reduce_parts(g_parts), states, got_late)
    )
    across_late = swapped(got_late, "dp", 2)
    seen = mine_rows.astype(jnp.float32)
    scale1 = lax.rsqrt(jnp.mean(seen * seen, axis=-1, keepdims=True) + EPS)
    weighted = gains[1] * g_xn
    g_norm = scale1 * weighted - seen * scale1**3 * jnp.mean(
        seen * weighted, axis=-1, keepdims=True
    )
    g_images = (g_mean[:half, None, :] + g_norm.reshape(half, tokens, width)).astype(jnp.bfloat16)
    g_eps = (-(sigma / alpha) * g_images.astype(jnp.float32)).astype(jnp.bfloat16)

    pieces = []
    for part in gather_parts(g_eps.reshape(half * tokens, width)):
        pieces += [part, swapped(part, "sec", 1)]
    other_out = assembled(got_late, across_late, sel)
    out_parts, in_parts = gradients(pieces, states, own[1], other_out, sel)
    grad_out, grad_in = sum_over_dp(*out_parts), sum_over_dp(*in_parts)
    return (grad_in, grad_out)


def solution(mesh):
    in_specs = (
        P(("dp", "tp"), None, None),
        P(("dp", "tp")),
        P(("dp", "tp")),
        P(),
        P(),
        P("sec", None, "tp"),
        P("sec", None, "tp"),
    )
    out_specs = (P(("sec", "dp"), "tp"), P(("sec", "dp"), "tp"))
    return jax.shard_map(
        on_device, mesh=mesh, in_specs=in_specs, out_specs=out_specs, check_vma=False
    )
```

```python
import functools
import math

import jax
import jax.numpy as jnp
from jax import lax
from jax.experimental import pallas as pl
from jax.experimental.pallas import tpu as pltpu
from jax.sharding import PartitionSpec as P

STEPS = 50


EPS = 1e-06
VMEM_BYTES = 8 * 1024 * 1024


def rotated(value, axis, steps):
    count = lax.axis_size(axis)
    return lax.ppermute(value, axis, [(i, (i + steps) % count) for i in range(count)])


def swapped(value, axis, bit):
    count = lax.axis_size(axis)
    return lax.ppermute(value, axis, [(i, i ^ bit) for i in range(count)])


def gather_parts(piece):
    return [piece] + [rotated(piece, "tp", k) for k in range(1, lax.axis_size("tp"))]


def own_share(weight):
    rows = weight.shape[0] // lax.axis_size("dp")
    return lax.dynamic_slice_in_dim(weight, lax.axis_index("dp") * rows, rows, 0)


def joined(share):
    return lax.all_gather(share, "dp", axis=0, tiled=True)


def gelu_pair(value):
    cdf = 0.5 * (1.0 + lax.erf(value * (1.0 / math.sqrt(2.0))))
    density = jnp.exp(-0.5 * value * value) * (1.0 / math.sqrt(2.0 * math.pi))
    return (value * cdf, cdf + value * density)


def normed(rows, gain):
    scale = lax.rsqrt(jnp.mean(rows * rows, axis=-1, keepdims=True) + EPS)
    return (rows * scale * gain).astype(jnp.bfloat16)


def dot_nn(a, b):
    return jnp.dot(a, b, preferred_element_type=jnp.float32)


def dot_nt(a, b):
    return lax.dot_general(a, b, (((1,), (1,)), ((), ())), preferred_element_type=jnp.float32)


def tile_of(hidden):
    for tile in (256, 128):
        if hidden % tile == 0:
            return tile
    return hidden


IN_VMEM = pl.BlockSpec(memory_space=pltpu.VMEM)
IN_SMEM = pl.BlockSpec(memory_space=pltpu.SMEM)


def run(body, name, sel, operands, outs, scratch):
    return pl.pallas_call(
        body,
        in_specs=[IN_SMEM] + [IN_VMEM] * len(operands),
        out_specs=[IN_VMEM] * len(outs),
        scratch_shapes=scratch,
        out_shape=outs,
        compiler_params=pltpu.CompilerParams(vmem_limit_bytes=VMEM_BYTES),
        name=name,
    )(sel, *operands)


def bf16(*shape):
    return jax.ShapeDtypeStruct(shape, jnp.bfloat16)


def tiles(hidden):
    tile = tile_of(hidden)
    return [slice(t, t + tile) for t in range(0, hidden, tile)]


def by_section(sel_ref, section, work, own, other):
    @pl.when(sel_ref[0] == section)
    def _():
        work(*own)

    @pl.when(sel_ref[0] != section)
    def _():
        work(*other)


def partial_body(count, sel_ref, *refs):
    parts, (gain, w_in, w_out) = refs[:count], refs[count : count + 3]
    stay, leave, xn, acc = refs[count + 3 :]
    rows = parts[0].shape[0]
    late = rows // 2
    for i, part in enumerate(parts):
        xn[i * rows : (i + 1) * rows, :] = normed(part[...].astype(jnp.float32), gain[...])
    for t, tile in enumerate(tiles(w_in.shape[1])):
        act, unused = gelu_pair(dot_nn(xn[...], w_in[:, tile]))
        term = dot_nt(act.astype(jnp.bfloat16), w_out[:, tile])
        acc[...] = term if t == 0 else acc[...] + term
    for i in range(count):
        start = i * rows
        leave[i] = acc[start : start + late, :].astype(jnp.bfloat16)
        stay[i] = acc[start + late : start + rows, :].astype(jnp.bfloat16)


def block0_partials(parts, gain, w_in, w_out, sel):
    rows, width = parts[0].shape
    hidden, n = w_in.shape[1], len(parts)
    return run(
        functools.partial(partial_body, n),
        "block0_partial",
        sel,
        [*parts, gain, w_in, w_out],
        [bf16(n, rows // 2, width)] * 2,
        [
            pltpu.VMEM((n * rows, width), jnp.bfloat16),
            pltpu.VMEM((n * rows, width), jnp.float32),
        ],
    )


def denoise_body(tokens, count, sel_ref, *refs):
    latents, sigma, alpha = refs[:3]
    sums, out = refs[3 : 3 + count], refs[3 + count]
    late = out.shape[0]
    base = latents[pl.ds(pl.multiple_of((1 - sel_ref[0]) * late, late), late), :]
    base = base.astype(jnp.float32)
    eps = base
    for part in sums:
        eps = eps + part[...].astype(jnp.float32)
    out[...] = ((base - sigma[...] * eps) / alpha[...]).astype(jnp.bfloat16)


def denoised(latents, sigma, alpha, sums, tokens, sel):
    return run(
        functools.partial(denoise_body, tokens, len(sums)),
        "denoise",
        sel,
        [latents, sigma, alpha, *sums],
        [bf16(latents.shape[0] // 2, latents.shape[1])],
        [],
    )[0]


def crossing(count):
    near = [k for k in range(1, count) if 2 * k != count]
    return [0] + near + [k for k in range(1, count) if 2 * k == count]


def state_body(count, sel_ref, *refs):
    parts = refs[:count]
    gain, own, other, act, slope, xn_cols, xn = refs[count:]
    rows = parts[0].shape[0]
    late = rows // 2
    share = xn_cols.shape[0]
    mine = pl.multiple_of((1 - sel_ref[0]) * late, late)
    theirs = pl.multiple_of(sel_ref[0] * late, late)
    at = 0
    for start, order in ((mine, range(len(parts))), (theirs, crossing(len(parts)))):
        for k in order:
            rows_k = parts[k][pl.ds(start, late), :].astype(jnp.float32)
            xn[at : at + late, :] = normed(rows_k, gain[...])
            at += late
    cols = xn[:, pl.ds(pl.multiple_of(sel_ref[0] * share, share), share)]
    xn_cols[...] = cols.T

    def work(weight):
        for tile in tiles(weight.shape[1]):
            value, grad = gelu_pair(dot_nn(xn[...], weight[:, tile]))
            act[:, tile] = value.astype(jnp.bfloat16)
            slope[:, tile] = grad.astype(jnp.bfloat16)

    by_section(sel_ref, 0, work, (own,), (other,))


def block0_state(parts, gain, own, other, sel):
    total, width = sum(part.shape[0] for part in parts), parts[0].shape[1]
    hidden = own.shape[1]
    return run(
        functools.partial(state_body, len(parts)),
        "block0_state",
        sel,
        [*parts, gain, own, other],
        [bf16(total, hidden), bf16(total, hidden), bf16(width // 2, total)],
        [pltpu.VMEM((total, width), jnp.bfloat16)],
    )


def reward_body(count, tokens, sel_ref, *refs):
    parts, (gain, text) = refs[:count], refs[count : count + 2]
    own_in, own_out, other_in, other_out = refs[count + 2 : count + 6]
    slopes, (pool, xn) = refs[count + 6 : 2 * count + 6], refs[2 * count + 6 :]
    rows = parts[0].shape[0]
    half = rows // tokens
    row = lax.broadcasted_iota(jnp.int32, pool.shape, 0)
    start = jnp.zeros(pool.shape, jnp.float32)
    for image in range(half):
        own_rows = parts[0][image * tokens : (image + 1) * tokens, :].astype(jnp.float32)
        start = jnp.where(row == image, jnp.mean(own_rows, axis=0, keepdims=True), start)
        start = jnp.where(row == count * half + image, text[image : image + 1, :], start)
    pool[...] = start
    for i, part in enumerate(parts):
        xn[i * rows : (i + 1) * rows, :] = normed(part[...].astype(jnp.float32), gain[...])

    def work(w_in, w_out):
        for tile in tiles(w_in.shape[1]):
            act, grad = gelu_pair(dot_nn(xn[...], w_in[:, tile]))
            for i in range(count):
                slopes[i][:, tile] = grad[i * rows : (i + 1) * rows, :].astype(jnp.bfloat16)
            means = [
                jnp.mean(act[at : at + tokens, :], axis=0, keepdims=True)
                for at in range(0, count * rows, tokens)
            ]
            place = lax.broadcasted_iota(jnp.int32, (pool.shape[0], act.shape[1]), 0)
            stacked = jnp.zeros(place.shape, jnp.float32)
            for i, mean in enumerate(means):
                stacked = jnp.where(place == i, mean, stacked)
            pool[...] += dot_nt(stacked.astype(jnp.bfloat16), w_out[:, tile])

    by_section(sel_ref, 1, work, (own_in, own_out), (other_in, other_out))


def reward_forward(parts, tokens, gain, text, own, other, sel):
    rows, width = parts[0].shape
    hidden, n = own[0].shape[1], len(parts)
    images = (n + 1) * rows // tokens
    outs = run(
        functools.partial(reward_body, n, tokens),
        "reward_forward",
        sel,
        [*parts, gain, text, *own, *other],
        [bf16(rows, hidden)] * n
        + [jax.ShapeDtypeStruct((-(-images // 8) * 8, width), jnp.float32)],
        [pltpu.VMEM((n * rows, width), jnp.bfloat16)],
    )
    return outs[:n], outs[n]


def score_gradient(pooled, text):
    unit = text * lax.rsqrt(jnp.mean(text * text, axis=-1, keepdims=True) + EPS)
    scale = lax.rsqrt(jnp.mean(pooled * pooled, axis=-1, keepdims=True) + EPS)
    along = jnp.mean(pooled * unit, axis=-1, keepdims=True)
    return (-100.0 / pooled.shape[-1]) * (scale * unit - pooled * scale**3 * along)


def back_body(count, tokens, sel_ref, *refs):
    pools, slopes = refs[:count], refs[count : 2 * count]
    own_in, own_out, other_in, other_out = refs[2 * count : 2 * count + 4]
    outs = refs[2 * count + 4 : 3 * count + 4]
    g_mean, acc = refs[3 * count + 4 :]
    rows = slopes[0].shape[0]
    half = rows // tokens
    images = count * half
    pooled, texts = [], []
    for j in range(images):
        at = [(j - k * half) % images for k in range(count)]
        pooled.append(sum(pools[k][at[k] : at[k] + 1, :] for k in range(count)))
        text = images + j % half
        texts.append(pools[j // half][text : text + 1, :])
    padded = -(-images // 16) * 16
    row = lax.broadcasted_iota(jnp.int32, (padded, acc.shape[1]), 0)
    stacked, spoken = jnp.zeros(row.shape, jnp.float32), jnp.zeros(row.shape, jnp.float32)
    for j in range(images):
        stacked = jnp.where(row == j, pooled[j], stacked)
        spoken = jnp.where(row == j, texts[j], spoken)
    g_all = score_gradient(stacked, spoken) * (1.0 / tokens)
    g_mean[...] = g_all[: g_mean.shape[0], :]
    g_tok = g_all.astype(jnp.bfloat16)

    def work(w_in, w_out):
        for t, tile in enumerate(tiles(w_in.shape[1])):
            g_h = dot_nn(g_tok, w_out[:, tile])
            terms = []
            for i in range(count):
                for image in range(half):
                    at = i * half + image
                    slope = slopes[i][image * tokens : (image + 1) * tokens, tile]
                    terms.append(
                        (slope.astype(jnp.float32) * g_h[at : at + 1, :]).astype(jnp.bfloat16)
                    )
            term = dot_nt(jnp.concatenate(terms, axis=0), w_in[:, tile])
            acc[...] = term if t == 0 else acc[...] + term

    by_section(sel_ref, 1, work, (own_in, own_out), (other_in, other_out))
    for i, out in enumerate(outs):
        out[...] = acc[i * rows : (i + 1) * rows, :].astype(jnp.bfloat16)


def reward_back(pools, slopes, tokens, own, other, sel):
    rows, hidden = slopes[0].shape
    width, n = own[0].shape[0], len(slopes)
    outs = run(
        functools.partial(back_body, n, tokens),
        "reward_back",
        sel,
        [*pools, *slopes, *own, *other],
        [bf16(rows, width)] * n + [jax.ShapeDtypeStruct((8, width), jnp.float32)],
        [pltpu.VMEM((n * rows, width), jnp.float32)],
    )
    return outs[:n], outs[n]


def eps_gradient_body(tokens, count, sel_ref, *refs):
    seen_ref, g_mean, gain, ratio = refs[:4]
    sums, out = refs[4 : 4 + count], refs[4 + count]
    g_xn = sums[0][...].astype(jnp.float32)
    for part in sums[1:]:
        g_xn = g_xn + part[...].astype(jnp.float32)
    seen = seen_ref[...].astype(jnp.float32)
    scale = lax.rsqrt(jnp.mean(seen * seen, axis=-1, keepdims=True) + EPS)
    weighted = gain[...] * g_xn
    along = jnp.mean(seen * weighted, axis=-1, keepdims=True)
    g_norm = scale * weighted - seen * scale**3 * along
    for image in range(out.shape[0] // tokens):
        at = slice(image * tokens, (image + 1) * tokens)
        g_images = (g_mean[image : image + 1, :] + g_norm[at, :]).astype(jnp.bfloat16)
        out[at, :] = (ratio[at, :] * g_images.astype(jnp.float32)).astype(jnp.bfloat16)


def eps_gradient(seen, g_mean, gain, ratio, sums, tokens, sel):
    return run(
        functools.partial(eps_gradient_body, tokens, len(sums)),
        "eps_gradient",
        sel,
        [seen, g_mean, gain, ratio, *sums],
        [bf16(*seen.shape)],
        [],
    )[0]


def put_rows(result, core, keep, away, tile):
    groups, rows, unused = keep.shape
    for g in range(groups):
        even = result[2 * g * rows : (2 * g + 1) * rows, :]
        odd = result[(2 * g + 1) * rows : (2 * g + 2) * rows, :]
        keep[g, :, tile] = jnp.where(core == 0, even, odd).astype(jnp.bfloat16)
        away[g, :, tile] = jnp.where(core == 0, odd, even).astype(jnp.bfloat16)


def gradient_body(count, sel_ref, *refs):
    pieces = refs[:count]
    act, slope, xn_cols, own, other = refs[count : count + 5]
    out_keep, out_away, in_keep, in_away, g_all, turned = refs[count + 5 :]
    share = turned.shape[0]
    core = sel_ref[1]
    at = 0
    for piece in pieces:
        g_all[at : at + piece.shape[0], :] = piece[...]
        at += piece.shape[0]
    cols = g_all[:, pl.ds(pl.multiple_of(sel_ref[0] * share, share), share)]
    turned[...] = cols.T

    def work(weight):
        for tile in tiles(weight.shape[1]):
            put_rows(dot_nn(turned[...], act[:, tile]), core, out_keep, out_away, tile)
            g_h = dot_nn(g_all[...], weight[:, tile])
            g_hidden = (g_h * slope[:, tile].astype(jnp.float32)).astype(jnp.bfloat16)
            put_rows(dot_nn(xn_cols[...], g_hidden), core, in_keep, in_away, tile)

    by_section(sel_ref, 0, work, (own,), (other,))


def gradients(pieces, states, own, other, sel):
    total, width = sum(piece.shape[0] for piece in pieces), pieces[0].shape[1]
    hidden = own.shape[1]
    groups = lax.axis_size("dp") // 2
    outs = run(
        functools.partial(gradient_body, len(pieces)),
        "gradients",
        sel,
        [*pieces, *states, own, other],
        [bf16(groups, width // 2 // (2 * groups), hidden)] * 4,
        [
            pltpu.VMEM((total, width), jnp.bfloat16),
            pltpu.VMEM((width // 2, total), jnp.bfloat16),
        ],
    )
    return outs[:2], outs[2:]


def chip_body(sel_ref, keep, arrived, mine, others):
    groups = keep.shape[0]
    for k in range(groups):
        at = (sel_ref[2] + k) % groups
        total = keep[at].astype(jnp.float32) + arrived[at].astype(jnp.float32)
        if k == 0:
            mine[...] = total
        else:
            others[k - 1] = total.astype(jnp.bfloat16)


def sum_over_dp(keep, away, sel):
    groups, rows, hidden = keep.shape
    total, others = run(
        chip_body,
        "chip_sum",
        sel,
        [keep, swapped(away, "dp", 1)],
        [jax.ShapeDtypeStruct((rows, hidden), jnp.float32), bf16(groups - 1, rows, hidden)],
        [],
    )
    for k in range(1, groups):
        total = total + rotated(others[k - 1], "dp", 2 * k).astype(jnp.float32)
    return total


def on_device(latents, timesteps, prompt_ids, prompt_table, gains, w_in, w_out):
    count, tokens, width = latents.shape
    half = count // 2
    n_tp = lax.axis_size("tp")
    segment = lax.axis_index("sec")
    first = segment == 0
    dp = lax.axis_index("dp")
    sel = jnp.stack([segment, dp % 2, dp // 2]).astype(jnp.int32)
    own = (w_in[0], w_out[0])

    def my_half(value):
        return jnp.where(first, value[half:], value[:half])

    theta = math.pi / 2.0 * (my_half(timesteps).astype(jnp.float32) + 1.0) / (STEPS + 1.0)
    theta = jnp.repeat(theta, tokens)[:, None]
    alpha, sigma = jnp.cos(theta), jnp.sin(theta)

    flat = latents.reshape(count * tokens, width)
    lat_parts = gather_parts(flat)
    got_in = swapped(own_share(own[0]), "sec", 1)
    out_share, got_in, lat_parts[1], lat_parts[-1] = lax.optimization_barrier(
        (own_share(own[1]), got_in, lat_parts[1], lat_parts[-1])
    )
    got_out = lax.ppermute(out_share, "sec", [(1, 0)])

    onehot = (
        my_half(prompt_ids)[:, None] == jnp.arange(prompt_table.shape[0], dtype=jnp.int32)[None, :]
    ).astype(jnp.bfloat16)
    text_mine = dot_nn(onehot, prompt_table)

    near = [k for k in range(1, n_tp) if 2 * k != n_tp]
    rest = [0] + [k for k in range(1, n_tp) if 2 * k == n_tp]
    sums = [None] * n_tp
    hop = got_in
    for ks in (near, rest):
        if ks:
            operands, unused = lax.optimization_barrier(([lat_parts[k] for k in ks], hop))
            stay, leave = block0_partials(operands, gains[:1], *own, sel)
            crossed = lax.ppermute(leave, "sec", [(0, 1)])
            if ks is rest:
                crossed, got_out, sums = lax.optimization_barrier((crossed, got_out, sums))
            chosen = jnp.where(first, stay, crossed)
            for i, k in enumerate(ks):
                sums[k] = rotated(chosen[i], "tp", -k) if k else chosen[i]
            hop = crossed
    mine_rows = denoised(flat, sigma, alpha, sums, tokens, sel)

    other = (joined(got_in), joined(got_out))
    seen_parts = gather_parts(mine_rows)
    slopes1, pool = reward_forward(seen_parts, tokens, gains[1:], text_mine, own, other, sel)
    pools = gather_parts(pool)
    g_parts, g_mean = reward_back(pools, slopes1, tokens, own, other, sel)

    states = block0_state(lat_parts, gains[:1], own[0], other[0], sel)
    late_share, unused = lax.optimization_barrier((out_share, mine_rows))
    got_late = lax.ppermute(late_share, "sec", [(0, 1)])

    g_sums = [g_parts[0]] + [rotated(g_parts[k], "tp", -k) for k in range(1, n_tp)]
    g_sums, states, got_late = lax.optimization_barrier((g_sums, states, got_late))
    g_eps = eps_gradient(mine_rows, g_mean, gains[1:], -(sigma / alpha), g_sums, tokens, sel)

    g_mine = gather_parts(g_eps)
    pieces = list(g_mine)
    for ks in ([0], near, rest[1:]):
        if ks:
            pieces.append(swapped(jnp.concatenate([g_mine[k] for k in ks], 0), "sec", 1))
    out_parts, in_parts = gradients(pieces, states, own[1], joined(got_late), sel)
    grad_out, grad_in = sum_over_dp(*out_parts, sel), sum_over_dp(*in_parts, sel)
    return (grad_in, grad_out)


def solution(mesh):
    in_specs = (
        P(("dp", "tp"), None, None),
        P(("dp", "tp")),
        P(("dp", "tp")),
        P(),
        P(),
        P("sec", None, "tp"),
        P("sec", None, "tp"),
    )
    out_specs = (P(("sec", "dp"), "tp"), P(("sec", "dp"), "tp"))
    return jax.shard_map(
        on_device, mesh=mesh, in_specs=in_specs, out_specs=out_specs, check_vma=False
    )
```

```python
import functools
import math

import jax
import jax.numpy as jnp
from jax import lax
from jax.experimental import pallas as pl
from jax.experimental.pallas import tpu as pltpu
from jax.sharding import PartitionSpec as P

STEPS = 50


EPS = 1e-06
VMEM_BYTES = 8 * 1024 * 1024


def rotated(value, axis, steps):
    count = lax.axis_size(axis)
    return lax.ppermute(value, axis, [(i, (i + steps) % count) for i in range(count)])


def swapped(value, axis, bit):
    count = lax.axis_size(axis)
    return lax.ppermute(value, axis, [(i, i ^ bit) for i in range(count)])


def gather_parts(piece):
    return [piece] + [rotated(piece, "tp", k) for k in range(1, lax.axis_size("tp"))]


def gelu_pair(value):
    cdf = 0.5 * (1.0 + lax.erf(value * (1.0 / math.sqrt(2.0))))
    density = jnp.exp(-0.5 * value * value) * (1.0 / math.sqrt(2.0 * math.pi))
    return (value * cdf, cdf + value * density)


def normed(rows, gain):
    scale = lax.rsqrt(jnp.mean(rows * rows, axis=-1, keepdims=True) + EPS)
    return (rows * scale * gain).astype(jnp.bfloat16)


def dot_nn(a, b):
    return jnp.dot(a, b, preferred_element_type=jnp.float32)


def dot_nt(a, b):
    return lax.dot_general(a, b, (((1,), (1,)), ((), ())), preferred_element_type=jnp.float32)


def tile_of(hidden):
    for tile in (256, 128):
        if hidden % tile == 0:
            return tile
    return hidden


IN_VMEM = pl.BlockSpec(memory_space=pltpu.VMEM)
IN_SMEM = pl.BlockSpec(memory_space=pltpu.SMEM)


IN_ANY = pl.BlockSpec(memory_space=pl.ANY)


def run(body, name, sel, operands, outs, scratch, after=()):
    used = 1 + len(operands)

    def without_after(*refs):
        body(*refs[:used], *refs[used + len(after) :])

    return pl.pallas_call(
        without_after,
        in_specs=[IN_SMEM] + [IN_VMEM] * len(operands) + [IN_ANY] * len(after),
        out_specs=[IN_VMEM] * len(outs),
        scratch_shapes=scratch,
        out_shape=outs,
        compiler_params=pltpu.CompilerParams(vmem_limit_bytes=VMEM_BYTES),
        name=name,
    )(sel, *operands, *after)


def bf16(*shape):
    return jax.ShapeDtypeStruct(shape, jnp.bfloat16)


def tiles(hidden):
    tile = tile_of(hidden)
    return [slice(t, t + tile) for t in range(0, hidden, tile)]


def by_section(sel_ref, section, work, own, other):
    @pl.when(sel_ref[0] == section)
    def _():
        work(*own)

    @pl.when(sel_ref[0] != section)
    def _():
        work(*other)


def share_body(group, sel_ref, weight, out):
    rows = out.shape[0]
    start = pl.multiple_of((sel_ref[3] % group) * rows, rows)
    out[...] = weight[pl.ds(start, rows), :]


def share(weight, group, sel, after):
    rows, hidden = weight.shape
    body = functools.partial(share_body, group)
    return run(body, "share", sel, [weight], [bf16(rows // group, hidden)], [], after)[0]


def stack_body(sel_ref, *refs):
    for i, piece in enumerate(refs[:-1]):
        refs[-1][i] = piece[...]


def assemble_body(count, sel_ref, *refs):
    pieces, beside, out = refs[:count], refs[count], refs[count + 1]
    rows = pieces[0].shape[0]
    for i, piece in enumerate(pieces):
        for q, value in ((2 * i, piece[...]), (2 * i + 1, beside[i])):
            place = (sel_ref[3] % (2 * count)) ^ q
            out[pl.ds(pl.multiple_of(place * rows, rows), rows), :] = value


def assembled(pieces, sel, after):
    rows, hidden = pieces[0].shape
    count = len(pieces)
    stacked = run(stack_body, "stack", sel, pieces, [bf16(count, rows, hidden)], [], after)[0]
    beside = swapped(stacked, "dp", 1)
    body = functools.partial(assemble_body, count)
    out = bf16(2 * count * rows, hidden)
    return run(body, "assemble", sel, [*pieces, beside], [out], [])[0]


def partial_body(count, sel_ref, *refs):
    parts, (gain, w_in, w_out) = refs[:count], refs[count : count + 3]
    stay, leave, xn, acc = refs[count + 3 :]
    rows = parts[0].shape[0]
    late = rows // 2
    for i, part in enumerate(parts):
        xn[i * rows : (i + 1) * rows, :] = normed(part[...].astype(jnp.float32), gain[...])
    for t, tile in enumerate(tiles(w_in.shape[1])):
        act, unused = gelu_pair(dot_nn(xn[...], w_in[:, tile]))
        term = dot_nt(act.astype(jnp.bfloat16), w_out[:, tile])
        acc[...] = term if t == 0 else acc[...] + term
    for i in range(count):
        start = i * rows
        leave[i] = acc[start : start + late, :].astype(jnp.bfloat16)
        stay[i] = acc[start + late : start + rows, :].astype(jnp.bfloat16)


def block0_partials(parts, gain, w_in, w_out, sel, after):
    rows, width = parts[0].shape
    hidden, n = w_in.shape[1], len(parts)
    return run(
        functools.partial(partial_body, n),
        "block0_partial",
        sel,
        [*parts, gain, w_in, w_out],
        [bf16(n, rows // 2, width)] * 2,
        [
            pltpu.VMEM((n * rows, width), jnp.bfloat16),
            pltpu.VMEM((n * rows, width), jnp.float32),
        ],
        after,
    )


def pick_body(sel_ref, stay, crossed, *outs):
    for i, out in enumerate(outs):
        out[...] = jnp.where(sel_ref[0] == 0, stay[i], crossed[i])


def picked(stay, crossed, sel, after):
    count, rows, width = stay.shape
    outs = [bf16(rows, width)] * count
    return run(pick_body, "pick", sel, [stay, crossed], outs, [], after)


def denoise_body(tokens, count, sel_ref, *refs):
    latents, sigma, alpha = refs[:3]
    sums, out = refs[3 : 3 + count], refs[3 + count]
    late = out.shape[0]
    base = latents[pl.ds(pl.multiple_of((1 - sel_ref[0]) * late, late), late), :]
    base = base.astype(jnp.float32)
    eps = base
    for part in sums:
        eps = eps + part[...].astype(jnp.float32)
    out[...] = ((base - sigma[...] * eps) / alpha[...]).astype(jnp.bfloat16)


def denoised(latents, sigma, alpha, sums, tokens, sel):
    return run(
        functools.partial(denoise_body, tokens, len(sums)),
        "denoise",
        sel,
        [latents, sigma, alpha, *sums],
        [bf16(latents.shape[0] // 2, latents.shape[1])],
        [],
    )[0]


def crossing(count):
    near = [k for k in range(1, count) if 2 * k != count]
    return [0] + near + [k for k in range(1, count) if 2 * k == count]


def state_body(count, sel_ref, *refs):
    parts = refs[:count]
    gain, own, other, act, slope, xn_cols, xn = refs[count:]
    rows = parts[0].shape[0]
    late = rows // 2
    share = xn_cols.shape[0]
    mine = pl.multiple_of((1 - sel_ref[0]) * late, late)
    theirs = pl.multiple_of(sel_ref[0] * late, late)
    at = 0
    for start, order in ((mine, range(len(parts))), (theirs, crossing(len(parts)))):
        for k in order:
            rows_k = parts[k][pl.ds(start, late), :].astype(jnp.float32)
            xn[at : at + late, :] = normed(rows_k, gain[...])
            at += late
    cols = xn[:, pl.ds(pl.multiple_of(sel_ref[0] * share, share), share)]
    xn_cols[...] = cols.T

    def work(weight):
        for tile in tiles(weight.shape[1]):
            value, grad = gelu_pair(dot_nn(xn[...], weight[:, tile]))
            act[:, tile] = value.astype(jnp.bfloat16)
            slope[:, tile] = grad.astype(jnp.bfloat16)

    by_section(sel_ref, 0, work, (own,), (other,))


def block0_state(parts, gain, own, other, sel):
    total, width = sum(part.shape[0] for part in parts), parts[0].shape[1]
    hidden = own.shape[1]
    return run(
        functools.partial(state_body, len(parts)),
        "block0_state",
        sel,
        [*parts, gain, own, other],
        [bf16(total, hidden), bf16(total, hidden), bf16(width // 2, total)],
        [pltpu.VMEM((total, width), jnp.bfloat16)],
    )


def reward_body(count, tokens, sel_ref, *refs):
    parts, (gain, text) = refs[:count], refs[count : count + 2]
    own_in, own_out, other_in, other_out = refs[count + 2 : count + 6]
    slopes, (pool, xn) = refs[count + 6 : 2 * count + 6], refs[2 * count + 6 :]
    rows = parts[0].shape[0]
    half = rows // tokens
    row = lax.broadcasted_iota(jnp.int32, pool.shape, 0)
    start = jnp.zeros(pool.shape, jnp.float32)
    for image in range(half):
        own_rows = parts[0][image * tokens : (image + 1) * tokens, :].astype(jnp.float32)
        start = jnp.where(row == image, jnp.mean(own_rows, axis=0, keepdims=True), start)
        start = jnp.where(row == count * half + image, text[image : image + 1, :], start)
    pool[...] = start
    for i, part in enumerate(parts):
        xn[i * rows : (i + 1) * rows, :] = normed(part[...].astype(jnp.float32), gain[...])

    def work(w_in, w_out):
        for tile in tiles(w_in.shape[1]):
            act, grad = gelu_pair(dot_nn(xn[...], w_in[:, tile]))
            for i in range(count):
                slopes[i][:, tile] = grad[i * rows : (i + 1) * rows, :].astype(jnp.bfloat16)
            means = [
                jnp.mean(act[at : at + tokens, :], axis=0, keepdims=True)
                for at in range(0, count * rows, tokens)
            ]
            place = lax.broadcasted_iota(jnp.int32, (pool.shape[0], act.shape[1]), 0)
            stacked = jnp.zeros(place.shape, jnp.float32)
            for i, mean in enumerate(means):
                stacked = jnp.where(place == i, mean, stacked)
            pool[...] += dot_nt(stacked.astype(jnp.bfloat16), w_out[:, tile])

    by_section(sel_ref, 1, work, (own_in, own_out), (other_in, other_out))


def reward_forward(parts, tokens, gain, text, own, other, sel):
    rows, width = parts[0].shape
    hidden, n = own[0].shape[1], len(parts)
    images = (n + 1) * rows // tokens
    outs = run(
        functools.partial(reward_body, n, tokens),
        "reward_forward",
        sel,
        [*parts, gain, text, *own, *other],
        [bf16(rows, hidden)] * n
        + [jax.ShapeDtypeStruct((-(-images // 8) * 8, width), jnp.float32)],
        [pltpu.VMEM((n * rows, width), jnp.bfloat16)],
    )
    return outs[:n], outs[n]


def score_gradient(pooled, text):
    unit = text * lax.rsqrt(jnp.mean(text * text, axis=-1, keepdims=True) + EPS)
    scale = lax.rsqrt(jnp.mean(pooled * pooled, axis=-1, keepdims=True) + EPS)
    along = jnp.mean(pooled * unit, axis=-1, keepdims=True)
    return (-100.0 / pooled.shape[-1]) * (scale * unit - pooled * scale**3 * along)


def back_body(count, tokens, sel_ref, *refs):
    pools, slopes = refs[:count], refs[count : 2 * count]
    own_in, own_out, other_in, other_out = refs[2 * count : 2 * count + 4]
    outs = refs[2 * count + 4 : 3 * count + 4]
    g_mean, acc = refs[3 * count + 4 :]
    rows = slopes[0].shape[0]
    half = rows // tokens
    images = count * half
    pooled, texts = [], []
    for j in range(images):
        at = [(j - k * half) % images for k in range(count)]
        pooled.append(sum(pools[k][at[k] : at[k] + 1, :] for k in range(count)))
        text = images + j % half
        texts.append(pools[j // half][text : text + 1, :])
    padded = -(-images // 16) * 16
    row = lax.broadcasted_iota(jnp.int32, (padded, acc.shape[1]), 0)
    stacked, spoken = jnp.zeros(row.shape, jnp.float32), jnp.zeros(row.shape, jnp.float32)
    for j in range(images):
        stacked = jnp.where(row == j, pooled[j], stacked)
        spoken = jnp.where(row == j, texts[j], spoken)
    g_all = score_gradient(stacked, spoken) * (1.0 / tokens)
    g_mean[...] = g_all[: g_mean.shape[0], :]
    g_tok = g_all.astype(jnp.bfloat16)

    def work(w_in, w_out):
        for t, tile in enumerate(tiles(w_in.shape[1])):
            g_h = dot_nn(g_tok, w_out[:, tile])
            terms = []
            for i in range(count):
                for image in range(half):
                    at = i * half + image
                    slope = slopes[i][image * tokens : (image + 1) * tokens, tile]
                    terms.append(
                        (slope.astype(jnp.float32) * g_h[at : at + 1, :]).astype(jnp.bfloat16)
                    )
            term = dot_nt(jnp.concatenate(terms, axis=0), w_in[:, tile])
            acc[...] = term if t == 0 else acc[...] + term

    by_section(sel_ref, 1, work, (own_in, own_out), (other_in, other_out))
    for i, out in enumerate(outs):
        out[...] = acc[i * rows : (i + 1) * rows, :].astype(jnp.bfloat16)


def reward_back(pools, slopes, tokens, own, other, sel):
    rows, hidden = slopes[0].shape
    width, n = own[0].shape[0], len(slopes)
    outs = run(
        functools.partial(back_body, n, tokens),
        "reward_back",
        sel,
        [*pools, *slopes, *own, *other],
        [bf16(rows, width)] * n + [jax.ShapeDtypeStruct((8, width), jnp.float32)],
        [pltpu.VMEM((n * rows, width), jnp.float32)],
    )
    return outs[:n], outs[n]


def eps_gradient_body(tokens, count, sel_ref, *refs):
    seen_ref, g_mean, gain, ratio = refs[:4]
    sums, out = refs[4 : 4 + count], refs[4 + count]
    g_xn = sums[0][...].astype(jnp.float32)
    for part in sums[1:]:
        g_xn = g_xn + part[...].astype(jnp.float32)
    seen = seen_ref[...].astype(jnp.float32)
    scale = lax.rsqrt(jnp.mean(seen * seen, axis=-1, keepdims=True) + EPS)
    weighted = gain[...] * g_xn
    along = jnp.mean(seen * weighted, axis=-1, keepdims=True)
    g_norm = scale * weighted - seen * scale**3 * along
    for image in range(out.shape[0] // tokens):
        at = slice(image * tokens, (image + 1) * tokens)
        g_images = (g_mean[image : image + 1, :] + g_norm[at, :]).astype(jnp.bfloat16)
        out[at, :] = (ratio[at, :] * g_images.astype(jnp.float32)).astype(jnp.bfloat16)


def eps_gradient(seen, g_mean, gain, ratio, sums, tokens, sel, after):
    return run(
        functools.partial(eps_gradient_body, tokens, len(sums)),
        "eps_gradient",
        sel,
        [seen, g_mean, gain, ratio, *sums],
        [bf16(*seen.shape)],
        [],
        after,
    )[0]


def put_rows(result, core, keep, away, tile):
    groups, rows, unused = keep.shape
    for g in range(groups):
        even = result[2 * g * rows : (2 * g + 1) * rows, :]
        odd = result[(2 * g + 1) * rows : (2 * g + 2) * rows, :]
        keep[g, :, tile] = jnp.where(core == 0, even, odd).astype(jnp.bfloat16)
        away[g, :, tile] = jnp.where(core == 0, odd, even).astype(jnp.bfloat16)


def gradient_body(count, sel_ref, *refs):
    pieces = refs[:count]
    act, slope, xn_cols, own, other = refs[count : count + 5]
    out_keep, out_away, in_keep, in_away, g_all, turned = refs[count + 5 :]
    share = turned.shape[0]
    core = sel_ref[1]
    at = 0
    for piece in pieces:
        g_all[at : at + piece.shape[0], :] = piece[...]
        at += piece.shape[0]
    cols = g_all[:, pl.ds(pl.multiple_of(sel_ref[0] * share, share), share)]
    turned[...] = cols.T

    def work(weight):
        for tile in tiles(weight.shape[1]):
            put_rows(dot_nn(turned[...], act[:, tile]), core, out_keep, out_away, tile)
            g_h = dot_nn(g_all[...], weight[:, tile])
            g_hidden = (g_h * slope[:, tile].astype(jnp.float32)).astype(jnp.bfloat16)
            put_rows(dot_nn(xn_cols[...], g_hidden), core, in_keep, in_away, tile)

    by_section(sel_ref, 0, work, (own,), (other,))


def gradients(pieces, states, own, other, sel):
    total, width = sum(piece.shape[0] for piece in pieces), pieces[0].shape[1]
    hidden = own.shape[1]
    groups = lax.axis_size("dp") // 2
    outs = run(
        functools.partial(gradient_body, len(pieces)),
        "gradients",
        sel,
        [*pieces, *states, own, other],
        [bf16(groups, width // 2 // (2 * groups), hidden)] * 4,
        [
            pltpu.VMEM((total, width), jnp.bfloat16),
            pltpu.VMEM((width // 2, total), jnp.bfloat16),
        ],
    )
    return outs[:2], outs[2:]


def chip_body(sel_ref, keep, arrived, mine, others):
    groups = keep.shape[0]
    for k in range(groups):
        at = (sel_ref[2] + k) % groups
        total = keep[at].astype(jnp.float32) + arrived[at].astype(jnp.float32)
        if k == 0:
            mine[...] = total
        else:
            others[k - 1] = total.astype(jnp.bfloat16)


def sum_over_dp(keep, away, sel):
    groups, rows, hidden = keep.shape
    total, others = run(
        chip_body,
        "chip_sum",
        sel,
        [keep, swapped(away, "dp", 1)],
        [jax.ShapeDtypeStruct((rows, hidden), jnp.float32), bf16(groups - 1, rows, hidden)],
        [],
    )
    for k in range(1, groups):
        total = total + rotated(others[k - 1], "dp", 2 * k).astype(jnp.float32)
    return total


def on_device(latents, timesteps, prompt_ids, prompt_table, gains, w_in, w_out):
    count, tokens, width = latents.shape
    half = count // 2
    n_tp = lax.axis_size("tp")
    segment = lax.axis_index("sec")
    first = segment == 0
    dp = lax.axis_index("dp")
    sel = jnp.stack([segment, dp % 2, dp // 2, dp % 4]).astype(jnp.int32)
    own = (w_in[0], w_out[0])

    def my_half(value):
        return jnp.where(first, value[half:], value[:half])

    theta = math.pi / 2.0 * (my_half(timesteps).astype(jnp.float32) + 1.0) / (STEPS + 1.0)
    theta = jnp.repeat(theta, tokens)[:, None]
    alpha, sigma = jnp.cos(theta), jnp.sin(theta)

    flat = latents.reshape(count * tokens, width)
    lat_parts = gather_parts(flat)
    got_in = swapped(share(own[0], 4, sel, ()), "sec", 1)
    across_in = swapped(got_in, "dp", 2)
    out_share = share(own[1], 2, sel, (lat_parts[1], lat_parts[-1]))
    got_out = lax.ppermute(out_share, "sec", [(1, 0)])

    onehot = (
        my_half(prompt_ids)[:, None] == jnp.arange(prompt_table.shape[0], dtype=jnp.int32)[None, :]
    ).astype(jnp.bfloat16)
    text_mine = dot_nn(onehot, prompt_table)

    near = [k for k in range(1, n_tp) if 2 * k != n_tp]
    rest = [0] + [k for k in range(1, n_tp) if 2 * k == n_tp]
    sums = [None] * n_tp
    before_kernel, before_pick = [got_in], []
    for ks in (near, rest):
        if ks:
            stay, leave = block0_partials(
                [lat_parts[k] for k in ks], gains[:1], *own, sel, before_kernel
            )
            crossed = lax.ppermute(leave, "sec", [(0, 1)])
            chosen = picked(stay, crossed, sel, before_pick)
            for k, part in zip(ks, chosen):
                sums[k] = rotated(part, "tp", -k) if k else part
            before_kernel, before_pick = [crossed], [sums[k] for k in ks]
    mine_rows = denoised(flat, sigma, alpha, sums, tokens, sel)

    seen_parts = gather_parts(mine_rows)
    other = (
        assembled([got_in, across_in], sel, [sums[0]]),
        assembled([got_out], sel, [sums[0]]),
    )
    slopes1, pool = reward_forward(seen_parts, tokens, gains[1:], text_mine, own, other, sel)
    pools = gather_parts(pool)
    g_parts, g_mean = reward_back(pools, slopes1, tokens, own, other, sel)

    states = block0_state(lat_parts, gains[:1], own[0], other[0], sel)
    got_late = lax.ppermute(share(own[1], 2, sel, [pool]), "sec", [(0, 1)])

    g_sums = [g_parts[0]] + [rotated(g_parts[k], "tp", -k) for k in range(1, n_tp)]
    ratio = -(sigma / alpha)
    g_eps = eps_gradient(
        mine_rows, g_mean, gains[1:], ratio, g_sums, tokens, sel, [states[0]]
    )

    g_mine = gather_parts(g_eps)
    pieces = list(g_mine)
    for ks in ([0], near, rest[1:]):
        if ks:
            pieces.append(swapped(jnp.concatenate([g_mine[k] for k in ks], 0), "sec", 1))
    late_out = assembled([got_late], sel, [g_mine[1], g_mine[-1]])
    out_parts, in_parts = gradients(pieces, states, own[1], late_out, sel)
    grad_out, grad_in = sum_over_dp(*out_parts, sel), sum_over_dp(*in_parts, sel)
    return (grad_in, grad_out)


def solution(mesh):
    in_specs = (
        P(("dp", "tp"), None, None),
        P(("dp", "tp")),
        P(("dp", "tp")),
        P(),
        P(),
        P("sec", None, "tp"),
        P("sec", None, "tp"),
    )
    out_specs = (P(("sec", "dp"), "tp"), P(("sec", "dp"), "tp"))
    return jax.shard_map(
        on_device, mesh=mesh, in_specs=in_specs, out_specs=out_specs, check_vma=False
    )
```

```python
import functools
import math

import jax
import jax.numpy as jnp
from jax import lax
from jax.experimental import pallas as pl
from jax.experimental.pallas import tpu as pltpu
from jax.sharding import PartitionSpec as P

STEPS = 50


EPS = 1e-06
VMEM_BYTES = 8 * 1024 * 1024
COST = 10**11


def rotated(value, axis, steps):
    count = lax.axis_size(axis)
    return lax.ppermute(value, axis, [(i, (i + steps) % count) for i in range(count)])


def swapped(value, axis, bit):
    count = lax.axis_size(axis)
    return lax.ppermute(value, axis, [(i, i ^ bit) for i in range(count)])


def gather_parts(piece):
    return [piece] + [rotated(piece, "tp", k) for k in range(1, lax.axis_size("tp"))]


def gelu_pair(value):
    cdf = 0.5 * (1.0 + lax.erf(value * (1.0 / math.sqrt(2.0))))
    density = jnp.exp(-0.5 * value * value) * (1.0 / math.sqrt(2.0 * math.pi))
    return (value * cdf, cdf + value * density)


def normed(rows, gain):
    scale = lax.rsqrt(jnp.mean(rows * rows, axis=-1, keepdims=True) + EPS)
    return (rows * scale * gain).astype(jnp.bfloat16)


def dot_nn(a, b):
    return jnp.dot(a, b, preferred_element_type=jnp.float32)


def dot_nt(a, b):
    return lax.dot_general(a, b, (((1,), (1,)), ((), ())), preferred_element_type=jnp.float32)


def tile_of(hidden):
    for tile in (256, 128):
        if hidden % tile == 0:
            return tile
    return hidden


IN_VMEM = pl.BlockSpec(memory_space=pltpu.VMEM)
IN_SMEM = pl.BlockSpec(memory_space=pltpu.SMEM)


TOKEN = jax.ShapeDtypeStruct((8, 128), jnp.float32)


def run(body, name, sel, operands, outs, scratch, after=()):
    used, last = 1 + len(operands), 1 + len(operands) + len(after) + len(outs)

    def with_token(*refs):
        refs[last][...] = jnp.zeros(TOKEN.shape, TOKEN.dtype)
        body(*refs[:used], *refs[used + len(after) : last], *refs[last + 1 :])

    held = [math.prod(x.shape) * jnp.dtype(x.dtype).itemsize for x in scratch]
    return pl.pallas_call(
        with_token,
        in_specs=[IN_SMEM] + [IN_VMEM] * (len(operands) + len(after)),
        out_specs=[IN_VMEM] * (len(outs) + 1),
        scratch_shapes=scratch,
        out_shape=[*outs, TOKEN],
        compiler_params=pltpu.CompilerParams(vmem_limit_bytes=max(VMEM_BYTES, 4 * sum(held))),
        cost_estimate=pl.CostEstimate(
            flops=COST, bytes_accessed=COST // 200, transcendentals=0
        ),
        name=name,
    )(sel, *operands, *after)


def bf16(*shape):
    return jax.ShapeDtypeStruct(shape, jnp.bfloat16)


def tiles(hidden):
    tile = tile_of(hidden)
    return [slice(t, t + tile) for t in range(0, hidden, tile)]


def by_section(sel_ref, section, work, own, other):
    @pl.when(sel_ref[0] == section)
    def _():
        work(*own)

    @pl.when(sel_ref[0] != section)
    def _():
        work(*other)


def share_body(group, sel_ref, weight, out):
    rows = out.shape[0]
    start = pl.multiple_of((sel_ref[3] % group) * rows, rows)
    out[...] = weight[pl.ds(start, rows), :]


def share(weight, group, sel, after):
    rows, hidden = weight.shape
    body = functools.partial(share_body, group)
    return run(body, "share", sel, [weight], [bf16(rows // group, hidden)], [], after)


def stack_body(sel_ref, *refs):
    for i, piece in enumerate(refs[:-1]):
        refs[-1][i] = piece[...]


def assemble_body(count, sel_ref, *refs):
    pieces, beside, out = refs[:count], refs[count], refs[count + 1]
    rows = pieces[0].shape[0]
    for i, piece in enumerate(pieces):
        for q, value in ((2 * i, piece[...]), (2 * i + 1, beside[i])):
            place = (sel_ref[3] % (2 * count)) ^ q
            out[pl.ds(pl.multiple_of(place * rows, rows), rows), :] = value


def assembled(pieces, sel, after):
    rows, hidden = pieces[0].shape
    count = len(pieces)
    out = bf16(count, rows, hidden)
    stacked = run(stack_body, "stack", sel, pieces, [out], [], after)[0]
    beside = swapped(stacked, "dp", 1)
    body = functools.partial(assemble_body, count)
    out = bf16(2 * count * rows, hidden)
    return run(body, "assemble", sel, [*pieces, beside], [out], [])


def partial_body(count, sel_ref, *refs):
    parts, (gain, w_in, w_out) = refs[:count], refs[count : count + 3]
    stay, leave, xn, acc = refs[count + 3 :]
    rows = parts[0].shape[0]
    late = rows // 2
    for i, part in enumerate(parts):
        xn[i * rows : (i + 1) * rows, :] = normed(part[...].astype(jnp.float32), gain[...])
    for t, tile in enumerate(tiles(w_in.shape[1])):
        act, unused = gelu_pair(dot_nn(xn[...], w_in[:, tile]))
        term = dot_nt(act.astype(jnp.bfloat16), w_out[:, tile])
        acc[...] = term if t == 0 else acc[...] + term
    for i in range(count):
        start = i * rows
        leave[i] = acc[start : start + late, :].astype(jnp.bfloat16)
        stay[i] = acc[start + late : start + rows, :].astype(jnp.bfloat16)


def block0_partials(parts, gain, w_in, w_out, sel, after):
    rows, width = parts[0].shape
    hidden, n = w_in.shape[1], len(parts)
    return run(
        functools.partial(partial_body, n),
        "block0_partial",
        sel,
        [*parts, gain, w_in, w_out],
        [bf16(n, rows // 2, width)] * 2,
        [
            pltpu.VMEM((n * rows, width), jnp.bfloat16),
            pltpu.VMEM((n * rows, width), jnp.float32),
        ],
        after,
    )


def pick_body(count, sel_ref, *refs):
    stay, crossed = refs[:2]
    arrived, outs = refs[2 : 2 + count], refs[2 + count :]
    for i, out in enumerate(outs):
        value = jnp.where(sel_ref[0] == 0, stay[i], crossed[i])
        if count and i == 0:
            value = value.astype(jnp.float32)
            for part in arrived:
                value = value + part[...].astype(jnp.float32)
        out[...] = value


def picked(stay, crossed, arrived, sel):
    count, rows, width = stay.shape
    outs = [bf16(rows, width)] * count
    if arrived:
        outs[0] = jax.ShapeDtypeStruct((rows, width), jnp.float32)
    body = functools.partial(pick_body, len(arrived))
    *chosen, token = run(body, "pick", sel, [stay, crossed, *arrived], outs, [])
    return chosen, token


def denoise_body(tokens, count, sel_ref, *refs):
    latents, sigma, alpha = refs[:3]
    sums, out = refs[3 : 3 + count], refs[3 + count]
    late = out.shape[0]
    base = latents[pl.ds(pl.multiple_of((1 - sel_ref[0]) * late, late), late), :]
    base = base.astype(jnp.float32)
    eps = base
    for part in sums:
        eps = eps + part[...].astype(jnp.float32)
    out[...] = ((base - sigma[...] * eps) / alpha[...]).astype(jnp.bfloat16)


def denoised(latents, sigma, alpha, sums, tokens, sel, after):
    return run(
        functools.partial(denoise_body, tokens, len(sums)),
        "denoise",
        sel,
        [latents, sigma, alpha, *sums],
        [bf16(latents.shape[0] // 2, latents.shape[1])],
        [],
        after,
    )[:2]


def crossing(count):
    near = [k for k in range(1, count) if 2 * k != count]
    return [0] + near + [k for k in range(1, count) if 2 * k == count]


def state_body(count, sel_ref, *refs):
    parts = refs[:count]
    gain, own, other, act, slope, xn_cols, xn = refs[count:]
    rows = parts[0].shape[0]
    late = rows // 2
    share = xn_cols.shape[0]
    mine = pl.multiple_of((1 - sel_ref[0]) * late, late)
    theirs = pl.multiple_of(sel_ref[0] * late, late)
    at = 0
    for start, order in ((mine, range(len(parts))), (theirs, crossing(len(parts)))):
        for k in order:
            rows_k = parts[k][pl.ds(start, late), :].astype(jnp.float32)
            xn[at : at + late, :] = normed(rows_k, gain[...])
            at += late
    cols = xn[:, pl.ds(pl.multiple_of(sel_ref[0] * share, share), share)]
    xn_cols[...] = cols.T

    def work(weight):
        for tile in tiles(weight.shape[1]):
            value, grad = gelu_pair(dot_nn(xn[...], weight[:, tile]))
            act[:, tile] = value.astype(jnp.bfloat16)
            slope[:, tile] = grad.astype(jnp.bfloat16)

    by_section(sel_ref, 0, work, (own,), (other,))


def block0_state(parts, gain, own, other, sel, after):
    total, width = sum(part.shape[0] for part in parts), parts[0].shape[1]
    hidden = own.shape[1]
    return run(
        functools.partial(state_body, len(parts)),
        "block0_state",
        sel,
        [*parts, gain, own, other],
        [bf16(total, hidden), bf16(total, hidden), bf16(width // 2, total)],
        [pltpu.VMEM((total, width), jnp.bfloat16)],
        after,
    )


def reward_body(count, tokens, sel_ref, *refs):
    parts, (gain, text) = refs[:count], refs[count : count + 2]
    own_in, own_out, other_in, other_out = refs[count + 2 : count + 6]
    slopes, (pool, xn) = refs[count + 6 : 2 * count + 6], refs[2 * count + 6 :]
    rows = parts[0].shape[0]
    half = rows // tokens
    row = lax.broadcasted_iota(jnp.int32, pool.shape, 0)
    start = jnp.zeros(pool.shape, jnp.float32)
    for image in range(half):
        own_rows = parts[0][image * tokens : (image + 1) * tokens, :].astype(jnp.float32)
        start = jnp.where(row == image, jnp.mean(own_rows, axis=0, keepdims=True), start)
        start = jnp.where(row == count * half + image, text[image : image + 1, :], start)
    pool[...] = start
    for i, part in enumerate(parts):
        xn[i * rows : (i + 1) * rows, :] = normed(part[...].astype(jnp.float32), gain[...])

    def work(w_in, w_out):
        for tile in tiles(w_in.shape[1]):
            act, grad = gelu_pair(dot_nn(xn[...], w_in[:, tile]))
            for i in range(count):
                slopes[i][:, tile] = grad[i * rows : (i + 1) * rows, :].astype(jnp.bfloat16)
            means = [
                jnp.mean(act[at : at + tokens, :], axis=0, keepdims=True)
                for at in range(0, count * rows, tokens)
            ]
            place = lax.broadcasted_iota(jnp.int32, (pool.shape[0], act.shape[1]), 0)
            stacked = jnp.zeros(place.shape, jnp.float32)
            for i, mean in enumerate(means):
                stacked = jnp.where(place == i, mean, stacked)
            pool[...] += dot_nt(stacked.astype(jnp.bfloat16), w_out[:, tile])

    by_section(sel_ref, 1, work, (own_in, own_out), (other_in, other_out))


def reward_forward(parts, tokens, gain, text, own, other, sel, after):
    rows, width = parts[0].shape
    hidden, n = own[0].shape[1], len(parts)
    images = (n + 1) * rows // tokens
    outs = run(
        functools.partial(reward_body, n, tokens),
        "reward_forward",
        sel,
        [*parts, gain, text, *own, *other],
        [bf16(rows, hidden)] * n
        + [jax.ShapeDtypeStruct((-(-images // 8) * 8, width), jnp.float32)],
        [pltpu.VMEM((n * rows, width), jnp.bfloat16)],
        after,
    )
    return outs[:n], outs[n]


def score_gradient(pooled, text):
    unit = text * lax.rsqrt(jnp.mean(text * text, axis=-1, keepdims=True) + EPS)
    scale = lax.rsqrt(jnp.mean(pooled * pooled, axis=-1, keepdims=True) + EPS)
    along = jnp.mean(pooled * unit, axis=-1, keepdims=True)
    return (-100.0 / pooled.shape[-1]) * (scale * unit - pooled * scale**3 * along)


def back_body(count, tokens, sel_ref, *refs):
    pools, slopes = refs[:count], refs[count : 2 * count]
    own_in, own_out, other_in, other_out = refs[2 * count : 2 * count + 4]
    outs = refs[2 * count + 4 : 3 * count + 4]
    g_mean, acc = refs[3 * count + 4 :]
    rows = slopes[0].shape[0]
    half = rows // tokens
    images = count * half
    pooled, texts = [], []
    for j in range(images):
        at = [(j - k * half) % images for k in range(count)]
        pooled.append(sum(pools[k][at[k] : at[k] + 1, :] for k in range(count)))
        text = images + j % half
        texts.append(pools[j // half][text : text + 1, :])
    padded = -(-images // 16) * 16
    row = lax.broadcasted_iota(jnp.int32, (padded, acc.shape[1]), 0)
    stacked, spoken = jnp.zeros(row.shape, jnp.float32), jnp.zeros(row.shape, jnp.float32)
    for j in range(images):
        stacked = jnp.where(row == j, pooled[j], stacked)
        spoken = jnp.where(row == j, texts[j], spoken)
    g_all = score_gradient(stacked, spoken) * (1.0 / tokens)
    g_mean[...] = g_all[: g_mean.shape[0], :]
    g_tok = g_all.astype(jnp.bfloat16)

    def work(w_in, w_out):
        for t, tile in enumerate(tiles(w_in.shape[1])):
            g_h = dot_nn(g_tok, w_out[:, tile])
            terms = []
            for i in range(count):
                for image in range(half):
                    at = i * half + image
                    slope = slopes[i][image * tokens : (image + 1) * tokens, tile]
                    terms.append(
                        (slope.astype(jnp.float32) * g_h[at : at + 1, :]).astype(jnp.bfloat16)
                    )
            term = dot_nt(jnp.concatenate(terms, axis=0), w_in[:, tile])
            acc[...] = term if t == 0 else acc[...] + term

    by_section(sel_ref, 1, work, (own_in, own_out), (other_in, other_out))
    for i, out in enumerate(outs):
        out[...] = acc[i * rows : (i + 1) * rows, :].astype(jnp.bfloat16)


def reward_back(pools, slopes, tokens, own, other, sel):
    rows, hidden = slopes[0].shape
    width, n = own[0].shape[0], len(slopes)
    outs = run(
        functools.partial(back_body, n, tokens),
        "reward_back",
        sel,
        [*pools, *slopes, *own, *other],
        [bf16(rows, width)] * n + [jax.ShapeDtypeStruct((8, width), jnp.float32)],
        [pltpu.VMEM((n * rows, width), jnp.float32)],
    )
    return outs[:n], outs[n]


def eps_gradient_body(tokens, count, sel_ref, *refs):
    seen_ref, g_mean, gain, ratio = refs[:4]
    sums, out = refs[4 : 4 + count], refs[4 + count]
    g_xn = sums[0][...].astype(jnp.float32)
    for part in sums[1:]:
        g_xn = g_xn + part[...].astype(jnp.float32)
    seen = seen_ref[...].astype(jnp.float32)
    scale = lax.rsqrt(jnp.mean(seen * seen, axis=-1, keepdims=True) + EPS)
    weighted = gain[...] * g_xn
    along = jnp.mean(seen * weighted, axis=-1, keepdims=True)
    g_norm = scale * weighted - seen * scale**3 * along
    for image in range(out.shape[0] // tokens):
        at = slice(image * tokens, (image + 1) * tokens)
        g_images = (g_mean[image : image + 1, :] + g_norm[at, :]).astype(jnp.bfloat16)
        out[at, :] = (ratio[at, :] * g_images.astype(jnp.float32)).astype(jnp.bfloat16)


def eps_gradient(seen, g_mean, gain, ratio, sums, tokens, sel, after):
    return run(
        functools.partial(eps_gradient_body, tokens, len(sums)),
        "eps_gradient",
        sel,
        [seen, g_mean, gain, ratio, *sums],
        [bf16(*seen.shape)],
        [],
        after,
    )


def put_rows(result, core, keep, away, tile):
    groups, rows, unused = keep.shape
    for g in range(groups):
        even = result[2 * g * rows : (2 * g + 1) * rows, :]
        odd = result[(2 * g + 1) * rows : (2 * g + 2) * rows, :]
        keep[g, :, tile] = jnp.where(core == 0, even, odd).astype(jnp.bfloat16)
        away[g, :, tile] = jnp.where(core == 0, odd, even).astype(jnp.bfloat16)


def gradient_body(count, sel_ref, *refs):
    pieces = refs[:count]
    act, slope, xn_cols, own, other = refs[count : count + 5]
    out_keep, out_away, in_keep, in_away, g_all, turned = refs[count + 5 :]
    share = turned.shape[0]
    core = sel_ref[1]
    at = 0
    for piece in pieces:
        g_all[at : at + piece.shape[0], :] = piece[...]
        at += piece.shape[0]
    cols = g_all[:, pl.ds(pl.multiple_of(sel_ref[0] * share, share), share)]
    turned[...] = cols.T

    def work(weight):
        for tile in tiles(weight.shape[1]):
            put_rows(dot_nn(turned[...], act[:, tile]), core, out_keep, out_away, tile)
            g_h = dot_nn(g_all[...], weight[:, tile])
            g_hidden = (g_h * slope[:, tile].astype(jnp.float32)).astype(jnp.bfloat16)
            put_rows(dot_nn(xn_cols[...], g_hidden), core, in_keep, in_away, tile)

    by_section(sel_ref, 0, work, (own,), (other,))


def gradients(pieces, states, own, other, sel):
    total, width = sum(piece.shape[0] for piece in pieces), pieces[0].shape[1]
    hidden = own.shape[1]
    groups = lax.axis_size("dp") // 2
    outs = run(
        functools.partial(gradient_body, len(pieces)),
        "gradients",
        sel,
        [*pieces, *states, own, other],
        [bf16(groups, width // 2 // (2 * groups), hidden)] * 4,
        [
            pltpu.VMEM((total, width), jnp.bfloat16),
            pltpu.VMEM((width // 2, total), jnp.bfloat16),
        ],
    )
    return outs[:2], outs[2:4]


def chip_body(sel_ref, keep, arrived, mine, others):
    groups = keep.shape[0]
    for k in range(groups):
        at = (sel_ref[2] + k) % groups
        total = keep[at].astype(jnp.float32) + arrived[at].astype(jnp.float32)
        if k == 0:
            mine[...] = total
        else:
            others[k - 1] = total.astype(jnp.bfloat16)


def sum_over_dp(keep, away, sel):
    groups, rows, hidden = keep.shape
    total, others, unused = run(
        chip_body,
        "chip_sum",
        sel,
        [keep, swapped(away, "dp", 1)],
        [jax.ShapeDtypeStruct((rows, hidden), jnp.float32), bf16(groups - 1, rows, hidden)],
        [],
    )
    for k in range(1, groups):
        total = total + rotated(others[k - 1], "dp", 2 * k).astype(jnp.float32)
    return total


def on_device(latents, timesteps, prompt_ids, prompt_table, gains, w_in, w_out):
    count, tokens, width = latents.shape
    half = count // 2
    n_tp = lax.axis_size("tp")
    segment = lax.axis_index("sec")
    first = segment == 0
    dp = lax.axis_index("dp")
    sel = jnp.stack([segment, dp % 2, dp // 2, dp % 4]).astype(jnp.int32)
    own = (w_in[0], w_out[0])

    def my_half(value):
        return jnp.where(first, value[half:], value[:half])

    theta = math.pi / 2.0 * (my_half(timesteps).astype(jnp.float32) + 1.0) / (STEPS + 1.0)
    theta = jnp.repeat(theta, tokens)[:, None]
    alpha, sigma = jnp.cos(theta), jnp.sin(theta)

    flat = latents.reshape(count * tokens, width)
    lat_parts = gather_parts(flat)
    got_in = swapped(share(own[0], 4, sel, ())[0], "sec", 1)
    across_in = swapped(got_in, "dp", 2)
    out_share, out_token = share(own[1], 2, sel, [lat_parts[1], lat_parts[-1]])
    got_out = lax.ppermute(out_share, "sec", [(1, 0)])

    onehot = (
        my_half(prompt_ids)[:, None] == jnp.arange(prompt_table.shape[0], dtype=jnp.int32)[None, :]
    ).astype(jnp.bfloat16)
    text_mine = dot_nn(onehot, prompt_table)

    near = [k for k in range(1, n_tp) if 2 * k != n_tp]
    rest = [0] + [k for k in range(1, n_tp) if 2 * k == n_tp]
    sums, before = [], [got_in]
    for ks in (near, rest):
        if ks:
            stay, leave, partial_token = block0_partials(
                [lat_parts[k] for k in ks], gains[:1], *own, sel, before
            )
            crossed = lax.ppermute(leave, "sec", [(0, 1)])
            chosen, picked_token = picked(stay, crossed, sums if ks is rest else [], sel)
            if ks is rest:
                sums = [chosen[0]] + [rotated(part, "tp", -k) for k, part in zip(ks[1:], chosen[1:])]
            else:
                sums = [rotated(part, "tp", -k) for k, part in zip(ks, chosen)]
                before = [picked_token, out_token]
    other_in, in_token = assembled([got_in, across_in], sel, [partial_token])
    mine_rows, unused = denoised(flat, sigma, alpha, sums, tokens, sel, [in_token])

    seen_parts = gather_parts(mine_rows)
    near_seen = [seen_parts[k] for k in near]
    other_out, out_token = assembled([got_out], sel, near_seen)
    other = (other_in, other_out)
    late_share, late_token = share(own[1], 2, sel, [out_token])
    got_late = lax.ppermute(late_share, "sec", [(0, 1)])
    slopes1, pool = reward_forward(
        seen_parts, tokens, gains[1:], text_mine, own, other, sel, ()
    )
    pools = gather_parts(pool)
    g_parts, g_mean = reward_back(pools, slopes1, tokens, own, other, sel)

    *states, state_token = block0_state(
        lat_parts, gains[:1], own[0], other[0], sel, ()
    )

    g_sums = [g_parts[0]] + [rotated(g_parts[k], "tp", -k) for k in range(1, n_tp)]
    ratio = -(sigma / alpha)
    g_eps, eps_token = eps_gradient(
        mine_rows, g_mean, gains[1:], ratio, g_sums, tokens, sel, [state_token]
    )

    late_out = assembled([got_late], sel, [state_token])[0]

    g_mine = gather_parts(g_eps)
    pieces = list(g_mine)
    for ks in ([0], near, rest[1:]):
        if ks:
            pieces.append(swapped(jnp.concatenate([g_mine[k] for k in ks], 0), "sec", 1))
    out_parts, in_parts = gradients(pieces, states, own[1], late_out, sel)
    grad_out, grad_in = sum_over_dp(*out_parts, sel), sum_over_dp(*in_parts, sel)
    return (grad_in, grad_out)


def solution(mesh):
    in_specs = (
        P(("dp", "tp"), None, None),
        P(("dp", "tp")),
        P(("dp", "tp")),
        P(),
        P(),
        P("sec", None, "tp"),
        P("sec", None, "tp"),
    )
    out_specs = (P(("sec", "dp"), "tp"), P(("sec", "dp"), "tp"))
    return jax.shard_map(
        on_device, mesh=mesh, in_specs=in_specs, out_specs=out_specs, check_vma=False
    )
```

```python
import functools
import math

import jax
import jax.numpy as jnp
from jax import lax
from jax.experimental import pallas as pl
from jax.experimental.pallas import tpu as pltpu
from jax.sharding import PartitionSpec as P

STEPS = 50


EPS = 1e-06
VMEM_BYTES = 8 * 1024 * 1024
COST = 10**11


def rotated(value, axis, steps):
    count = lax.axis_size(axis)
    return lax.ppermute(value, axis, [(i, (i + steps) % count) for i in range(count)])


def swapped(value, axis, bit):
    count = lax.axis_size(axis)
    return lax.ppermute(value, axis, [(i, i ^ bit) for i in range(count)])


def gather_parts(piece):
    return [piece] + [rotated(piece, "tp", k) for k in range(1, lax.axis_size("tp"))]


def near_and_far(count):
    near = [k for k in range(1, count) if 2 * k != count]
    return near, [k for k in range(1, count) if 2 * k == count]


def gather_in_turn(piece, sel):
    near, far = near_and_far(lax.axis_size("tp"))
    parts = [piece] + [None] * (len(near) + len(far))
    for k in near:
        parts[k] = rotated(piece, "tp", k)
    again, token = relayed(piece, sel, [parts[k] for k in near])
    for k in far:
        parts[k] = rotated(again, "tp", k)
    return parts, token


def gelu_pair(value):
    cdf = 0.5 * (1.0 + lax.erf(value * (1.0 / math.sqrt(2.0))))
    density = jnp.exp(-0.5 * value * value) * (1.0 / math.sqrt(2.0 * math.pi))
    return (value * cdf, cdf + value * density)


def normed(rows, gain):
    scale = lax.rsqrt(jnp.mean(rows * rows, axis=-1, keepdims=True) + EPS)
    return (rows * scale * gain).astype(jnp.bfloat16)


def dot_nn(a, b):
    return jnp.dot(a, b, preferred_element_type=jnp.float32)


def dot_nt(a, b):
    return lax.dot_general(a, b, (((1,), (1,)), ((), ())), preferred_element_type=jnp.float32)


def tile_of(hidden):
    for tile in (256, 128):
        if hidden % tile == 0:
            return tile
    return hidden


IN_VMEM = pl.BlockSpec(memory_space=pltpu.VMEM)
IN_SMEM = pl.BlockSpec(memory_space=pltpu.SMEM)


TOKEN = jax.ShapeDtypeStruct((8, 128), jnp.float32)


def run(body, name, sel, operands, outs, scratch, after=(), cost=COST):
    used, last = 1 + len(operands), 1 + len(operands) + len(after) + len(outs)

    def with_token(*refs):
        refs[last][...] = jnp.zeros(TOKEN.shape, TOKEN.dtype)
        body(*refs[:used], *refs[used + len(after) : last], *refs[last + 1 :])

    held = [math.prod(x.shape) * jnp.dtype(x.dtype).itemsize for x in scratch]
    return pl.pallas_call(
        with_token,
        in_specs=[IN_SMEM] + [IN_VMEM] * (len(operands) + len(after)),
        out_specs=[IN_VMEM] * (len(outs) + 1),
        scratch_shapes=scratch,
        out_shape=[*outs, TOKEN],
        compiler_params=pltpu.CompilerParams(vmem_limit_bytes=max(VMEM_BYTES, 4 * sum(held))),
        cost_estimate=pl.CostEstimate(
            flops=cost, bytes_accessed=cost // 200, transcendentals=0
        ),
        name=name,
    )(sel, *operands, *after)


def bf16(*shape):
    return jax.ShapeDtypeStruct(shape, jnp.bfloat16)


def tiles(hidden):
    tile = tile_of(hidden)
    return [slice(t, t + tile) for t in range(0, hidden, tile)]


def by_section(sel_ref, section, work, own, other):
    @pl.when(sel_ref[0] == section)
    def _():
        work(*own)

    @pl.when(sel_ref[0] != section)
    def _():
        work(*other)


def share_body(group, sel_ref, weight, out):
    rows = out.shape[0]
    start = pl.multiple_of((sel_ref[3] % group) * rows, rows)
    out[...] = weight[pl.ds(start, rows), :]


def share(weight, group, sel, after):
    rows, hidden = weight.shape
    body = functools.partial(share_body, group)
    return run(body, "share", sel, [weight], [bf16(rows // group, hidden)], [], after)


def relay_body(sel_ref, value, out):
    out[...] = value[...]


def relayed(value, sel, after):
    return run(relay_body, "relay", sel, [value], [bf16(*value.shape)], [], after)


def stack_body(sel_ref, *refs):
    for i, piece in enumerate(refs[:-1]):
        refs[-1][i] = piece[...]


def assemble_body(count, sel_ref, *refs):
    pieces, beside, out = refs[:count], refs[count], refs[count + 1]
    rows = pieces[0].shape[0]
    for i, piece in enumerate(pieces):
        for q, value in ((2 * i, piece[...]), (2 * i + 1, beside[i])):
            place = (sel_ref[3] % (2 * count)) ^ q
            out[pl.ds(pl.multiple_of(place * rows, rows), rows), :] = value


def assembled(pieces, sel, after):
    rows, hidden = pieces[0].shape
    count = len(pieces)
    out = bf16(count, rows, hidden)
    stacked, token = run(stack_body, "stack", sel, pieces, [out], [], after)
    beside = swapped(stacked, "dp", 1)
    body = functools.partial(assemble_body, count)
    out = bf16(2 * count * rows, hidden)
    whole, done = run(body, "assemble", sel, [*pieces, beside], [out], [])
    return whole, token, done


def partial_body(count, sel_ref, *refs):
    parts, (gain, w_in, w_out) = refs[:count], refs[count : count + 3]
    stay, leave, xn, acc = refs[count + 3 :]
    rows = parts[0].shape[0]
    late = rows // 2
    for i, part in enumerate(parts):
        xn[i * rows : (i + 1) * rows, :] = normed(part[...].astype(jnp.float32), gain[...])
    for t, tile in enumerate(tiles(w_in.shape[1])):
        act, unused = gelu_pair(dot_nn(xn[...], w_in[:, tile]))
        term = dot_nt(act.astype(jnp.bfloat16), w_out[:, tile])
        acc[...] = term if t == 0 else acc[...] + term
    for i in range(count):
        start = i * rows
        leave[i] = acc[start : start + late, :].astype(jnp.bfloat16)
        stay[i] = acc[start + late : start + rows, :].astype(jnp.bfloat16)


def block0_partials(parts, gain, w_in, w_out, sel, after):
    rows, width = parts[0].shape
    hidden, n = w_in.shape[1], len(parts)
    return run(
        functools.partial(partial_body, n),
        "block0_partial",
        sel,
        [*parts, gain, w_in, w_out],
        [bf16(n, rows // 2, width)] * 2,
        [
            pltpu.VMEM((n * rows, width), jnp.bfloat16),
            pltpu.VMEM((n * rows, width), jnp.float32),
        ],
        after,
    )


def pick_body(count, sel_ref, *refs):
    stay, crossed = refs[:2]
    arrived, outs = refs[2 : 2 + count], refs[2 + count :]
    for i, out in enumerate(outs):
        value = jnp.where(sel_ref[0] == 0, stay[i], crossed[i])
        if count and i == 0:
            value = value.astype(jnp.float32)
            for part in arrived:
                value = value + part[...].astype(jnp.float32)
        out[...] = value


def picked(stay, crossed, arrived, sel):
    count, rows, width = stay.shape
    outs = [bf16(rows, width)] * count
    if arrived:
        outs[0] = jax.ShapeDtypeStruct((rows, width), jnp.float32)
    body = functools.partial(pick_body, len(arrived))
    *chosen, token = run(body, "pick", sel, [stay, crossed, *arrived], outs, [])
    return chosen, token


def denoise_body(tokens, count, sel_ref, *refs):
    latents, sigma, alpha = refs[:3]
    sums, out = refs[3 : 3 + count], refs[3 + count]
    late = out.shape[0]
    base = latents[pl.ds(pl.multiple_of((1 - sel_ref[0]) * late, late), late), :]
    base = base.astype(jnp.float32)
    eps = base
    for part in sums:
        eps = eps + part[...].astype(jnp.float32)
    out[...] = ((base - sigma[...] * eps) / alpha[...]).astype(jnp.bfloat16)


def denoised(latents, sigma, alpha, sums, tokens, sel, after):
    return run(
        functools.partial(denoise_body, tokens, len(sums)),
        "denoise",
        sel,
        [latents, sigma, alpha, *sums],
        [bf16(latents.shape[0] // 2, latents.shape[1])],
        [],
        after,
    )[:2]


def crossing(count):
    near, far = near_and_far(count)
    return [0] + near + far


def state_body(count, sel_ref, *refs):
    parts = refs[:count]
    gain, own, other, act, slope, xn_cols, xn = refs[count:]
    rows = parts[0].shape[0]
    late = rows // 2
    share = xn_cols.shape[0]
    mine = pl.multiple_of((1 - sel_ref[0]) * late, late)
    theirs = pl.multiple_of(sel_ref[0] * late, late)
    at = 0
    for start, order in ((mine, range(len(parts))), (theirs, crossing(len(parts)))):
        for k in order:
            rows_k = parts[k][pl.ds(start, late), :].astype(jnp.float32)
            xn[at : at + late, :] = normed(rows_k, gain[...])
            at += late
    cols = xn[:, pl.ds(pl.multiple_of(sel_ref[0] * share, share), share)]
    xn_cols[...] = cols.T

    def work(weight):
        for tile in tiles(weight.shape[1]):
            value, grad = gelu_pair(dot_nn(xn[...], weight[:, tile]))
            act[:, tile] = value.astype(jnp.bfloat16)
            slope[:, tile] = grad.astype(jnp.bfloat16)

    by_section(sel_ref, 0, work, (own,), (other,))


def block0_state(parts, gain, own, other, sel, after):
    total, width = sum(part.shape[0] for part in parts), parts[0].shape[1]
    hidden = own.shape[1]
    return run(
        functools.partial(state_body, len(parts)),
        "block0_state",
        sel,
        [*parts, gain, own, other],
        [bf16(total, hidden), bf16(total, hidden), bf16(width // 2, total)],
        [pltpu.VMEM((total, width), jnp.bfloat16)],
        after,
        cost=COST // 100,
    )


def reward_body(count, tokens, sel_ref, *refs):
    parts, (gain, text) = refs[:count], refs[count : count + 2]
    own_in, own_out, other_in, other_out = refs[count + 2 : count + 6]
    slopes, (pool, xn) = refs[count + 6 : 2 * count + 6], refs[2 * count + 6 :]
    rows = parts[0].shape[0]
    half = rows // tokens
    row = lax.broadcasted_iota(jnp.int32, pool.shape, 0)
    start = jnp.zeros(pool.shape, jnp.float32)
    for image in range(half):
        own_rows = parts[0][image * tokens : (image + 1) * tokens, :].astype(jnp.float32)
        start = jnp.where(row == image, jnp.mean(own_rows, axis=0, keepdims=True), start)
        start = jnp.where(row == count * half + image, text[image : image + 1, :], start)
    pool[...] = start
    for i, part in enumerate(parts):
        xn[i * rows : (i + 1) * rows, :] = normed(part[...].astype(jnp.float32), gain[...])

    def work(w_in, w_out):
        for tile in tiles(w_in.shape[1]):
            act, grad = gelu_pair(dot_nn(xn[...], w_in[:, tile]))
            for i in range(count):
                slopes[i][:, tile] = grad[i * rows : (i + 1) * rows, :].astype(jnp.bfloat16)
            means = [
                jnp.mean(act[at : at + tokens, :], axis=0, keepdims=True)
                for at in range(0, count * rows, tokens)
            ]
            place = lax.broadcasted_iota(jnp.int32, (pool.shape[0], act.shape[1]), 0)
            stacked = jnp.zeros(place.shape, jnp.float32)
            for i, mean in enumerate(means):
                stacked = jnp.where(place == i, mean, stacked)
            pool[...] += dot_nt(stacked.astype(jnp.bfloat16), w_out[:, tile])

    by_section(sel_ref, 1, work, (own_in, own_out), (other_in, other_out))


def reward_forward(parts, tokens, gain, text, own, other, sel, after):
    rows, width = parts[0].shape
    hidden, n = own[0].shape[1], len(parts)
    images = (n + 1) * rows // tokens
    outs = run(
        functools.partial(reward_body, n, tokens),
        "reward_forward",
        sel,
        [*parts, gain, text, *own, *other],
        [bf16(rows, hidden)] * n
        + [jax.ShapeDtypeStruct((-(-images // 8) * 8, width), jnp.float32)],
        [pltpu.VMEM((n * rows, width), jnp.bfloat16)],
        after,
        cost=COST // 100,
    )
    return outs[:n], outs[n]


def score_gradient(pooled, text):
    unit = text * lax.rsqrt(jnp.mean(text * text, axis=-1, keepdims=True) + EPS)
    scale = lax.rsqrt(jnp.mean(pooled * pooled, axis=-1, keepdims=True) + EPS)
    along = jnp.mean(pooled * unit, axis=-1, keepdims=True)
    return (-100.0 / pooled.shape[-1]) * (scale * unit - pooled * scale**3 * along)


def back_body(count, tokens, sel_ref, *refs):
    pools, slopes = refs[:count], refs[count : 2 * count]
    own_in, own_out, other_in, other_out = refs[2 * count : 2 * count + 4]
    outs = refs[2 * count + 4 : 3 * count + 4]
    g_mean, acc = refs[3 * count + 4 :]
    rows = slopes[0].shape[0]
    half = rows // tokens
    images = count * half
    pooled, texts = [], []
    for j in range(images):
        at = [(j - k * half) % images for k in range(count)]
        pooled.append(sum(pools[k][at[k] : at[k] + 1, :] for k in range(count)))
        text = images + j % half
        texts.append(pools[j // half][text : text + 1, :])
    padded = -(-images // 16) * 16
    row = lax.broadcasted_iota(jnp.int32, (padded, acc.shape[1]), 0)
    stacked, spoken = jnp.zeros(row.shape, jnp.float32), jnp.zeros(row.shape, jnp.float32)
    for j in range(images):
        stacked = jnp.where(row == j, pooled[j], stacked)
        spoken = jnp.where(row == j, texts[j], spoken)
    g_all = score_gradient(stacked, spoken) * (1.0 / tokens)
    g_mean[...] = g_all[: g_mean.shape[0], :]
    g_tok = g_all.astype(jnp.bfloat16)

    def work(w_in, w_out):
        for t, tile in enumerate(tiles(w_in.shape[1])):
            g_h = dot_nn(g_tok, w_out[:, tile])
            terms = []
            for i in range(count):
                for image in range(half):
                    at = i * half + image
                    slope = slopes[i][image * tokens : (image + 1) * tokens, tile]
                    terms.append(
                        (slope.astype(jnp.float32) * g_h[at : at + 1, :]).astype(jnp.bfloat16)
                    )
            term = dot_nt(jnp.concatenate(terms, axis=0), w_in[:, tile])
            acc[...] = term if t == 0 else acc[...] + term

    by_section(sel_ref, 1, work, (own_in, own_out), (other_in, other_out))
    for i, out in enumerate(outs):
        out[...] = acc[i * rows : (i + 1) * rows, :].astype(jnp.bfloat16)


def reward_back(pools, slopes, tokens, own, other, sel):
    rows, hidden = slopes[0].shape
    width, n = own[0].shape[0], len(slopes)
    outs = run(
        functools.partial(back_body, n, tokens),
        "reward_back",
        sel,
        [*pools, *slopes, *own, *other],
        [bf16(rows, width)] * n + [jax.ShapeDtypeStruct((8, width), jnp.float32)],
        [pltpu.VMEM((n * rows, width), jnp.float32)],
        cost=COST // 100,
    )
    return outs[:n], outs[n]


def eps_gradient_body(tokens, count, sel_ref, *refs):
    seen_ref, g_mean, gain, ratio = refs[:4]
    sums, out = refs[4 : 4 + count], refs[4 + count]
    g_xn = sums[0][...].astype(jnp.float32)
    for part in sums[1:]:
        g_xn = g_xn + part[...].astype(jnp.float32)
    seen = seen_ref[...].astype(jnp.float32)
    scale = lax.rsqrt(jnp.mean(seen * seen, axis=-1, keepdims=True) + EPS)
    weighted = gain[...] * g_xn
    along = jnp.mean(seen * weighted, axis=-1, keepdims=True)
    g_norm = scale * weighted - seen * scale**3 * along
    for image in range(out.shape[0] // tokens):
        at = slice(image * tokens, (image + 1) * tokens)
        g_images = (g_mean[image : image + 1, :] + g_norm[at, :]).astype(jnp.bfloat16)
        out[at, :] = (ratio[at, :] * g_images.astype(jnp.float32)).astype(jnp.bfloat16)


def eps_gradient(seen, g_mean, gain, ratio, sums, tokens, sel, after):
    return run(
        functools.partial(eps_gradient_body, tokens, len(sums)),
        "eps_gradient",
        sel,
        [seen, g_mean, gain, ratio, *sums],
        [bf16(*seen.shape)],
        [],
        after,
    )


def put_rows(result, core, keep, away, tile):
    groups, rows, unused = keep.shape
    for g in range(groups):
        even = result[2 * g * rows : (2 * g + 1) * rows, :]
        odd = result[(2 * g + 1) * rows : (2 * g + 2) * rows, :]
        keep[g, :, tile] = jnp.where(core == 0, even, odd).astype(jnp.bfloat16)
        away[g, :, tile] = jnp.where(core == 0, odd, even).astype(jnp.bfloat16)


def gradient_body(count, sel_ref, *refs):
    pieces = refs[:count]
    act, slope, xn_cols, own, other = refs[count : count + 5]
    out_keep, out_away, in_keep, in_away, g_all, turned = refs[count + 5 :]
    share = turned.shape[0]
    core = sel_ref[1]
    at = 0
    for piece in pieces:
        g_all[at : at + piece.shape[0], :] = piece[...]
        at += piece.shape[0]
    cols = g_all[:, pl.ds(pl.multiple_of(sel_ref[0] * share, share), share)]
    turned[...] = cols.T

    def work(weight):
        for tile in tiles(weight.shape[1]):
            put_rows(dot_nn(turned[...], act[:, tile]), core, out_keep, out_away, tile)
            g_h = dot_nn(g_all[...], weight[:, tile])
            g_hidden = (g_h * slope[:, tile].astype(jnp.float32)).astype(jnp.bfloat16)
            put_rows(dot_nn(xn_cols[...], g_hidden), core, in_keep, in_away, tile)

    by_section(sel_ref, 0, work, (own,), (other,))


def gradients(pieces, states, own, other, sel):
    total, width = sum(piece.shape[0] for piece in pieces), pieces[0].shape[1]
    hidden = own.shape[1]
    groups = lax.axis_size("dp") // 2
    outs = run(
        functools.partial(gradient_body, len(pieces)),
        "gradients",
        sel,
        [*pieces, *states, own, other],
        [bf16(groups, width // 2 // (2 * groups), hidden)] * 4,
        [
            pltpu.VMEM((total, width), jnp.bfloat16),
            pltpu.VMEM((width // 2, total), jnp.bfloat16),
        ],
    )
    return outs[:2], outs[2:4]


def chip_body(sel_ref, keep, arrived, mine, others):
    groups = keep.shape[0]
    for k in range(groups):
        at = (sel_ref[2] + k) % groups
        total = keep[at].astype(jnp.float32) + arrived[at].astype(jnp.float32)
        if k == 0:
            mine[...] = total
        else:
            others[k - 1] = total.astype(jnp.bfloat16)


def sum_over_dp(keep, away, sel):
    groups, rows, hidden = keep.shape
    total, others, unused = run(
        chip_body,
        "chip_sum",
        sel,
        [keep, swapped(away, "dp", 1)],
        [jax.ShapeDtypeStruct((rows, hidden), jnp.float32), bf16(groups - 1, rows, hidden)],
        [],
    )
    for k in range(1, groups):
        total = total + rotated(others[k - 1], "dp", 2 * k).astype(jnp.float32)
    return total


def on_device(latents, timesteps, prompt_ids, prompt_table, gains, w_in, w_out):
    count, tokens, width = latents.shape
    half = count // 2
    n_tp = lax.axis_size("tp")
    segment = lax.axis_index("sec")
    first = segment == 0
    dp = lax.axis_index("dp")
    sel = jnp.stack([segment, dp % 2, dp // 2, dp % 4]).astype(jnp.int32)
    own = (w_in[0], w_out[0])

    def my_half(value):
        return jnp.where(first, value[half:], value[:half])

    theta = math.pi / 2.0 * (my_half(timesteps).astype(jnp.float32) + 1.0) / (STEPS + 1.0)
    theta = jnp.repeat(theta, tokens)[:, None]
    alpha, sigma = jnp.cos(theta), jnp.sin(theta)

    flat = latents.reshape(count * tokens, width)
    near, far = near_and_far(n_tp)
    rest = [0] + far
    lat_parts, near_token = gather_in_turn(flat, sel)
    in_share, in_token = share(own[0], 4, sel, ())
    got_in = swapped(in_share, "sec", 1)
    across_in = swapped(got_in, "dp", 2)
    out_share, out_token = share(own[1], 2, sel, [in_token])
    got_out = lax.ppermute(out_share, "sec", [(1, 0)])

    onehot = (
        my_half(prompt_ids)[:, None] == jnp.arange(prompt_table.shape[0], dtype=jnp.int32)[None, :]
    ).astype(jnp.bfloat16)
    text_mine = dot_nn(onehot, prompt_table)

    sums, before = [], [got_in, near_token]
    for ks in (near, rest):
        if ks:
            stay, leave, partial_token = block0_partials(
                [lat_parts[k] for k in ks], gains[:1], *own, sel, before
            )
            crossed = lax.ppermute(leave, "sec", [(0, 1)])
            chosen, picked_token = picked(stay, crossed, sums if ks is rest else [], sel)
            if ks is rest:
                sums = [chosen[0]] + [rotated(part, "tp", -k) for k, part in zip(ks[1:], chosen[1:])]
            else:
                sums = [rotated(part, "tp", -k) for k, part in zip(ks, chosen)]
                before = [picked_token, out_token]
    other_in, unused, in_token = assembled([got_in, across_in], sel, [partial_token])
    other_out, out_token, unused = assembled([got_out], sel, [picked_token])
    other = (other_in, other_out)
    late_share, late_token = share(own[1], 2, sel, [picked_token])
    got_late = lax.ppermute(late_share, "sec", [(0, 1)])
    mine_rows, unused = denoised(
        flat, sigma, alpha, sums, tokens, sel, [in_token, out_token, late_token]
    )

    seen_parts = gather_parts(mine_rows)
    slopes1, pool = reward_forward(
        seen_parts, tokens, gains[1:], text_mine, own, other, sel, ()
    )
    pools = gather_parts(pool)
    g_parts, g_mean = reward_back(pools, slopes1, tokens, own, other, sel)

    *states, state_token = block0_state(
        lat_parts, gains[:1], own[0], other[0], sel, g_parts[:1]
    )

    g_sums = [g_parts[0]] + [rotated(g_parts[k], "tp", -k) for k in range(1, n_tp)]
    ratio = -(sigma / alpha)
    g_eps, eps_token = eps_gradient(
        mine_rows, g_mean, gains[1:], ratio, g_sums, tokens, sel, [state_token]
    )


    g_mine = gather_parts(g_eps)
    pieces = list(g_mine)
    for ks in ([0], near, far):
        if ks:
            pieces.append(swapped(jnp.concatenate([g_mine[k] for k in ks], 0), "sec", 1))
    late_out = assembled([got_late], sel, [state_token])[0]
    out_parts, in_parts = gradients(pieces, states, own[1], late_out, sel)
    grad_out, grad_in = sum_over_dp(*out_parts, sel), sum_over_dp(*in_parts, sel)
    return (grad_in, grad_out)


def solution(mesh):
    in_specs = (
        P(("dp", "tp"), None, None),
        P(("dp", "tp")),
        P(("dp", "tp")),
        P(),
        P(),
        P("sec", None, "tp"),
        P("sec", None, "tp"),
    )
    out_specs = (P(("sec", "dp"), "tp"), P(("sec", "dp"), "tp"))
    return jax.shard_map(
        on_device, mesh=mesh, in_specs=in_specs, out_specs=out_specs, check_vma=False
    )
```

```python
import functools
import math

import jax
import jax.numpy as jnp
from jax import lax
from jax.experimental import pallas as pl
from jax.experimental.pallas import tpu as pltpu
from jax.sharding import PartitionSpec as P

STEPS = 50


EPS = 1e-06
VMEM_BYTES = 8 * 1024 * 1024
COST = 10**11


def rotated(value, axis, steps):
    count = lax.axis_size(axis)
    return lax.ppermute(value, axis, [(i, (i + steps) % count) for i in range(count)])


def swapped(value, axis, bit):
    count = lax.axis_size(axis)
    return lax.ppermute(value, axis, [(i, i ^ bit) for i in range(count)])


def gather_parts(piece):
    return [piece] + [rotated(piece, "tp", k) for k in range(1, lax.axis_size("tp"))]


def gelu_pair(value):
    cdf = 0.5 * (1.0 + lax.erf(value * (1.0 / math.sqrt(2.0))))
    density = jnp.exp(-0.5 * value * value) * (1.0 / math.sqrt(2.0 * math.pi))
    return (value * cdf, cdf + value * density)


def normed(rows, gain):
    scale = lax.rsqrt(jnp.mean(rows * rows, axis=-1, keepdims=True) + EPS)
    return (rows * scale * gain).astype(jnp.bfloat16)


def dot_nn(a, b):
    return jnp.dot(a, b, preferred_element_type=jnp.float32)


def dot_nt(a, b):
    return lax.dot_general(a, b, (((1,), (1,)), ((), ())), preferred_element_type=jnp.float32)


def tile_of(hidden):
    for tile in (256, 128):
        if hidden % tile == 0:
            return tile
    return hidden


IN_VMEM = pl.BlockSpec(memory_space=pltpu.VMEM)
IN_SMEM = pl.BlockSpec(memory_space=pltpu.SMEM)


TOKEN = jax.ShapeDtypeStruct((8, 128), jnp.float32)


def run(body, name, sel, operands, outs, scratch, after=(), cost=COST):
    used, last = 1 + len(operands), 1 + len(operands) + len(after) + len(outs)

    def with_token(*refs):
        refs[last][...] = jnp.zeros(TOKEN.shape, TOKEN.dtype)
        body(*refs[:used], *refs[used + len(after) : last], *refs[last + 1 :])

    held = [math.prod(x.shape) * jnp.dtype(x.dtype).itemsize for x in scratch]
    return pl.pallas_call(
        with_token,
        in_specs=[IN_SMEM] + [IN_VMEM] * (len(operands) + len(after)),
        out_specs=[IN_VMEM] * (len(outs) + 1),
        scratch_shapes=scratch,
        out_shape=[*outs, TOKEN],
        compiler_params=pltpu.CompilerParams(vmem_limit_bytes=max(VMEM_BYTES, 4 * sum(held))),
        cost_estimate=pl.CostEstimate(
            flops=cost, bytes_accessed=cost // 200, transcendentals=0
        ),
        name=name,
    )(sel, *operands, *after)


def bf16(*shape):
    return jax.ShapeDtypeStruct(shape, jnp.bfloat16)


def tiles(hidden):
    tile = tile_of(hidden)
    return [slice(t, t + tile) for t in range(0, hidden, tile)]


def by_section(sel_ref, section, work, own, other):
    @pl.when(sel_ref[0] == section)
    def _():
        work(*own)

    @pl.when(sel_ref[0] != section)
    def _():
        work(*other)


def share_body(group, sel_ref, weight, out):
    rows = out.shape[0]
    start = pl.multiple_of((sel_ref[3] % group) * rows, rows)
    out[...] = weight[pl.ds(start, rows), :]


def share(weight, group, sel, after):
    rows, hidden = weight.shape
    body = functools.partial(share_body, group)
    return run(body, "share", sel, [weight], [bf16(rows // group, hidden)], [], after)


def relay_body(sel_ref, value, out):
    out[...] = value[...]


def relayed(value, sel, after):
    return run(relay_body, "relay", sel, [value], [bf16(*value.shape)], [], after)


def stack_body(sel_ref, *refs):
    for i, piece in enumerate(refs[:-1]):
        refs[-1][i] = piece[...]


def assemble_body(count, sel_ref, *refs):
    pieces, beside, out = refs[:count], refs[count], refs[count + 1]
    rows = pieces[0].shape[0]
    for i, piece in enumerate(pieces):
        for q, value in ((2 * i, piece[...]), (2 * i + 1, beside[i])):
            place = (sel_ref[3] % (2 * count)) ^ q
            out[pl.ds(pl.multiple_of(place * rows, rows), rows), :] = value


def assembled(pieces, sel, after):
    rows, hidden = pieces[0].shape
    count = len(pieces)
    out = bf16(count, rows, hidden)
    stacked = run(stack_body, "stack", sel, pieces, [out], [], after)[0]
    beside = swapped(stacked, "dp", 1)
    body = functools.partial(assemble_body, count)
    out = bf16(2 * count * rows, hidden)
    return run(body, "assemble", sel, [*pieces, beside], [out], [])


def partial_body(count, sel_ref, *refs):
    parts, (gain, w_in, w_out) = refs[:count], refs[count : count + 3]
    stay, leave, xn, acc = refs[count + 3 :]
    rows = parts[0].shape[0]
    late = rows // 2
    for i, part in enumerate(parts):
        xn[i * rows : (i + 1) * rows, :] = normed(part[...].astype(jnp.float32), gain[...])
    for t, tile in enumerate(tiles(w_in.shape[1])):
        act, unused = gelu_pair(dot_nn(xn[...], w_in[:, tile]))
        term = dot_nt(act.astype(jnp.bfloat16), w_out[:, tile])
        acc[...] = term if t == 0 else acc[...] + term
    for i in range(count):
        start = i * rows
        leave[i] = acc[start : start + late, :].astype(jnp.bfloat16)
        stay[i] = acc[start + late : start + rows, :].astype(jnp.bfloat16)


def block0_partials(parts, gain, w_in, w_out, sel, after):
    rows, width = parts[0].shape
    hidden, n = w_in.shape[1], len(parts)
    return run(
        functools.partial(partial_body, n),
        "block0_partial",
        sel,
        [*parts, gain, w_in, w_out],
        [bf16(n, rows // 2, width)] * 2,
        [
            pltpu.VMEM((n * rows, width), jnp.bfloat16),
            pltpu.VMEM((n * rows, width), jnp.float32),
        ],
        after,
    )


def pick_body(count, sel_ref, *refs):
    stay, crossed = refs[:2]
    arrived, outs = refs[2 : 2 + count], refs[2 + count :]
    for i, out in enumerate(outs):
        value = jnp.where(sel_ref[0] == 0, stay[i], crossed[i])
        if count and i == 0:
            value = value.astype(jnp.float32)
            for part in arrived:
                value = value + part[...].astype(jnp.float32)
        out[...] = value


def picked(stay, crossed, arrived, sel):
    count, rows, width = stay.shape
    outs = [bf16(rows, width)] * count
    if arrived:
        outs[0] = jax.ShapeDtypeStruct((rows, width), jnp.float32)
    body = functools.partial(pick_body, len(arrived))
    *chosen, token = run(body, "pick", sel, [stay, crossed, *arrived], outs, [])
    return chosen, token


def denoise_body(tokens, count, sel_ref, *refs):
    latents, sigma, alpha = refs[:3]
    sums, out = refs[3 : 3 + count], refs[3 + count]
    late = out.shape[0]
    base = latents[pl.ds(pl.multiple_of((1 - sel_ref[0]) * late, late), late), :]
    base = base.astype(jnp.float32)
    eps = base
    for part in sums:
        eps = eps + part[...].astype(jnp.float32)
    out[...] = ((base - sigma[...] * eps) / alpha[...]).astype(jnp.bfloat16)


def denoised(latents, sigma, alpha, sums, tokens, sel, after):
    return run(
        functools.partial(denoise_body, tokens, len(sums)),
        "denoise",
        sel,
        [latents, sigma, alpha, *sums],
        [bf16(latents.shape[0] // 2, latents.shape[1])],
        [],
        after,
    )[:2]


def crossing(count):
    near = [k for k in range(1, count) if 2 * k != count]
    return [0] + near + [k for k in range(1, count) if 2 * k == count]


def state_body(count, sel_ref, *refs):
    parts = refs[:count]
    gain, own, other, act, slope, xn_cols, xn = refs[count:]
    rows = parts[0].shape[0]
    late = rows // 2
    share = xn_cols.shape[0]
    mine = pl.multiple_of((1 - sel_ref[0]) * late, late)
    theirs = pl.multiple_of(sel_ref[0] * late, late)
    at = 0
    for start, order in ((mine, range(len(parts))), (theirs, crossing(len(parts)))):
        for k in order:
            rows_k = parts[k][pl.ds(start, late), :].astype(jnp.float32)
            xn[at : at + late, :] = normed(rows_k, gain[...])
            at += late
    cols = xn[:, pl.ds(pl.multiple_of(sel_ref[0] * share, share), share)]
    xn_cols[...] = cols.T

    def work(weight):
        for tile in tiles(weight.shape[1]):
            value, grad = gelu_pair(dot_nn(xn[...], weight[:, tile]))
            act[:, tile] = value.astype(jnp.bfloat16)
            slope[:, tile] = grad.astype(jnp.bfloat16)

    by_section(sel_ref, 0, work, (own,), (other,))


def block0_state(parts, gain, own, other, sel, after):
    total, width = sum(part.shape[0] for part in parts), parts[0].shape[1]
    hidden = own.shape[1]
    return run(
        functools.partial(state_body, len(parts)),
        "block0_state",
        sel,
        [*parts, gain, own, other],
        [bf16(total, hidden), bf16(total, hidden), bf16(width // 2, total)],
        [pltpu.VMEM((total, width), jnp.bfloat16)],
        after,
    )


def reward_body(count, tokens, sel_ref, *refs):
    parts, (gain, text) = refs[:count], refs[count : count + 2]
    own_in, own_out, other_in, other_out = refs[count + 2 : count + 6]
    slopes, (pool, xn) = refs[count + 6 : 2 * count + 6], refs[2 * count + 6 :]
    rows = parts[0].shape[0]
    half = rows // tokens
    row = lax.broadcasted_iota(jnp.int32, pool.shape, 0)
    start = jnp.zeros(pool.shape, jnp.float32)
    for image in range(half):
        own_rows = parts[0][image * tokens : (image + 1) * tokens, :].astype(jnp.float32)
        start = jnp.where(row == image, jnp.mean(own_rows, axis=0, keepdims=True), start)
        start = jnp.where(row == count * half + image, text[image : image + 1, :], start)
    pool[...] = start
    for i, part in enumerate(parts):
        xn[i * rows : (i + 1) * rows, :] = normed(part[...].astype(jnp.float32), gain[...])

    def work(w_in, w_out):
        for tile in tiles(w_in.shape[1]):
            act, grad = gelu_pair(dot_nn(xn[...], w_in[:, tile]))
            for i in range(count):
                slopes[i][:, tile] = grad[i * rows : (i + 1) * rows, :].astype(jnp.bfloat16)
            means = [
                jnp.mean(act[at : at + tokens, :], axis=0, keepdims=True)
                for at in range(0, count * rows, tokens)
            ]
            place = lax.broadcasted_iota(jnp.int32, (pool.shape[0], act.shape[1]), 0)
            stacked = jnp.zeros(place.shape, jnp.float32)
            for i, mean in enumerate(means):
                stacked = jnp.where(place == i, mean, stacked)
            pool[...] += dot_nt(stacked.astype(jnp.bfloat16), w_out[:, tile])

    by_section(sel_ref, 1, work, (own_in, own_out), (other_in, other_out))


def reward_forward(parts, tokens, gain, text, own, other, sel, after):
    rows, width = parts[0].shape
    hidden, n = own[0].shape[1], len(parts)
    images = (n + 1) * rows // tokens
    outs = run(
        functools.partial(reward_body, n, tokens),
        "reward_forward",
        sel,
        [*parts, gain, text, *own, *other],
        [bf16(rows, hidden)] * n
        + [jax.ShapeDtypeStruct((-(-images // 8) * 8, width), jnp.float32)],
        [pltpu.VMEM((n * rows, width), jnp.bfloat16)],
        after,
    )
    return outs[:n], outs[n]


def score_gradient(pooled, text):
    unit = text * lax.rsqrt(jnp.mean(text * text, axis=-1, keepdims=True) + EPS)
    scale = lax.rsqrt(jnp.mean(pooled * pooled, axis=-1, keepdims=True) + EPS)
    along = jnp.mean(pooled * unit, axis=-1, keepdims=True)
    return (-100.0 / pooled.shape[-1]) * (scale * unit - pooled * scale**3 * along)


def back_body(count, tokens, sel_ref, *refs):
    pools, slopes = refs[:count], refs[count : 2 * count]
    own_in, own_out, other_in, other_out = refs[2 * count : 2 * count + 4]
    outs = refs[2 * count + 4 : 3 * count + 4]
    g_mean, acc = refs[3 * count + 4 :]
    rows = slopes[0].shape[0]
    half = rows // tokens
    images = count * half
    pooled, texts = [], []
    for j in range(images):
        at = [(j - k * half) % images for k in range(count)]
        pooled.append(sum(pools[k][at[k] : at[k] + 1, :] for k in range(count)))
        text = images + j % half
        texts.append(pools[j // half][text : text + 1, :])
    padded = -(-images // 16) * 16
    row = lax.broadcasted_iota(jnp.int32, (padded, acc.shape[1]), 0)
    stacked, spoken = jnp.zeros(row.shape, jnp.float32), jnp.zeros(row.shape, jnp.float32)
    for j in range(images):
        stacked = jnp.where(row == j, pooled[j], stacked)
        spoken = jnp.where(row == j, texts[j], spoken)
    g_all = score_gradient(stacked, spoken) * (1.0 / tokens)
    g_mean[...] = g_all[: g_mean.shape[0], :]
    g_tok = g_all.astype(jnp.bfloat16)

    def work(w_in, w_out):
        for t, tile in enumerate(tiles(w_in.shape[1])):
            g_h = dot_nn(g_tok, w_out[:, tile])
            terms = []
            for i in range(count):
                for image in range(half):
                    at = i * half + image
                    slope = slopes[i][image * tokens : (image + 1) * tokens, tile]
                    terms.append(
                        (slope.astype(jnp.float32) * g_h[at : at + 1, :]).astype(jnp.bfloat16)
                    )
            term = dot_nt(jnp.concatenate(terms, axis=0), w_in[:, tile])
            acc[...] = term if t == 0 else acc[...] + term

    by_section(sel_ref, 1, work, (own_in, own_out), (other_in, other_out))
    for i, out in enumerate(outs):
        out[...] = acc[i * rows : (i + 1) * rows, :].astype(jnp.bfloat16)


def reward_back(pools, slopes, tokens, own, other, sel):
    rows, hidden = slopes[0].shape
    width, n = own[0].shape[0], len(slopes)
    outs = run(
        functools.partial(back_body, n, tokens),
        "reward_back",
        sel,
        [*pools, *slopes, *own, *other],
        [bf16(rows, width)] * n + [jax.ShapeDtypeStruct((8, width), jnp.float32)],
        [pltpu.VMEM((n * rows, width), jnp.float32)],
    )
    return outs[:n], outs[n]


def eps_gradient_body(tokens, count, sel_ref, *refs):
    seen_ref, g_mean, gain, ratio = refs[:4]
    sums, out = refs[4 : 4 + count], refs[4 + count]
    g_xn = sums[0][...].astype(jnp.float32)
    for part in sums[1:]:
        g_xn = g_xn + part[...].astype(jnp.float32)
    seen = seen_ref[...].astype(jnp.float32)
    scale = lax.rsqrt(jnp.mean(seen * seen, axis=-1, keepdims=True) + EPS)
    weighted = gain[...] * g_xn
    along = jnp.mean(seen * weighted, axis=-1, keepdims=True)
    g_norm = scale * weighted - seen * scale**3 * along
    for image in range(out.shape[0] // tokens):
        at = slice(image * tokens, (image + 1) * tokens)
        g_images = (g_mean[image : image + 1, :] + g_norm[at, :]).astype(jnp.bfloat16)
        out[at, :] = (ratio[at, :] * g_images.astype(jnp.float32)).astype(jnp.bfloat16)


def eps_gradient(seen, g_mean, gain, ratio, sums, tokens, sel, after):
    return run(
        functools.partial(eps_gradient_body, tokens, len(sums)),
        "eps_gradient",
        sel,
        [seen, g_mean, gain, ratio, *sums],
        [bf16(*seen.shape)],
        [],
        after,
    )


def put_rows(result, core, keep, away, tile):
    groups, rows, unused = keep.shape
    for g in range(groups):
        even = result[2 * g * rows : (2 * g + 1) * rows, :]
        odd = result[(2 * g + 1) * rows : (2 * g + 2) * rows, :]
        keep[g, :, tile] = jnp.where(core == 0, even, odd).astype(jnp.bfloat16)
        away[g, :, tile] = jnp.where(core == 0, odd, even).astype(jnp.bfloat16)


def gradient_body(count, sel_ref, *refs):
    pieces = refs[:count]
    act, slope, xn_cols, own, other = refs[count : count + 5]
    out_keep, out_away, in_keep, in_away, g_all, turned = refs[count + 5 :]
    share = turned.shape[0]
    core = sel_ref[1]
    at = 0
    for piece in pieces:
        g_all[at : at + piece.shape[0], :] = piece[...]
        at += piece.shape[0]
    cols = g_all[:, pl.ds(pl.multiple_of(sel_ref[0] * share, share), share)]
    turned[...] = cols.T

    def work(weight):
        for tile in tiles(weight.shape[1]):
            put_rows(dot_nn(turned[...], act[:, tile]), core, out_keep, out_away, tile)
            g_h = dot_nn(g_all[...], weight[:, tile])
            g_hidden = (g_h * slope[:, tile].astype(jnp.float32)).astype(jnp.bfloat16)
            put_rows(dot_nn(xn_cols[...], g_hidden), core, in_keep, in_away, tile)

    by_section(sel_ref, 0, work, (own,), (other,))


def gradients(pieces, states, own, other, sel):
    total, width = sum(piece.shape[0] for piece in pieces), pieces[0].shape[1]
    hidden = own.shape[1]
    groups = lax.axis_size("dp") // 2
    outs = run(
        functools.partial(gradient_body, len(pieces)),
        "gradients",
        sel,
        [*pieces, *states, own, other],
        [bf16(groups, width // 2 // (2 * groups), hidden)] * 4,
        [
            pltpu.VMEM((total, width), jnp.bfloat16),
            pltpu.VMEM((width // 2, total), jnp.bfloat16),
        ],
    )
    return outs[:2], outs[2:4]


def chip_body(sel_ref, keep, arrived, mine, others):
    groups = keep.shape[0]
    for k in range(groups):
        at = (sel_ref[2] + k) % groups
        total = keep[at].astype(jnp.float32) + arrived[at].astype(jnp.float32)
        if k == 0:
            mine[...] = total
        else:
            others[k - 1] = total.astype(jnp.bfloat16)


def sum_over_dp(keep, away, sel):
    groups, rows, hidden = keep.shape
    total, others, unused = run(
        chip_body,
        "chip_sum",
        sel,
        [keep, swapped(away, "dp", 1)],
        [jax.ShapeDtypeStruct((rows, hidden), jnp.float32), bf16(groups - 1, rows, hidden)],
        [],
    )
    for k in range(1, groups):
        total = total + rotated(others[k - 1], "dp", 2 * k).astype(jnp.float32)
    return total


def on_device(latents, timesteps, prompt_ids, prompt_table, gains, w_in, w_out):
    count, tokens, width = latents.shape
    half = count // 2
    n_tp = lax.axis_size("tp")
    segment = lax.axis_index("sec")
    first = segment == 0
    dp = lax.axis_index("dp")
    sel = jnp.stack([segment, dp % 2, dp // 2, dp % 4]).astype(jnp.int32)
    own = (w_in[0], w_out[0])

    def my_half(value):
        return jnp.where(first, value[half:], value[:half])

    theta = math.pi / 2.0 * (my_half(timesteps).astype(jnp.float32) + 1.0) / (STEPS + 1.0)
    theta = jnp.repeat(theta, tokens)[:, None]
    alpha, sigma = jnp.cos(theta), jnp.sin(theta)

    flat = latents.reshape(count * tokens, width)
    near = [k for k in range(1, n_tp) if 2 * k != n_tp]
    rest = [0] + [k for k in range(1, n_tp) if 2 * k == n_tp]
    lat_parts = [flat] + [None] * (n_tp - 1)
    for k in near:
        lat_parts[k] = rotated(flat, "tp", k)
    again, near_token = relayed(flat, sel, [lat_parts[k] for k in near])
    for k in rest[1:]:
        lat_parts[k] = rotated(again, "tp", k)
    got_in = swapped(share(own[0], 4, sel, ())[0], "sec", 1)
    got_again, in_token = relayed(got_in, sel, [near_token])
    across_in = swapped(got_again, "dp", 2)
    out_share, out_token = share(own[1], 2, sel, [near_token])
    got_out = lax.ppermute(out_share, "sec", [(1, 0)])

    onehot = (
        my_half(prompt_ids)[:, None] == jnp.arange(prompt_table.shape[0], dtype=jnp.int32)[None, :]
    ).astype(jnp.bfloat16)
    text_mine = dot_nn(onehot, prompt_table)

    sums, before = [], [in_token]
    for ks in (near, rest):
        if ks:
            stay, leave, partial_token = block0_partials(
                [lat_parts[k] for k in ks], gains[:1], *own, sel, before
            )
            crossed = lax.ppermute(leave, "sec", [(0, 1)])
            chosen, picked_token = picked(stay, crossed, sums if ks is rest else [], sel)
            if ks is rest:
                sums = [chosen[0]] + [rotated(part, "tp", -k) for k, part in zip(ks[1:], chosen[1:])]
            else:
                sums = [rotated(part, "tp", -k) for k, part in zip(ks, chosen)]
                before = [partial_token, out_token]
    other_in, in_token = assembled([got_in, across_in], sel, [partial_token])
    mine_rows, unused = denoised(flat, sigma, alpha, sums, tokens, sel, [in_token])

    seen_parts = gather_parts(mine_rows)
    near_seen = [seen_parts[k] for k in near]
    other_out, joined_token = assembled([got_out], sel, near_seen)
    other = (other_in, other_out)
    late_share, late_token = share(own[1], 2, sel, [joined_token])
    got_late = lax.ppermute(late_share, "sec", [(0, 1)])
    slopes1, pool = reward_forward(
        seen_parts, tokens, gains[1:], text_mine, own, other, sel, ()
    )
    pools = gather_parts(pool)
    g_parts, g_mean = reward_back(pools, slopes1, tokens, own, other, sel)

    *states, state_token = block0_state(
        lat_parts, gains[:1], own[0], other[0], sel, g_parts[:1]
    )

    g_sums = [g_parts[0]] + [rotated(g_parts[k], "tp", -k) for k in range(1, n_tp)]
    ratio = -(sigma / alpha)
    g_eps, eps_token = eps_gradient(
        mine_rows, g_mean, gains[1:], ratio, g_sums, tokens, sel, [state_token]
    )


    g_mine = gather_parts(g_eps)
    pieces = list(g_mine)
    for ks in ([0], near, rest[1:]):
        if ks:
            pieces.append(swapped(jnp.concatenate([g_mine[k] for k in ks], 0), "sec", 1))
    late_out = assembled([got_late], sel, [g_mine[k] for k in near])[0]
    out_parts, in_parts = gradients(pieces, states, own[1], late_out, sel)
    grad_out, grad_in = sum_over_dp(*out_parts, sel), sum_over_dp(*in_parts, sel)
    return (grad_in, grad_out)


def solution(mesh):
    in_specs = (
        P(("dp", "tp"), None, None),
        P(("dp", "tp")),
        P(("dp", "tp")),
        P(),
        P(),
        P("sec", None, "tp"),
        P("sec", None, "tp"),
    )
    out_specs = (P(("sec", "dp"), "tp"), P(("sec", "dp"), "tp"))
    return jax.shard_map(
        on_device, mesh=mesh, in_specs=in_specs, out_specs=out_specs, check_vma=False
    )
```

```python
import functools
import math

import jax
import jax.numpy as jnp
from jax import lax
from jax.experimental import pallas as pl
from jax.experimental.pallas import tpu as pltpu
from jax.sharding import PartitionSpec as P

STEPS = 50


EPS = 1e-06
VMEM_BYTES = 8 * 1024 * 1024
COST = 10**11


def rotated(value, axis, steps):
    count = lax.axis_size(axis)
    return lax.ppermute(value, axis, [(i, (i + steps) % count) for i in range(count)])


def swapped(value, axis, bit):
    count = lax.axis_size(axis)
    return lax.ppermute(value, axis, [(i, i ^ bit) for i in range(count)])


def gather_parts(piece):
    return [piece] + [rotated(piece, "tp", k) for k in range(1, lax.axis_size("tp"))]


def gelu_pair(value):
    cdf = 0.5 * (1.0 + lax.erf(value * (1.0 / math.sqrt(2.0))))
    density = jnp.exp(-0.5 * value * value) * (1.0 / math.sqrt(2.0 * math.pi))
    return (value * cdf, cdf + value * density)


def normed(rows, gain):
    scale = lax.rsqrt(jnp.mean(rows * rows, axis=-1, keepdims=True) + EPS)
    return (rows * scale * gain).astype(jnp.bfloat16)


def dot_nn(a, b):
    return jnp.dot(a, b, preferred_element_type=jnp.float32)


def dot_nt(a, b):
    return lax.dot_general(a, b, (((1,), (1,)), ((), ())), preferred_element_type=jnp.float32)


def tile_of(hidden):
    for tile in (256, 128):
        if hidden % tile == 0:
            return tile
    return hidden


IN_VMEM = pl.BlockSpec(memory_space=pltpu.VMEM)
IN_SMEM = pl.BlockSpec(memory_space=pltpu.SMEM)


TOKEN = jax.ShapeDtypeStruct((8, 128), jnp.float32)


def run(body, name, sel, operands, outs, scratch, after=(), cost=COST):
    used, last = 1 + len(operands), 1 + len(operands) + len(after) + len(outs)

    def with_token(*refs):
        refs[last][...] = jnp.zeros(TOKEN.shape, TOKEN.dtype)
        body(*refs[:used], *refs[used + len(after) : last], *refs[last + 1 :])

    held = [math.prod(x.shape) * jnp.dtype(x.dtype).itemsize for x in scratch]
    return pl.pallas_call(
        with_token,
        in_specs=[IN_SMEM] + [IN_VMEM] * (len(operands) + len(after)),
        out_specs=[IN_VMEM] * (len(outs) + 1),
        scratch_shapes=scratch,
        out_shape=[*outs, TOKEN],
        compiler_params=pltpu.CompilerParams(vmem_limit_bytes=max(VMEM_BYTES, 4 * sum(held))),
        cost_estimate=pl.CostEstimate(
            flops=cost, bytes_accessed=cost // 200, transcendentals=0
        ),
        name=name,
    )(sel, *operands, *after)


def bf16(*shape):
    return jax.ShapeDtypeStruct(shape, jnp.bfloat16)


def tiles(hidden):
    tile = tile_of(hidden)
    return [slice(t, t + tile) for t in range(0, hidden, tile)]


def by_section(sel_ref, section, work, own, other):
    @pl.when(sel_ref[0] == section)
    def _():
        work(*own)

    @pl.when(sel_ref[0] != section)
    def _():
        work(*other)


def share_body(group, sel_ref, weight, out):
    rows = out.shape[0]
    start = pl.multiple_of((sel_ref[3] % group) * rows, rows)
    out[...] = weight[pl.ds(start, rows), :]


def share(weight, group, sel, after):
    rows, hidden = weight.shape
    body = functools.partial(share_body, group)
    return run(body, "share", sel, [weight], [bf16(rows // group, hidden)], [], after)


def relay_body(sel_ref, value, out):
    out[...] = value[...]


def relayed(value, sel, after):
    return run(relay_body, "relay", sel, [value], [bf16(*value.shape)], [], after)


def join_body(sel_ref, *refs):
    rows = refs[0].shape[0]
    for i, piece in enumerate(refs[:-1]):
        refs[-1][i * rows : (i + 1) * rows, :] = piece[...]


def joined_rows(pieces, sel):
    out = bf16(sum(piece.shape[0] for piece in pieces), pieces[0].shape[1])
    return run(join_body, "join", sel, pieces, [out], [], (), 1)


def stack_body(sel_ref, *refs):
    for i, piece in enumerate(refs[:-1]):
        refs[-1][i] = piece[...]


def assemble_body(count, sel_ref, *refs):
    pieces, beside, out = refs[:count], refs[count], refs[count + 1]
    rows = pieces[0].shape[0]
    for i, piece in enumerate(pieces):
        for q, value in ((2 * i, piece[...]), (2 * i + 1, beside[i])):
            place = (sel_ref[3] % (2 * count)) ^ q
            out[pl.ds(pl.multiple_of(place * rows, rows), rows), :] = value


def assembled(pieces, sel, after, cost=COST):
    rows, hidden = pieces[0].shape
    count = len(pieces)
    out = bf16(count, rows, hidden)
    stacked = run(stack_body, "stack", sel, pieces, [out], [], after, cost)[0]
    beside = swapped(stacked, "dp", 1)
    body = functools.partial(assemble_body, count)
    out = bf16(2 * count * rows, hidden)
    return run(body, "assemble", sel, [*pieces, beside], [out], [], (), cost)


def partial_body(count, sel_ref, *refs):
    parts, (gain, w_in, w_out) = refs[:count], refs[count : count + 3]
    stay, leave, xn, acc = refs[count + 3 :]
    rows = parts[0].shape[0]
    late = rows // 2
    for i, part in enumerate(parts):
        xn[i * rows : (i + 1) * rows, :] = normed(part[...].astype(jnp.float32), gain[...])
    for t, tile in enumerate(tiles(w_in.shape[1])):
        act, unused = gelu_pair(dot_nn(xn[...], w_in[:, tile]))
        term = dot_nt(act.astype(jnp.bfloat16), w_out[:, tile])
        acc[...] = term if t == 0 else acc[...] + term
    for i in range(count):
        start = i * rows
        leave[i] = acc[start : start + late, :].astype(jnp.bfloat16)
        stay[i] = acc[start + late : start + rows, :].astype(jnp.bfloat16)


def block0_partials(parts, gain, w_in, w_out, sel, after):
    rows, width = parts[0].shape
    hidden, n = w_in.shape[1], len(parts)
    return run(
        functools.partial(partial_body, n),
        "block0_partial",
        sel,
        [*parts, gain, w_in, w_out],
        [bf16(n, rows // 2, width)] * 2,
        [
            pltpu.VMEM((n * rows, width), jnp.bfloat16),
            pltpu.VMEM((n * rows, width), jnp.float32),
        ],
        after,
    )


def pick_body(count, sel_ref, *refs):
    stay, crossed = refs[:2]
    arrived, outs = refs[2 : 2 + count], refs[2 + count :]
    for i, out in enumerate(outs):
        value = jnp.where(sel_ref[0] == 0, stay[i], crossed[i])
        if count and i == 0:
            value = value.astype(jnp.float32)
            for part in arrived:
                value = value + part[...].astype(jnp.float32)
        out[...] = value


def picked(stay, crossed, arrived, sel):
    count, rows, width = stay.shape
    outs = [bf16(rows, width)] * count
    if arrived:
        outs[0] = jax.ShapeDtypeStruct((rows, width), jnp.float32)
    body = functools.partial(pick_body, len(arrived))
    *chosen, token = run(body, "pick", sel, [stay, crossed, *arrived], outs, [])
    return chosen, token


def denoise_body(tokens, count, sel_ref, *refs):
    latents, sigma, alpha = refs[:3]
    sums, out = refs[3 : 3 + count], refs[3 + count]
    late = out.shape[0]
    base = latents[pl.ds(pl.multiple_of((1 - sel_ref[0]) * late, late), late), :]
    base = base.astype(jnp.float32)
    eps = base
    for part in sums:
        eps = eps + part[...].astype(jnp.float32)
    out[...] = ((base - sigma[...] * eps) / alpha[...]).astype(jnp.bfloat16)


def denoised(latents, sigma, alpha, sums, tokens, sel, after):
    return run(
        functools.partial(denoise_body, tokens, len(sums)),
        "denoise",
        sel,
        [latents, sigma, alpha, *sums],
        [bf16(latents.shape[0] // 2, latents.shape[1])],
        [],
        after,
    )[:2]


def crossing(count):
    near = [k for k in range(1, count) if 2 * k != count]
    return [0] + near + [k for k in range(1, count) if 2 * k == count]


def state_body(count, sel_ref, *refs):
    parts = refs[:count]
    gain, own, other, act, slope, xn_cols, xn = refs[count:]
    rows = parts[0].shape[0]
    late = rows // 2
    share = xn_cols.shape[0]
    mine = pl.multiple_of((1 - sel_ref[0]) * late, late)
    theirs = pl.multiple_of(sel_ref[0] * late, late)
    at = 0
    for start, order in ((mine, range(len(parts))), (theirs, crossing(len(parts)))):
        for k in order:
            rows_k = parts[k][pl.ds(start, late), :].astype(jnp.float32)
            xn[at : at + late, :] = normed(rows_k, gain[...])
            at += late
    cols = xn[:, pl.ds(pl.multiple_of(sel_ref[0] * share, share), share)]
    xn_cols[...] = cols.T

    def work(weight):
        for tile in tiles(weight.shape[1]):
            value, grad = gelu_pair(dot_nn(xn[...], weight[:, tile]))
            act[:, tile] = value.astype(jnp.bfloat16)
            slope[:, tile] = grad.astype(jnp.bfloat16)

    by_section(sel_ref, 0, work, (own,), (other,))


def block0_state(parts, gain, own, other, sel, after):
    total, width = sum(part.shape[0] for part in parts), parts[0].shape[1]
    hidden = own.shape[1]
    return run(
        functools.partial(state_body, len(parts)),
        "block0_state",
        sel,
        [*parts, gain, own, other],
        [bf16(total, hidden), bf16(total, hidden), bf16(width // 2, total)],
        [pltpu.VMEM((total, width), jnp.bfloat16)],
        after,
    )


def reward_body(count, tokens, sel_ref, *refs):
    parts, (gain, text) = refs[:count], refs[count : count + 2]
    own_in, own_out, other_in, other_out = refs[count + 2 : count + 6]
    slopes, (pool, xn) = refs[count + 6 : 2 * count + 6], refs[2 * count + 6 :]
    rows = parts[0].shape[0]
    half = rows // tokens
    row = lax.broadcasted_iota(jnp.int32, pool.shape, 0)
    start = jnp.zeros(pool.shape, jnp.float32)
    for image in range(half):
        own_rows = parts[0][image * tokens : (image + 1) * tokens, :].astype(jnp.float32)
        start = jnp.where(row == image, jnp.mean(own_rows, axis=0, keepdims=True), start)
        start = jnp.where(row == count * half + image, text[image : image + 1, :], start)
    pool[...] = start
    for i, part in enumerate(parts):
        xn[i * rows : (i + 1) * rows, :] = normed(part[...].astype(jnp.float32), gain[...])

    def work(w_in, w_out):
        for tile in tiles(w_in.shape[1]):
            act, grad = gelu_pair(dot_nn(xn[...], w_in[:, tile]))
            for i in range(count):
                slopes[i][:, tile] = grad[i * rows : (i + 1) * rows, :].astype(jnp.bfloat16)
            means = [
                jnp.mean(act[at : at + tokens, :], axis=0, keepdims=True)
                for at in range(0, count * rows, tokens)
            ]
            place = lax.broadcasted_iota(jnp.int32, (pool.shape[0], act.shape[1]), 0)
            stacked = jnp.zeros(place.shape, jnp.float32)
            for i, mean in enumerate(means):
                stacked = jnp.where(place == i, mean, stacked)
            pool[...] += dot_nt(stacked.astype(jnp.bfloat16), w_out[:, tile])

    by_section(sel_ref, 1, work, (own_in, own_out), (other_in, other_out))


def reward_forward(parts, tokens, gain, text, own, other, sel, after):
    rows, width = parts[0].shape
    hidden, n = own[0].shape[1], len(parts)
    images = (n + 1) * rows // tokens
    outs = run(
        functools.partial(reward_body, n, tokens),
        "reward_forward",
        sel,
        [*parts, gain, text, *own, *other],
        [bf16(rows, hidden)] * n
        + [jax.ShapeDtypeStruct((-(-images // 8) * 8, width), jnp.float32)],
        [pltpu.VMEM((n * rows, width), jnp.bfloat16)],
        after,
    )
    return outs[:n], outs[n]


def score_gradient(pooled, text):
    unit = text * lax.rsqrt(jnp.mean(text * text, axis=-1, keepdims=True) + EPS)
    scale = lax.rsqrt(jnp.mean(pooled * pooled, axis=-1, keepdims=True) + EPS)
    along = jnp.mean(pooled * unit, axis=-1, keepdims=True)
    return (-100.0 / pooled.shape[-1]) * (scale * unit - pooled * scale**3 * along)


def back_body(count, tokens, sel_ref, *refs):
    pools, slopes = refs[:count], refs[count : 2 * count]
    own_in, own_out, other_in, other_out = refs[2 * count : 2 * count + 4]
    outs = refs[2 * count + 4 : 3 * count + 4]
    g_mean, acc = refs[3 * count + 4 :]
    rows = slopes[0].shape[0]
    half = rows // tokens
    images = count * half
    pooled, texts = [], []
    for j in range(images):
        at = [(j - k * half) % images for k in range(count)]
        pooled.append(sum(pools[k][at[k] : at[k] + 1, :] for k in range(count)))
        text = images + j % half
        texts.append(pools[j // half][text : text + 1, :])
    padded = -(-images // 16) * 16
    row = lax.broadcasted_iota(jnp.int32, (padded, acc.shape[1]), 0)
    stacked, spoken = jnp.zeros(row.shape, jnp.float32), jnp.zeros(row.shape, jnp.float32)
    for j in range(images):
        stacked = jnp.where(row == j, pooled[j], stacked)
        spoken = jnp.where(row == j, texts[j], spoken)
    g_all = score_gradient(stacked, spoken) * (1.0 / tokens)
    g_mean[...] = g_all[: g_mean.shape[0], :]
    g_tok = g_all.astype(jnp.bfloat16)

    def work(w_in, w_out):
        for t, tile in enumerate(tiles(w_in.shape[1])):
            g_h = dot_nn(g_tok, w_out[:, tile])
            terms = []
            for i in range(count):
                for image in range(half):
                    at = i * half + image
                    slope = slopes[i][image * tokens : (image + 1) * tokens, tile]
                    terms.append(
                        (slope.astype(jnp.float32) * g_h[at : at + 1, :]).astype(jnp.bfloat16)
                    )
            term = dot_nt(jnp.concatenate(terms, axis=0), w_in[:, tile])
            acc[...] = term if t == 0 else acc[...] + term

    by_section(sel_ref, 1, work, (own_in, own_out), (other_in, other_out))
    for i, out in enumerate(outs):
        out[...] = acc[i * rows : (i + 1) * rows, :].astype(jnp.bfloat16)


def reward_back(pools, slopes, tokens, own, other, sel):
    rows, hidden = slopes[0].shape
    width, n = own[0].shape[0], len(slopes)
    outs = run(
        functools.partial(back_body, n, tokens),
        "reward_back",
        sel,
        [*pools, *slopes, *own, *other],
        [bf16(rows, width)] * n + [jax.ShapeDtypeStruct((8, width), jnp.float32)],
        [pltpu.VMEM((n * rows, width), jnp.float32)],
    )
    return outs[:n], outs[n]


def eps_gradient_body(tokens, count, sel_ref, *refs):
    seen_ref, g_mean, gain, ratio = refs[:4]
    sums, out = refs[4 : 4 + count], refs[4 + count]
    g_xn = sums[0][...].astype(jnp.float32)
    for part in sums[1:]:
        g_xn = g_xn + part[...].astype(jnp.float32)
    seen = seen_ref[...].astype(jnp.float32)
    scale = lax.rsqrt(jnp.mean(seen * seen, axis=-1, keepdims=True) + EPS)
    weighted = gain[...] * g_xn
    along = jnp.mean(seen * weighted, axis=-1, keepdims=True)
    g_norm = scale * weighted - seen * scale**3 * along
    for image in range(out.shape[0] // tokens):
        at = slice(image * tokens, (image + 1) * tokens)
        g_images = (g_mean[image : image + 1, :] + g_norm[at, :]).astype(jnp.bfloat16)
        out[at, :] = (ratio[at, :] * g_images.astype(jnp.float32)).astype(jnp.bfloat16)


def eps_gradient(seen, g_mean, gain, ratio, sums, tokens, sel, after):
    return run(
        functools.partial(eps_gradient_body, tokens, len(sums)),
        "eps_gradient",
        sel,
        [seen, g_mean, gain, ratio, *sums],
        [bf16(*seen.shape)],
        [],
        after,
    )


def put_rows(result, core, keep, away, tile):
    groups, rows, unused = keep.shape
    for g in range(groups):
        even = result[2 * g * rows : (2 * g + 1) * rows, :]
        odd = result[(2 * g + 1) * rows : (2 * g + 2) * rows, :]
        keep[g, :, tile] = jnp.where(core == 0, even, odd).astype(jnp.bfloat16)
        away[g, :, tile] = jnp.where(core == 0, odd, even).astype(jnp.bfloat16)


def gradient_body(count, sel_ref, *refs):
    pieces = refs[:count]
    act, slope, xn_cols, own, other = refs[count : count + 5]
    out_keep, out_away, in_keep, in_away, g_all, turned = refs[count + 5 :]
    share = turned.shape[0]
    core = sel_ref[1]
    at = 0
    for piece in pieces:
        g_all[at : at + piece.shape[0], :] = piece[...]
        at += piece.shape[0]
    cols = g_all[:, pl.ds(pl.multiple_of(sel_ref[0] * share, share), share)]
    turned[...] = cols.T

    def work(weight):
        for tile in tiles(weight.shape[1]):
            put_rows(dot_nn(turned[...], act[:, tile]), core, out_keep, out_away, tile)
            g_h = dot_nn(g_all[...], weight[:, tile])
            g_hidden = (g_h * slope[:, tile].astype(jnp.float32)).astype(jnp.bfloat16)
            put_rows(dot_nn(xn_cols[...], g_hidden), core, in_keep, in_away, tile)

    by_section(sel_ref, 0, work, (own,), (other,))


def gradients(pieces, states, own, other, sel):
    total, width = sum(piece.shape[0] for piece in pieces), pieces[0].shape[1]
    hidden = own.shape[1]
    groups = lax.axis_size("dp") // 2
    outs = run(
        functools.partial(gradient_body, len(pieces)),
        "gradients",
        sel,
        [*pieces, *states, own, other],
        [bf16(groups, width // 2 // (2 * groups), hidden)] * 4,
        [
            pltpu.VMEM((total, width), jnp.bfloat16),
            pltpu.VMEM((width // 2, total), jnp.bfloat16),
        ],
    )
    return outs[:2], outs[2:4]


def chip_body(sel_ref, keep, arrived, mine, others):
    groups = keep.shape[0]
    for k in range(groups):
        at = (sel_ref[2] + k) % groups
        total = keep[at].astype(jnp.float32) + arrived[at].astype(jnp.float32)
        if k == 0:
            mine[...] = total
        else:
            others[k - 1] = total.astype(jnp.bfloat16)


def sum_over_dp(keep, away, sel):
    groups, rows, hidden = keep.shape
    total, others, unused = run(
        chip_body,
        "chip_sum",
        sel,
        [keep, swapped(away, "dp", 1)],
        [jax.ShapeDtypeStruct((rows, hidden), jnp.float32), bf16(groups - 1, rows, hidden)],
        [],
    )
    for k in range(1, groups):
        total = total + rotated(others[k - 1], "dp", 2 * k).astype(jnp.float32)
    return total


def on_device(latents, timesteps, prompt_ids, prompt_table, gains, w_in, w_out):
    count, tokens, width = latents.shape
    half = count // 2
    n_tp = lax.axis_size("tp")
    segment = lax.axis_index("sec")
    first = segment == 0
    dp = lax.axis_index("dp")
    sel = jnp.stack([segment, dp % 2, dp // 2, dp % 4]).astype(jnp.int32)
    own = (w_in[0], w_out[0])

    def my_half(value):
        return jnp.where(first, value[half:], value[:half])

    theta = math.pi / 2.0 * (my_half(timesteps).astype(jnp.float32) + 1.0) / (STEPS + 1.0)
    theta = jnp.repeat(theta, tokens)[:, None]
    alpha, sigma = jnp.cos(theta), jnp.sin(theta)

    flat = latents.reshape(count * tokens, width)
    near = [k for k in range(1, n_tp) if 2 * k != n_tp]
    rest = [0] + [k for k in range(1, n_tp) if 2 * k == n_tp]
    lat_parts = [flat] + [None] * (n_tp - 1)
    for k in near:
        lat_parts[k] = rotated(flat, "tp", k)
    again, near_token = relayed(flat, sel, [lat_parts[k] for k in near])
    for k in rest[1:]:
        lat_parts[k] = rotated(again, "tp", k)
    got_in = swapped(share(own[0], 4, sel, ())[0], "sec", 1)
    got_again, in_token = relayed(got_in, sel, [near_token])
    across_in = swapped(got_again, "dp", 2)
    out_share, out_token = share(own[1], 2, sel, [near_token])
    got_out = lax.ppermute(out_share, "sec", [(1, 0)])

    onehot = (
        my_half(prompt_ids)[:, None] == jnp.arange(prompt_table.shape[0], dtype=jnp.int32)[None, :]
    ).astype(jnp.bfloat16)
    text_mine = dot_nn(onehot, prompt_table)

    sums, before = [], [in_token]
    for ks in (near, rest):
        if ks:
            stay, leave, partial_token = block0_partials(
                [lat_parts[k] for k in ks], gains[:1], *own, sel, before
            )
            crossed = lax.ppermute(leave, "sec", [(0, 1)])
            chosen, picked_token = picked(stay, crossed, sums if ks is rest else [], sel)
            if ks is rest:
                sums = [chosen[0]] + [rotated(part, "tp", -k) for k, part in zip(ks[1:], chosen[1:])]
            else:
                sums = [rotated(part, "tp", -k) for k, part in zip(ks, chosen)]
                before = [partial_token, out_token]
    other_in, in_token = assembled([got_in, across_in], sel, [partial_token])
    mine_rows, unused = denoised(flat, sigma, alpha, sums, tokens, sel, [in_token])

    seen_parts = gather_parts(mine_rows)
    near_seen = [seen_parts[k] for k in near]
    other_out, joined_token = assembled([got_out], sel, near_seen)
    other = (other_in, other_out)
    late_share, late_token = share(own[1], 2, sel, [joined_token])
    got_late = lax.ppermute(late_share, "sec", [(0, 1)])
    slopes1, pool = reward_forward(
        seen_parts, tokens, gains[1:], text_mine, own, other, sel, ()
    )
    pools = gather_parts(pool)
    g_parts, g_mean = reward_back(pools, slopes1, tokens, own, other, sel)

    *states, state_token = block0_state(
        lat_parts, gains[:1], own[0], other[0], sel, g_parts[:1]
    )

    g_sums = [g_parts[0]] + [rotated(g_parts[k], "tp", -k) for k in range(1, n_tp)]
    ratio = -(sigma / alpha)
    g_eps, eps_token = eps_gradient(
        mine_rows, g_mean, gains[1:], ratio, g_sums, tokens, sel, [state_token]
    )


    g_mine = gather_parts(g_eps)
    pieces = g_mine + [swapped(g_eps, "sec", 1)]
    arrived = [pieces[-1]]
    for ks in (near, rest[1:]):
        if ks:
            joined, token = joined_rows([g_mine[k] for k in ks], sel)
            pieces.append(swapped(joined, "sec", 1))
            arrived += [pieces[-1]] if ks is near else [token]
    late_out = assembled([got_late], sel, arrived, 1)[0]
    out_parts, in_parts = gradients(pieces, states, own[1], late_out, sel)
    grad_out, grad_in = sum_over_dp(*out_parts, sel), sum_over_dp(*in_parts, sel)
    return (grad_in, grad_out)


def solution(mesh):
    in_specs = (
        P(("dp", "tp"), None, None),
        P(("dp", "tp")),
        P(("dp", "tp")),
        P(),
        P(),
        P("sec", None, "tp"),
        P("sec", None, "tp"),
    )
    out_specs = (P(("sec", "dp"), "tp"), P(("sec", "dp"), "tp"))
    return jax.shard_map(
        on_device, mesh=mesh, in_specs=in_specs, out_specs=out_specs, check_vma=False
    )
```

```python
import functools
import math

import jax
import jax.numpy as jnp
from jax import lax
from jax.experimental import pallas as pl
from jax.experimental.pallas import tpu as pltpu
from jax.sharding import PartitionSpec as P

STEPS = 50


EPS = 1e-06
VMEM_BYTES = 8 * 1024 * 1024
COST = 10**11


def rotated(value, axis, steps):
    count = lax.axis_size(axis)
    return lax.ppermute(value, axis, [(i, (i + steps) % count) for i in range(count)])


def swapped(value, axis, bit):
    count = lax.axis_size(axis)
    return lax.ppermute(value, axis, [(i, i ^ bit) for i in range(count)])


def gather_parts(piece):
    return [piece] + [rotated(piece, "tp", k) for k in range(1, lax.axis_size("tp"))]


def gelu_pair(value):
    cdf = 0.5 * (1.0 + lax.erf(value * (1.0 / math.sqrt(2.0))))
    density = jnp.exp(-0.5 * value * value) * (1.0 / math.sqrt(2.0 * math.pi))
    return (value * cdf, cdf + value * density)


def normed(rows, gain):
    scale = lax.rsqrt(jnp.mean(rows * rows, axis=-1, keepdims=True) + EPS)
    return (rows * scale * gain).astype(jnp.bfloat16)


def dot_nn(a, b):
    return jnp.dot(a, b, preferred_element_type=jnp.float32)


def dot_nt(a, b):
    return lax.dot_general(a, b, (((1,), (1,)), ((), ())), preferred_element_type=jnp.float32)


def tile_of(hidden):
    for tile in (256, 128):
        if hidden % tile == 0:
            return tile
    return hidden


IN_VMEM = pl.BlockSpec(memory_space=pltpu.VMEM)
IN_SMEM = pl.BlockSpec(memory_space=pltpu.SMEM)


TOKEN = jax.ShapeDtypeStruct((8, 128), jnp.float32)


def run(body, name, sel, operands, outs, scratch, after=(), cost=COST):
    used, last = 1 + len(operands), 1 + len(operands) + len(after) + len(outs)

    def with_token(*refs):
        refs[last][...] = jnp.zeros(TOKEN.shape, TOKEN.dtype)
        body(*refs[:used], *refs[used + len(after) : last], *refs[last + 1 :])

    held = [math.prod(x.shape) * jnp.dtype(x.dtype).itemsize for x in scratch]
    return pl.pallas_call(
        with_token,
        in_specs=[IN_SMEM] + [IN_VMEM] * (len(operands) + len(after)),
        out_specs=[IN_VMEM] * (len(outs) + 1),
        scratch_shapes=scratch,
        out_shape=[*outs, TOKEN],
        compiler_params=pltpu.CompilerParams(vmem_limit_bytes=max(VMEM_BYTES, 4 * sum(held))),
        cost_estimate=pl.CostEstimate(
            flops=cost, bytes_accessed=cost // 200, transcendentals=0
        ),
        name=name,
    )(sel, *operands, *after)


def bf16(*shape):
    return jax.ShapeDtypeStruct(shape, jnp.bfloat16)


def tiles(hidden):
    tile = tile_of(hidden)
    return [slice(t, t + tile) for t in range(0, hidden, tile)]


def by_section(sel_ref, section, work, own, other):
    @pl.when(sel_ref[0] == section)
    def _():
        work(*own)

    @pl.when(sel_ref[0] != section)
    def _():
        work(*other)


def share_body(group, sel_ref, weight, out):
    rows = out.shape[0]
    start = pl.multiple_of((sel_ref[3] % group) * rows, rows)
    out[...] = weight[pl.ds(start, rows), :]


def share(weight, group, sel, after):
    rows, hidden = weight.shape
    body = functools.partial(share_body, group)
    return run(body, "share", sel, [weight], [bf16(rows // group, hidden)], [], after)


def relay_body(sel_ref, value, out):
    out[...] = value[...]


def relayed(value, sel, after):
    return run(relay_body, "relay", sel, [value], [bf16(*value.shape)], [], after)


def join_body(sel_ref, *refs):
    rows = refs[0].shape[0]
    for i, piece in enumerate(refs[:-1]):
        refs[-1][i * rows : (i + 1) * rows, :] = piece[...]


def joined_rows(pieces, sel):
    out = bf16(sum(piece.shape[0] for piece in pieces), pieces[0].shape[1])
    return run(join_body, "join", sel, pieces, [out], [], (), 1)


def stack_body(sel_ref, *refs):
    for i, piece in enumerate(refs[:-1]):
        refs[-1][i] = piece[...]


def assemble_body(count, sel_ref, *refs):
    pieces, beside, out = refs[:count], refs[count], refs[count + 1]
    rows = pieces[0].shape[0]
    for i, piece in enumerate(pieces):
        for q, value in ((2 * i, piece[...]), (2 * i + 1, beside[i])):
            place = (sel_ref[3] % (2 * count)) ^ q
            out[pl.ds(pl.multiple_of(place * rows, rows), rows), :] = value


def assembled(pieces, sel, after, cost=COST):
    rows, hidden = pieces[0].shape
    count = len(pieces)
    out = bf16(count, rows, hidden)
    stacked, token = run(stack_body, "stack", sel, pieces, [out], [], after, cost)
    beside = swapped(stacked, "dp", 1)
    body = functools.partial(assemble_body, count)
    out = bf16(2 * count * rows, hidden)
    whole, done = run(body, "assemble", sel, [*pieces, beside], [out], [], (), cost)
    return whole, token, done


def partial_body(count, sel_ref, *refs):
    parts, (gain, w_in, w_out) = refs[:count], refs[count : count + 3]
    stay, leave, xn, acc = refs[count + 3 :]
    rows = parts[0].shape[0]
    late = rows // 2
    for i, part in enumerate(parts):
        xn[i * rows : (i + 1) * rows, :] = normed(part[...].astype(jnp.float32), gain[...])
    for t, tile in enumerate(tiles(w_in.shape[1])):
        act, unused = gelu_pair(dot_nn(xn[...], w_in[:, tile]))
        term = dot_nt(act.astype(jnp.bfloat16), w_out[:, tile])
        acc[...] = term if t == 0 else acc[...] + term
    for i in range(count):
        start = i * rows
        leave[i] = acc[start : start + late, :].astype(jnp.bfloat16)
        stay[i] = acc[start + late : start + rows, :].astype(jnp.bfloat16)


def block0_partials(parts, gain, w_in, w_out, sel, after):
    rows, width = parts[0].shape
    hidden, n = w_in.shape[1], len(parts)
    return run(
        functools.partial(partial_body, n),
        "block0_partial",
        sel,
        [*parts, gain, w_in, w_out],
        [bf16(n, rows // 2, width)] * 2,
        [
            pltpu.VMEM((n * rows, width), jnp.bfloat16),
            pltpu.VMEM((n * rows, width), jnp.float32),
        ],
        after,
    )


def pick_body(count, sel_ref, *refs):
    stay, crossed = refs[:2]
    arrived, outs = refs[2 : 2 + count], refs[2 + count :]
    for i, out in enumerate(outs):
        value = jnp.where(sel_ref[0] == 0, stay[i], crossed[i])
        if count and i == 0:
            value = value.astype(jnp.float32)
            for part in arrived:
                value = value + part[...].astype(jnp.float32)
        out[...] = value


def picked(stay, crossed, arrived, sel):
    count, rows, width = stay.shape
    outs = [bf16(rows, width)] * count
    if arrived:
        outs[0] = jax.ShapeDtypeStruct((rows, width), jnp.float32)
    body = functools.partial(pick_body, len(arrived))
    *chosen, token = run(body, "pick", sel, [stay, crossed, *arrived], outs, [])
    return chosen, token


def denoise_body(tokens, count, sel_ref, *refs):
    latents, sigma, alpha = refs[:3]
    sums, out = refs[3 : 3 + count], refs[3 + count]
    late = out.shape[0]
    base = latents[pl.ds(pl.multiple_of((1 - sel_ref[0]) * late, late), late), :]
    base = base.astype(jnp.float32)
    eps = base
    for part in sums:
        eps = eps + part[...].astype(jnp.float32)
    out[...] = ((base - sigma[...] * eps) / alpha[...]).astype(jnp.bfloat16)


def denoised(latents, sigma, alpha, sums, tokens, sel, after):
    return run(
        functools.partial(denoise_body, tokens, len(sums)),
        "denoise",
        sel,
        [latents, sigma, alpha, *sums],
        [bf16(latents.shape[0] // 2, latents.shape[1])],
        [],
        after,
    )[:2]


def crossing(count):
    near = [k for k in range(1, count) if 2 * k != count]
    return [0] + near + [k for k in range(1, count) if 2 * k == count]


def state_body(count, sel_ref, *refs):
    parts = refs[:count]
    gain, own, other, act, slope, xn_cols, xn = refs[count:]
    rows = parts[0].shape[0]
    late = rows // 2
    share = xn_cols.shape[0]
    mine = pl.multiple_of((1 - sel_ref[0]) * late, late)
    theirs = pl.multiple_of(sel_ref[0] * late, late)
    at = 0
    for start, order in ((mine, range(len(parts))), (theirs, crossing(len(parts)))):
        for k in order:
            rows_k = parts[k][pl.ds(start, late), :].astype(jnp.float32)
            xn[at : at + late, :] = normed(rows_k, gain[...])
            at += late
    cols = xn[:, pl.ds(pl.multiple_of(sel_ref[0] * share, share), share)]
    xn_cols[...] = cols.T

    def work(weight):
        for tile in tiles(weight.shape[1]):
            value, grad = gelu_pair(dot_nn(xn[...], weight[:, tile]))
            act[:, tile] = value.astype(jnp.bfloat16)
            slope[:, tile] = grad.astype(jnp.bfloat16)

    by_section(sel_ref, 0, work, (own,), (other,))


def block0_state(parts, gain, own, other, sel, after):
    total, width = sum(part.shape[0] for part in parts), parts[0].shape[1]
    hidden = own.shape[1]
    return run(
        functools.partial(state_body, len(parts)),
        "block0_state",
        sel,
        [*parts, gain, own, other],
        [bf16(total, hidden), bf16(total, hidden), bf16(width // 2, total)],
        [pltpu.VMEM((total, width), jnp.bfloat16)],
        after,
    )


def reward_body(count, tokens, sel_ref, *refs):
    parts, (gain, text) = refs[:count], refs[count : count + 2]
    own_in, own_out, other_in, other_out = refs[count + 2 : count + 6]
    slopes, (pool, xn) = refs[count + 6 : 2 * count + 6], refs[2 * count + 6 :]
    rows = parts[0].shape[0]
    half = rows // tokens
    row = lax.broadcasted_iota(jnp.int32, pool.shape, 0)
    start = jnp.zeros(pool.shape, jnp.float32)
    for image in range(half):
        own_rows = parts[0][image * tokens : (image + 1) * tokens, :].astype(jnp.float32)
        start = jnp.where(row == image, jnp.mean(own_rows, axis=0, keepdims=True), start)
        start = jnp.where(row == count * half + image, text[image : image + 1, :], start)
    pool[...] = start
    for i, part in enumerate(parts):
        xn[i * rows : (i + 1) * rows, :] = normed(part[...].astype(jnp.float32), gain[...])

    def work(w_in, w_out):
        for tile in tiles(w_in.shape[1]):
            act, grad = gelu_pair(dot_nn(xn[...], w_in[:, tile]))
            for i in range(count):
                slopes[i][:, tile] = grad[i * rows : (i + 1) * rows, :].astype(jnp.bfloat16)
            means = [
                jnp.mean(act[at : at + tokens, :], axis=0, keepdims=True)
                for at in range(0, count * rows, tokens)
            ]
            place = lax.broadcasted_iota(jnp.int32, (pool.shape[0], act.shape[1]), 0)
            stacked = jnp.zeros(place.shape, jnp.float32)
            for i, mean in enumerate(means):
                stacked = jnp.where(place == i, mean, stacked)
            pool[...] += dot_nt(stacked.astype(jnp.bfloat16), w_out[:, tile])

    by_section(sel_ref, 1, work, (own_in, own_out), (other_in, other_out))


def reward_forward(parts, tokens, gain, text, own, other, sel, after):
    rows, width = parts[0].shape
    hidden, n = own[0].shape[1], len(parts)
    images = (n + 1) * rows // tokens
    outs = run(
        functools.partial(reward_body, n, tokens),
        "reward_forward",
        sel,
        [*parts, gain, text, *own, *other],
        [bf16(rows, hidden)] * n
        + [jax.ShapeDtypeStruct((-(-images // 8) * 8, width), jnp.float32)],
        [pltpu.VMEM((n * rows, width), jnp.bfloat16)],
        after,
    )
    return outs[:n], outs[n]


def score_gradient(pooled, text):
    unit = text * lax.rsqrt(jnp.mean(text * text, axis=-1, keepdims=True) + EPS)
    scale = lax.rsqrt(jnp.mean(pooled * pooled, axis=-1, keepdims=True) + EPS)
    along = jnp.mean(pooled * unit, axis=-1, keepdims=True)
    return (-100.0 / pooled.shape[-1]) * (scale * unit - pooled * scale**3 * along)


def back_body(count, tokens, sel_ref, *refs):
    pools, slopes = refs[:count], refs[count : 2 * count]
    own_in, own_out, other_in, other_out = refs[2 * count : 2 * count + 4]
    outs = refs[2 * count + 4 : 3 * count + 4]
    g_mean, acc = refs[3 * count + 4 :]
    rows = slopes[0].shape[0]
    half = rows // tokens
    images = count * half
    pooled, texts = [], []
    for j in range(images):
        at = [(j - k * half) % images for k in range(count)]
        pooled.append(sum(pools[k][at[k] : at[k] + 1, :] for k in range(count)))
        text = images + j % half
        texts.append(pools[j // half][text : text + 1, :])
    padded = -(-images // 16) * 16
    row = lax.broadcasted_iota(jnp.int32, (padded, acc.shape[1]), 0)
    stacked, spoken = jnp.zeros(row.shape, jnp.float32), jnp.zeros(row.shape, jnp.float32)
    for j in range(images):
        stacked = jnp.where(row == j, pooled[j], stacked)
        spoken = jnp.where(row == j, texts[j], spoken)
    g_all = score_gradient(stacked, spoken) * (1.0 / tokens)
    g_mean[...] = g_all[: g_mean.shape[0], :]
    g_tok = g_all.astype(jnp.bfloat16)

    def work(w_in, w_out):
        for t, tile in enumerate(tiles(w_in.shape[1])):
            g_h = dot_nn(g_tok, w_out[:, tile])
            terms = []
            for i in range(count):
                for image in range(half):
                    at = i * half + image
                    slope = slopes[i][image * tokens : (image + 1) * tokens, tile]
                    terms.append(
                        (slope.astype(jnp.float32) * g_h[at : at + 1, :]).astype(jnp.bfloat16)
                    )
            term = dot_nt(jnp.concatenate(terms, axis=0), w_in[:, tile])
            acc[...] = term if t == 0 else acc[...] + term

    by_section(sel_ref, 1, work, (own_in, own_out), (other_in, other_out))
    for i, out in enumerate(outs):
        out[...] = acc[i * rows : (i + 1) * rows, :].astype(jnp.bfloat16)


def reward_back(pools, slopes, tokens, own, other, sel):
    rows, hidden = slopes[0].shape
    width, n = own[0].shape[0], len(slopes)
    outs = run(
        functools.partial(back_body, n, tokens),
        "reward_back",
        sel,
        [*pools, *slopes, *own, *other],
        [bf16(rows, width)] * n + [jax.ShapeDtypeStruct((8, width), jnp.float32)],
        [pltpu.VMEM((n * rows, width), jnp.float32)],
    )
    return outs[:n], outs[n]


def eps_gradient_body(tokens, count, sel_ref, *refs):
    seen_ref, g_mean, gain, ratio = refs[:4]
    sums, out = refs[4 : 4 + count], refs[4 + count]
    g_xn = sums[0][...].astype(jnp.float32)
    for part in sums[1:]:
        g_xn = g_xn + part[...].astype(jnp.float32)
    seen = seen_ref[...].astype(jnp.float32)
    scale = lax.rsqrt(jnp.mean(seen * seen, axis=-1, keepdims=True) + EPS)
    weighted = gain[...] * g_xn
    along = jnp.mean(seen * weighted, axis=-1, keepdims=True)
    g_norm = scale * weighted - seen * scale**3 * along
    for image in range(out.shape[0] // tokens):
        at = slice(image * tokens, (image + 1) * tokens)
        g_images = (g_mean[image : image + 1, :] + g_norm[at, :]).astype(jnp.bfloat16)
        out[at, :] = (ratio[at, :] * g_images.astype(jnp.float32)).astype(jnp.bfloat16)


def eps_gradient(seen, g_mean, gain, ratio, sums, tokens, sel, after):
    return run(
        functools.partial(eps_gradient_body, tokens, len(sums)),
        "eps_gradient",
        sel,
        [seen, g_mean, gain, ratio, *sums],
        [bf16(*seen.shape)],
        [],
        after,
    )


def put_rows(result, core, keep, away, tile):
    groups, rows, unused = keep.shape
    for g in range(groups):
        even = result[2 * g * rows : (2 * g + 1) * rows, :]
        odd = result[(2 * g + 1) * rows : (2 * g + 2) * rows, :]
        keep[g, :, tile] = jnp.where(core == 0, even, odd).astype(jnp.bfloat16)
        away[g, :, tile] = jnp.where(core == 0, odd, even).astype(jnp.bfloat16)


def gradient_body(count, sel_ref, *refs):
    pieces = refs[:count]
    act, slope, xn_cols, own, other = refs[count : count + 5]
    out_keep, out_away, in_keep, in_away, g_all, turned = refs[count + 5 :]
    share = turned.shape[0]
    core = sel_ref[1]
    at = 0
    for piece in pieces:
        g_all[at : at + piece.shape[0], :] = piece[...]
        at += piece.shape[0]
    cols = g_all[:, pl.ds(pl.multiple_of(sel_ref[0] * share, share), share)]
    turned[...] = cols.T

    def work(weight):
        for tile in tiles(weight.shape[1]):
            put_rows(dot_nn(turned[...], act[:, tile]), core, out_keep, out_away, tile)
            g_h = dot_nn(g_all[...], weight[:, tile])
            g_hidden = (g_h * slope[:, tile].astype(jnp.float32)).astype(jnp.bfloat16)
            put_rows(dot_nn(xn_cols[...], g_hidden), core, in_keep, in_away, tile)

    by_section(sel_ref, 0, work, (own,), (other,))


def gradients(pieces, states, own, other, sel):
    total, width = sum(piece.shape[0] for piece in pieces), pieces[0].shape[1]
    hidden = own.shape[1]
    groups = lax.axis_size("dp") // 2
    outs = run(
        functools.partial(gradient_body, len(pieces)),
        "gradients",
        sel,
        [*pieces, *states, own, other],
        [bf16(groups, width // 2 // (2 * groups), hidden)] * 4,
        [
            pltpu.VMEM((total, width), jnp.bfloat16),
            pltpu.VMEM((width // 2, total), jnp.bfloat16),
        ],
    )
    return outs[:2], outs[2:4]


def chip_body(sel_ref, keep, arrived, mine, others):
    groups = keep.shape[0]
    for k in range(groups):
        at = (sel_ref[2] + k) % groups
        total = keep[at].astype(jnp.float32) + arrived[at].astype(jnp.float32)
        if k == 0:
            mine[...] = total
        else:
            others[k - 1] = total.astype(jnp.bfloat16)


def sum_over_dp(keep, away, sel):
    groups, rows, hidden = keep.shape
    total, others, unused = run(
        chip_body,
        "chip_sum",
        sel,
        [keep, swapped(away, "dp", 1)],
        [jax.ShapeDtypeStruct((rows, hidden), jnp.float32), bf16(groups - 1, rows, hidden)],
        [],
    )
    for k in range(1, groups):
        total = total + rotated(others[k - 1], "dp", 2 * k).astype(jnp.float32)
    return total


def on_device(latents, timesteps, prompt_ids, prompt_table, gains, w_in, w_out):
    count, tokens, width = latents.shape
    half = count // 2
    n_tp = lax.axis_size("tp")
    segment = lax.axis_index("sec")
    first = segment == 0
    dp = lax.axis_index("dp")
    sel = jnp.stack([segment, dp % 2, dp // 2, dp % 4]).astype(jnp.int32)
    own = (w_in[0], w_out[0])

    def my_half(value):
        return jnp.where(first, value[half:], value[:half])

    theta = math.pi / 2.0 * (my_half(timesteps).astype(jnp.float32) + 1.0) / (STEPS + 1.0)
    theta = jnp.repeat(theta, tokens)[:, None]
    alpha, sigma = jnp.cos(theta), jnp.sin(theta)

    flat = latents.reshape(count * tokens, width)
    near = [k for k in range(1, n_tp) if 2 * k != n_tp]
    rest = [0] + [k for k in range(1, n_tp) if 2 * k == n_tp]
    lat_parts = [flat] + [None] * (n_tp - 1)
    for k in near:
        lat_parts[k] = rotated(flat, "tp", k)
    again, near_token = relayed(flat, sel, [lat_parts[k] for k in near])
    for k in rest[1:]:
        lat_parts[k] = rotated(again, "tp", k)
    got_in = swapped(share(own[0], 4, sel, ())[0], "sec", 1)
    got_again, in_token = relayed(got_in, sel, [near_token])
    across_in = swapped(got_again, "dp", 2)
    out_share, out_token = share(own[1], 2, sel, [near_token])
    got_out = lax.ppermute(out_share, "sec", [(1, 0)])

    onehot = (
        my_half(prompt_ids)[:, None] == jnp.arange(prompt_table.shape[0], dtype=jnp.int32)[None, :]
    ).astype(jnp.bfloat16)
    text_mine = dot_nn(onehot, prompt_table)

    sums, before = [], [in_token]
    for ks in (near, rest):
        if ks:
            stay, leave, partial_token = block0_partials(
                [lat_parts[k] for k in ks], gains[:1], *own, sel, before
            )
            crossed = lax.ppermute(leave, "sec", [(0, 1)])
            chosen, picked_token = picked(stay, crossed, sums if ks is rest else [], sel)
            if ks is rest:
                sums = [chosen[0]] + [rotated(part, "tp", -k) for k, part in zip(ks[1:], chosen[1:])]
            else:
                sums = [rotated(part, "tp", -k) for k, part in zip(ks, chosen)]
                before = [partial_token, out_token]
    other_in, unused, in_token = assembled([got_in, across_in], sel, [partial_token])
    other_out, out_token, joined_token = assembled([got_out], sel, [in_token], COST)
    other = (other_in, other_out)
    mine_rows, unused = denoised(flat, sigma, alpha, sums, tokens, sel, [in_token, out_token])

    seen_parts = gather_parts(mine_rows)
    late_share, late_token = share(own[1], 2, sel, [joined_token])
    got_late = lax.ppermute(late_share, "sec", [(0, 1)])
    slopes1, pool = reward_forward(
        seen_parts, tokens, gains[1:], text_mine, own, other, sel, ()
    )
    pools = gather_parts(pool)
    g_parts, g_mean = reward_back(pools, slopes1, tokens, own, other, sel)

    *states, state_token = block0_state(
        lat_parts, gains[:1], own[0], other[0], sel, g_parts[:1]
    )

    g_sums = [g_parts[0]] + [rotated(g_parts[k], "tp", -k) for k in range(1, n_tp)]
    ratio = -(sigma / alpha)
    g_eps, eps_token = eps_gradient(
        mine_rows, g_mean, gains[1:], ratio, g_sums, tokens, sel, [state_token]
    )


    g_mine = gather_parts(g_eps)
    pieces = g_mine + [swapped(g_eps, "sec", 1)]
    arrived = [pieces[-1]]
    for ks in (near, rest[1:]):
        if ks:
            joined, token = joined_rows([g_mine[k] for k in ks], sel)
            pieces.append(swapped(joined, "sec", 1))
            arrived += [pieces[-1]] if ks is near else [token]
    late_out = assembled([got_late], sel, arrived, 1)[0]
    out_parts, in_parts = gradients(pieces, states, own[1], late_out, sel)
    grad_out, grad_in = sum_over_dp(*out_parts, sel), sum_over_dp(*in_parts, sel)
    return (grad_in, grad_out)


def solution(mesh):
    in_specs = (
        P(("dp", "tp"), None, None),
        P(("dp", "tp")),
        P(("dp", "tp")),
        P(),
        P(),
        P("sec", None, "tp"),
        P("sec", None, "tp"),
    )
    out_specs = (P(("sec", "dp"), "tp"), P(("sec", "dp"), "tp"))
    return jax.shard_map(
        on_device, mesh=mesh, in_specs=in_specs, out_specs=out_specs, check_vma=False
    )
```

```python
import functools
import math

import jax
import jax.numpy as jnp
from jax import lax
from jax.experimental import pallas as pl
from jax.experimental.pallas import tpu as pltpu
from jax.sharding import PartitionSpec as P

STEPS = 50


EPS = 1e-06
VMEM_BYTES = 8 * 1024 * 1024
COST = 10**11


def rotated(value, axis, steps):
    count = lax.axis_size(axis)
    return lax.ppermute(value, axis, [(i, (i + steps) % count) for i in range(count)])


def swapped(value, axis, bit):
    count = lax.axis_size(axis)
    return lax.ppermute(value, axis, [(i, i ^ bit) for i in range(count)])


def gather_parts(piece):
    return [piece] + [rotated(piece, "tp", k) for k in range(1, lax.axis_size("tp"))]


def gelu_pair(value):
    cdf = 0.5 * (1.0 + lax.erf(value * (1.0 / math.sqrt(2.0))))
    density = jnp.exp(-0.5 * value * value) * (1.0 / math.sqrt(2.0 * math.pi))
    return (value * cdf, cdf + value * density)


def normed(rows, gain):
    scale = lax.rsqrt(jnp.mean(rows * rows, axis=-1, keepdims=True) + EPS)
    return (rows * scale * gain).astype(jnp.bfloat16)


def dot_nn(a, b):
    return jnp.dot(a, b, preferred_element_type=jnp.float32)


def dot_nt(a, b):
    return lax.dot_general(a, b, (((1,), (1,)), ((), ())), preferred_element_type=jnp.float32)


def tile_of(hidden):
    for tile in (256, 128):
        if hidden % tile == 0:
            return tile
    return hidden


IN_VMEM = pl.BlockSpec(memory_space=pltpu.VMEM)
IN_SMEM = pl.BlockSpec(memory_space=pltpu.SMEM)


TOKEN = jax.ShapeDtypeStruct((8, 128), jnp.float32)


def run(body, name, sel, operands, outs, scratch, after=(), cost=COST):
    used, last = 1 + len(operands), 1 + len(operands) + len(after) + len(outs)

    def with_token(*refs):
        refs[last][...] = jnp.zeros(TOKEN.shape, TOKEN.dtype)
        body(*refs[:used], *refs[used + len(after) : last], *refs[last + 1 :])

    held = [math.prod(x.shape) * jnp.dtype(x.dtype).itemsize for x in scratch]
    return pl.pallas_call(
        with_token,
        in_specs=[IN_SMEM] + [IN_VMEM] * (len(operands) + len(after)),
        out_specs=[IN_VMEM] * (len(outs) + 1),
        scratch_shapes=scratch,
        out_shape=[*outs, TOKEN],
        compiler_params=pltpu.CompilerParams(vmem_limit_bytes=max(VMEM_BYTES, 4 * sum(held))),
        cost_estimate=pl.CostEstimate(
            flops=cost, bytes_accessed=cost // 200, transcendentals=0
        ),
        name=name,
    )(sel, *operands, *after)


def bf16(*shape):
    return jax.ShapeDtypeStruct(shape, jnp.bfloat16)


def tiles(hidden):
    tile = tile_of(hidden)
    return [slice(t, t + tile) for t in range(0, hidden, tile)]


def by_section(sel_ref, section, work, own, other):
    @pl.when(sel_ref[0] == section)
    def _():
        work(*own)

    @pl.when(sel_ref[0] != section)
    def _():
        work(*other)


def share_body(group, sel_ref, weight, out):
    rows = out.shape[0]
    start = pl.multiple_of((sel_ref[3] % group) * rows, rows)
    out[...] = weight[pl.ds(start, rows), :]


def share(weight, group, sel, after):
    rows, hidden = weight.shape
    body = functools.partial(share_body, group)
    return run(body, "share", sel, [weight], [bf16(rows // group, hidden)], [], after)


def relay_body(sel_ref, value, out):
    out[...] = value[...]


def relayed(value, sel, after):
    return run(relay_body, "relay", sel, [value], [bf16(*value.shape)], [], after)


def join_body(sel_ref, *refs):
    rows = refs[0].shape[0]
    for i, piece in enumerate(refs[:-1]):
        refs[-1][i * rows : (i + 1) * rows, :] = piece[...]


def joined_rows(pieces, sel):
    out = bf16(sum(piece.shape[0] for piece in pieces), pieces[0].shape[1])
    return run(join_body, "join", sel, pieces, [out], [], (), 1)


def stack_body(sel_ref, *refs):
    for i, piece in enumerate(refs[:-1]):
        refs[-1][i] = piece[...]


def assemble_body(count, sel_ref, *refs):
    pieces, beside, out = refs[:count], refs[count], refs[count + 1]
    rows = pieces[0].shape[0]
    for i, piece in enumerate(pieces):
        for q, value in ((2 * i, piece[...]), (2 * i + 1, beside[i])):
            place = (sel_ref[3] % (2 * count)) ^ q
            out[pl.ds(pl.multiple_of(place * rows, rows), rows), :] = value


def assembled(pieces, sel, after, cost=COST):
    rows, hidden = pieces[0].shape
    count = len(pieces)
    out = bf16(count, rows, hidden)
    stacked, token = run(stack_body, "stack", sel, pieces, [out], [], after, cost)
    beside = swapped(stacked, "dp", 1)
    body = functools.partial(assemble_body, count)
    out = bf16(2 * count * rows, hidden)
    whole, done = run(body, "assemble", sel, [*pieces, beside], [out], [], (), cost)
    return whole, token, done


def partial_body(count, sel_ref, *refs):
    parts, (gain, w_in, w_out) = refs[:count], refs[count : count + 3]
    stay, leave, xn, acc = refs[count + 3 :]
    rows = parts[0].shape[0]
    late = rows // 2
    for i, part in enumerate(parts):
        xn[i * rows : (i + 1) * rows, :] = normed(part[...].astype(jnp.float32), gain[...])
    for t, tile in enumerate(tiles(w_in.shape[1])):
        act, unused = gelu_pair(dot_nn(xn[...], w_in[:, tile]))
        term = dot_nt(act.astype(jnp.bfloat16), w_out[:, tile])
        acc[...] = term if t == 0 else acc[...] + term
    for i in range(count):
        start = i * rows
        leave[i] = acc[start : start + late, :].astype(jnp.bfloat16)
        stay[i] = acc[start + late : start + rows, :].astype(jnp.bfloat16)


def block0_partials(parts, gain, w_in, w_out, sel, after, cost):
    rows, width = parts[0].shape
    hidden, n = w_in.shape[1], len(parts)
    return run(
        functools.partial(partial_body, n),
        "block0_partial",
        sel,
        [*parts, gain, w_in, w_out],
        [bf16(n, rows // 2, width)] * 2,
        [
            pltpu.VMEM((n * rows, width), jnp.bfloat16),
            pltpu.VMEM((n * rows, width), jnp.float32),
        ],
        after,
        cost,
    )


def pick_body(count, sel_ref, *refs):
    stay, crossed = refs[:2]
    arrived, outs = refs[2 : 2 + count], refs[2 + count :]
    for i, out in enumerate(outs):
        value = jnp.where(sel_ref[0] == 0, stay[i], crossed[i])
        if count and i == 0:
            value = value.astype(jnp.float32)
            for part in arrived:
                value = value + part[...].astype(jnp.float32)
        out[...] = value


def picked(stay, crossed, arrived, sel, after):
    count, rows, width = stay.shape
    outs = [bf16(rows, width)] * count
    if arrived:
        outs[0] = jax.ShapeDtypeStruct((rows, width), jnp.float32)
    body = functools.partial(pick_body, len(arrived))
    *chosen, token = run(body, "pick", sel, [stay, crossed, *arrived], outs, [], after)
    return chosen, token


def denoise_body(tokens, count, sel_ref, *refs):
    latents, sigma, alpha = refs[:3]
    sums, out = refs[3 : 3 + count], refs[3 + count]
    late = out.shape[0]
    base = latents[pl.ds(pl.multiple_of((1 - sel_ref[0]) * late, late), late), :]
    base = base.astype(jnp.float32)
    eps = base
    for part in sums:
        eps = eps + part[...].astype(jnp.float32)
    out[...] = ((base - sigma[...] * eps) / alpha[...]).astype(jnp.bfloat16)


def denoised(latents, sigma, alpha, sums, tokens, sel, after):
    return run(
        functools.partial(denoise_body, tokens, len(sums)),
        "denoise",
        sel,
        [latents, sigma, alpha, *sums],
        [bf16(latents.shape[0] // 2, latents.shape[1])],
        [],
        after,
    )[:2]


def crossing(count):
    near = [k for k in range(1, count) if 2 * k != count]
    return [0] + near + [k for k in range(1, count) if 2 * k == count]


def state_body(count, sel_ref, *refs):
    parts = refs[:count]
    gain, own, other, act, slope, xn_cols, xn = refs[count:]
    rows = parts[0].shape[0]
    late = rows // 2
    share = xn_cols.shape[0]
    mine = pl.multiple_of((1 - sel_ref[0]) * late, late)
    theirs = pl.multiple_of(sel_ref[0] * late, late)
    at = 0
    for start, order in ((mine, range(len(parts))), (theirs, crossing(len(parts)))):
        for k in order:
            rows_k = parts[k][pl.ds(start, late), :].astype(jnp.float32)
            xn[at : at + late, :] = normed(rows_k, gain[...])
            at += late
    cols = xn[:, pl.ds(pl.multiple_of(sel_ref[0] * share, share), share)]
    xn_cols[...] = cols.T

    def work(weight):
        for tile in tiles(weight.shape[1]):
            value, grad = gelu_pair(dot_nn(xn[...], weight[:, tile]))
            act[:, tile] = value.astype(jnp.bfloat16)
            slope[:, tile] = grad.astype(jnp.bfloat16)

    by_section(sel_ref, 0, work, (own,), (other,))


def block0_state(parts, gain, own, other, sel, after):
    total, width = sum(part.shape[0] for part in parts), parts[0].shape[1]
    hidden = own.shape[1]
    return run(
        functools.partial(state_body, len(parts)),
        "block0_state",
        sel,
        [*parts, gain, own, other],
        [bf16(total, hidden), bf16(total, hidden), bf16(width // 2, total)],
        [pltpu.VMEM((total, width), jnp.bfloat16)],
        after,
    )


def reward_body(count, tokens, sel_ref, *refs):
    parts, (gain, text) = refs[:count], refs[count : count + 2]
    own_in, own_out, other_in, other_out = refs[count + 2 : count + 6]
    slopes, (pool, xn) = refs[count + 6 : 2 * count + 6], refs[2 * count + 6 :]
    rows = parts[0].shape[0]
    half = rows // tokens
    row = lax.broadcasted_iota(jnp.int32, pool.shape, 0)
    start = jnp.zeros(pool.shape, jnp.float32)
    for image in range(half):
        own_rows = parts[0][image * tokens : (image + 1) * tokens, :].astype(jnp.float32)
        start = jnp.where(row == image, jnp.mean(own_rows, axis=0, keepdims=True), start)
        start = jnp.where(row == count * half + image, text[image : image + 1, :], start)
    pool[...] = start
    for i, part in enumerate(parts):
        xn[i * rows : (i + 1) * rows, :] = normed(part[...].astype(jnp.float32), gain[...])

    def work(w_in, w_out):
        for tile in tiles(w_in.shape[1]):
            act, grad = gelu_pair(dot_nn(xn[...], w_in[:, tile]))
            for i in range(count):
                slopes[i][:, tile] = grad[i * rows : (i + 1) * rows, :].astype(jnp.bfloat16)
            means = [
                jnp.mean(act[at : at + tokens, :], axis=0, keepdims=True)
                for at in range(0, count * rows, tokens)
            ]
            place = lax.broadcasted_iota(jnp.int32, (pool.shape[0], act.shape[1]), 0)
            stacked = jnp.zeros(place.shape, jnp.float32)
            for i, mean in enumerate(means):
                stacked = jnp.where(place == i, mean, stacked)
            pool[...] += dot_nt(stacked.astype(jnp.bfloat16), w_out[:, tile])

    by_section(sel_ref, 1, work, (own_in, own_out), (other_in, other_out))


def reward_forward(parts, tokens, gain, text, own, other, sel, after):
    rows, width = parts[0].shape
    hidden, n = own[0].shape[1], len(parts)
    images = (n + 1) * rows // tokens
    outs = run(
        functools.partial(reward_body, n, tokens),
        "reward_forward",
        sel,
        [*parts, gain, text, *own, *other],
        [bf16(rows, hidden)] * n
        + [jax.ShapeDtypeStruct((-(-images // 8) * 8, width), jnp.float32)],
        [pltpu.VMEM((n * rows, width), jnp.bfloat16)],
        after,
    )
    return outs[:n], outs[n]


def score_gradient(pooled, text):
    unit = text * lax.rsqrt(jnp.mean(text * text, axis=-1, keepdims=True) + EPS)
    scale = lax.rsqrt(jnp.mean(pooled * pooled, axis=-1, keepdims=True) + EPS)
    along = jnp.mean(pooled * unit, axis=-1, keepdims=True)
    return (-100.0 / pooled.shape[-1]) * (scale * unit - pooled * scale**3 * along)


def back_body(count, tokens, sel_ref, *refs):
    pools, slopes = refs[:count], refs[count : 2 * count]
    own_in, own_out, other_in, other_out = refs[2 * count : 2 * count + 4]
    outs = refs[2 * count + 4 : 3 * count + 4]
    g_mean, acc = refs[3 * count + 4 :]
    rows = slopes[0].shape[0]
    half = rows // tokens
    images = count * half
    pooled, texts = [], []
    for j in range(images):
        at = [(j - k * half) % images for k in range(count)]
        pooled.append(sum(pools[k][at[k] : at[k] + 1, :] for k in range(count)))
        text = images + j % half
        texts.append(pools[j // half][text : text + 1, :])
    padded = -(-images // 16) * 16
    row = lax.broadcasted_iota(jnp.int32, (padded, acc.shape[1]), 0)
    stacked, spoken = jnp.zeros(row.shape, jnp.float32), jnp.zeros(row.shape, jnp.float32)
    for j in range(images):
        stacked = jnp.where(row == j, pooled[j], stacked)
        spoken = jnp.where(row == j, texts[j], spoken)
    g_all = score_gradient(stacked, spoken) * (1.0 / tokens)
    g_mean[...] = g_all[: g_mean.shape[0], :]
    g_tok = g_all.astype(jnp.bfloat16)

    def work(w_in, w_out):
        for t, tile in enumerate(tiles(w_in.shape[1])):
            g_h = dot_nn(g_tok, w_out[:, tile])
            terms = []
            for i in range(count):
                for image in range(half):
                    at = i * half + image
                    slope = slopes[i][image * tokens : (image + 1) * tokens, tile]
                    terms.append(
                        (slope.astype(jnp.float32) * g_h[at : at + 1, :]).astype(jnp.bfloat16)
                    )
            term = dot_nt(jnp.concatenate(terms, axis=0), w_in[:, tile])
            acc[...] = term if t == 0 else acc[...] + term

    by_section(sel_ref, 1, work, (own_in, own_out), (other_in, other_out))
    for i, out in enumerate(outs):
        out[...] = acc[i * rows : (i + 1) * rows, :].astype(jnp.bfloat16)


def reward_back(pools, slopes, tokens, own, other, sel):
    rows, hidden = slopes[0].shape
    width, n = own[0].shape[0], len(slopes)
    outs = run(
        functools.partial(back_body, n, tokens),
        "reward_back",
        sel,
        [*pools, *slopes, *own, *other],
        [bf16(rows, width)] * n + [jax.ShapeDtypeStruct((8, width), jnp.float32)],
        [pltpu.VMEM((n * rows, width), jnp.float32)],
    )
    return outs[:n], outs[n]


def eps_gradient_body(tokens, count, sel_ref, *refs):
    seen_ref, g_mean, gain, ratio = refs[:4]
    sums, out = refs[4 : 4 + count], refs[4 + count]
    g_xn = sums[0][...].astype(jnp.float32)
    for part in sums[1:]:
        g_xn = g_xn + part[...].astype(jnp.float32)
    seen = seen_ref[...].astype(jnp.float32)
    scale = lax.rsqrt(jnp.mean(seen * seen, axis=-1, keepdims=True) + EPS)
    weighted = gain[...] * g_xn
    along = jnp.mean(seen * weighted, axis=-1, keepdims=True)
    g_norm = scale * weighted - seen * scale**3 * along
    for image in range(out.shape[0] // tokens):
        at = slice(image * tokens, (image + 1) * tokens)
        g_images = (g_mean[image : image + 1, :] + g_norm[at, :]).astype(jnp.bfloat16)
        out[at, :] = (ratio[at, :] * g_images.astype(jnp.float32)).astype(jnp.bfloat16)


def eps_gradient(seen, g_mean, gain, ratio, sums, tokens, sel, after):
    return run(
        functools.partial(eps_gradient_body, tokens, len(sums)),
        "eps_gradient",
        sel,
        [seen, g_mean, gain, ratio, *sums],
        [bf16(*seen.shape)],
        [],
        after,
    )


def put_rows(result, core, keep, away, tile):
    groups, rows, unused = keep.shape
    for g in range(groups):
        even = result[2 * g * rows : (2 * g + 1) * rows, :]
        odd = result[(2 * g + 1) * rows : (2 * g + 2) * rows, :]
        keep[g, :, tile] = jnp.where(core == 0, even, odd).astype(jnp.bfloat16)
        away[g, :, tile] = jnp.where(core == 0, odd, even).astype(jnp.bfloat16)


def gradient_body(count, sel_ref, *refs):
    pieces = refs[:count]
    act, slope, xn_cols, own, other = refs[count : count + 5]
    out_keep, out_away, in_keep, in_away, g_all, turned = refs[count + 5 :]
    share = turned.shape[0]
    core = sel_ref[1]
    at = 0
    for piece in pieces:
        g_all[at : at + piece.shape[0], :] = piece[...]
        at += piece.shape[0]
    cols = g_all[:, pl.ds(pl.multiple_of(sel_ref[0] * share, share), share)]
    turned[...] = cols.T

    def work(weight):
        for tile in tiles(weight.shape[1]):
            put_rows(dot_nn(turned[...], act[:, tile]), core, out_keep, out_away, tile)
            g_h = dot_nn(g_all[...], weight[:, tile])
            g_hidden = (g_h * slope[:, tile].astype(jnp.float32)).astype(jnp.bfloat16)
            put_rows(dot_nn(xn_cols[...], g_hidden), core, in_keep, in_away, tile)

    by_section(sel_ref, 0, work, (own,), (other,))


def gradients(pieces, states, own, other, sel):
    total, width = sum(piece.shape[0] for piece in pieces), pieces[0].shape[1]
    hidden = own.shape[1]
    groups = lax.axis_size("dp") // 2
    outs = run(
        functools.partial(gradient_body, len(pieces)),
        "gradients",
        sel,
        [*pieces, *states, own, other],
        [bf16(groups, width // 2 // (2 * groups), hidden)] * 4,
        [
            pltpu.VMEM((total, width), jnp.bfloat16),
            pltpu.VMEM((width // 2, total), jnp.bfloat16),
        ],
    )
    return outs[:2], outs[2:4]


def chip_body(sel_ref, keep, arrived, mine, others):
    groups = keep.shape[0]
    for k in range(groups):
        at = (sel_ref[2] + k) % groups
        total = keep[at].astype(jnp.float32) + arrived[at].astype(jnp.float32)
        if k == 0:
            mine[...] = total
        else:
            others[k - 1] = total.astype(jnp.bfloat16)


def sum_over_dp(keep, away, sel):
    groups, rows, hidden = keep.shape
    total, others, unused = run(
        chip_body,
        "chip_sum",
        sel,
        [keep, swapped(away, "dp", 1)],
        [jax.ShapeDtypeStruct((rows, hidden), jnp.float32), bf16(groups - 1, rows, hidden)],
        [],
    )
    for k in range(1, groups):
        total = total + rotated(others[k - 1], "dp", 2 * k).astype(jnp.float32)
    return total


def on_device(latents, timesteps, prompt_ids, prompt_table, gains, w_in, w_out):
    count, tokens, width = latents.shape
    half = count // 2
    n_tp = lax.axis_size("tp")
    segment = lax.axis_index("sec")
    first = segment == 0
    dp = lax.axis_index("dp")
    sel = jnp.stack([segment, dp % 2, dp // 2, dp % 4]).astype(jnp.int32)
    own = (w_in[0], w_out[0])

    def my_half(value):
        return jnp.where(first, value[half:], value[:half])

    theta = math.pi / 2.0 * (my_half(timesteps).astype(jnp.float32) + 1.0) / (STEPS + 1.0)
    theta = jnp.repeat(theta, tokens)[:, None]
    alpha, sigma = jnp.cos(theta), jnp.sin(theta)

    flat = latents.reshape(count * tokens, width)
    near = [k for k in range(1, n_tp) if 2 * k != n_tp]
    rest = [0] + [k for k in range(1, n_tp) if 2 * k == n_tp]
    lat_parts = [flat] + [None] * (n_tp - 1)
    for k in near:
        lat_parts[k] = rotated(flat, "tp", k)
    again, near_token = relayed(flat, sel, [lat_parts[k] for k in near])
    for k in rest[1:]:
        lat_parts[k] = rotated(again, "tp", k)
    got_in = swapped(share(own[0], 4, sel, ())[0], "sec", 1)
    got_again, in_token = relayed(got_in, sel, [near_token])
    across_in = swapped(got_again, "dp", 2)
    out_share, out_token = share(own[1], 2, sel, [near_token])
    got_out = lax.ppermute(out_share, "sec", [(1, 0)])

    onehot = (
        my_half(prompt_ids)[:, None] == jnp.arange(prompt_table.shape[0], dtype=jnp.int32)[None, :]
    ).astype(jnp.bfloat16)
    text_mine = dot_nn(onehot, prompt_table)

    sums, before = [], [in_token]
    for ks in (near, rest):
        if ks:
            stay, leave, partial_token = block0_partials(
                [lat_parts[k] for k in ks], gains[:1], *own, sel, before, 1 if ks is rest else COST
            )
            crossed = lax.ppermute(leave, "sec", [(0, 1)])
            chosen, picked_token = picked(
                stay, crossed, sums if ks is rest else [], sel, [] if ks is rest else [across_in]
            )
            if ks is rest:
                sums = [chosen[0]] + [rotated(part, "tp", -k) for k, part in zip(ks[1:], chosen[1:])]
            else:
                sums = [rotated(part, "tp", -k) for k, part in zip(ks, chosen)]
                before = [partial_token, out_token]
    other_in, unused, in_token = assembled([got_in, across_in], sel, [partial_token])
    other_out, out_token, joined_token = assembled([got_out], sel, [in_token], COST)
    other = (other_in, other_out)
    mine_rows, unused = denoised(flat, sigma, alpha, sums, tokens, sel, [in_token, out_token])

    seen_parts = gather_parts(mine_rows)
    late_share, late_token = share(own[1], 2, sel, [joined_token])
    got_late = lax.ppermute(late_share, "sec", [(0, 1)])
    slopes1, pool = reward_forward(
        seen_parts, tokens, gains[1:], text_mine, own, other, sel, ()
    )
    pools = gather_parts(pool)
    g_parts, g_mean = reward_back(pools, slopes1, tokens, own, other, sel)

    *states, state_token = block0_state(
        lat_parts, gains[:1], own[0], other[0], sel, g_parts[:1]
    )

    g_sums = [g_parts[0]] + [rotated(g_parts[k], "tp", -k) for k in range(1, n_tp)]
    ratio = -(sigma / alpha)
    g_eps, eps_token = eps_gradient(
        mine_rows, g_mean, gains[1:], ratio, g_sums, tokens, sel, [state_token]
    )


    g_mine = gather_parts(g_eps)
    pieces = g_mine + [swapped(g_eps, "sec", 1)]
    arrived = [pieces[-1]]
    for ks in (near, rest[1:]):
        if ks:
            joined, token = joined_rows([g_mine[k] for k in ks], sel)
            pieces.append(swapped(joined, "sec", 1))
            arrived += [pieces[-1]] if ks is near else [token]
    late_out = assembled([got_late], sel, arrived, 1)[0]
    out_parts, in_parts = gradients(pieces, states, own[1], late_out, sel)
    grad_out, grad_in = sum_over_dp(*out_parts, sel), sum_over_dp(*in_parts, sel)
    return (grad_in, grad_out)


def solution(mesh):
    in_specs = (
        P(("dp", "tp"), None, None),
        P(("dp", "tp")),
        P(("dp", "tp")),
        P(),
        P(),
        P("sec", None, "tp"),
        P("sec", None, "tp"),
    )
    out_specs = (P(("sec", "dp"), "tp"), P(("sec", "dp"), "tp"))
    return jax.shard_map(
        on_device, mesh=mesh, in_specs=in_specs, out_specs=out_specs, check_vma=False
    )
```

```python
import functools
import math

import jax
import jax.numpy as jnp
from jax import lax
from jax.experimental import pallas as pl
from jax.experimental.pallas import tpu as pltpu
from jax.sharding import PartitionSpec as P

STEPS = 50


EPS = 1e-06
VMEM_BYTES = 8 * 1024 * 1024
COST = 10**11


def rotated(value, axis, steps):
    count = lax.axis_size(axis)
    return lax.ppermute(value, axis, [(i, (i + steps) % count) for i in range(count)])


def swapped(value, axis, bit):
    count = lax.axis_size(axis)
    return lax.ppermute(value, axis, [(i, i ^ bit) for i in range(count)])


def gather_parts(piece):
    return [piece] + [rotated(piece, "tp", k) for k in range(1, lax.axis_size("tp"))]


def gelu_pair(value):
    cdf = 0.5 * (1.0 + lax.erf(value * (1.0 / math.sqrt(2.0))))
    density = jnp.exp(-0.5 * value * value) * (1.0 / math.sqrt(2.0 * math.pi))
    return (value * cdf, cdf + value * density)


def normed(rows, gain):
    scale = lax.rsqrt(jnp.mean(rows * rows, axis=-1, keepdims=True) + EPS)
    return (rows * scale * gain).astype(jnp.bfloat16)


def dot_nn(a, b):
    return jnp.dot(a, b, preferred_element_type=jnp.float32)


def dot_nt(a, b):
    return lax.dot_general(a, b, (((1,), (1,)), ((), ())), preferred_element_type=jnp.float32)


def tile_of(hidden):
    for tile in (256, 128):
        if hidden % tile == 0:
            return tile
    return hidden


IN_VMEM = pl.BlockSpec(memory_space=pltpu.VMEM)
IN_SMEM = pl.BlockSpec(memory_space=pltpu.SMEM)


TOKEN = jax.ShapeDtypeStruct((8, 128), jnp.float32)


def run(body, name, sel, operands, outs, scratch, after=(), cost=COST):
    used, last = 1 + len(operands), 1 + len(operands) + len(after) + len(outs)

    def with_token(*refs):
        refs[last][...] = jnp.zeros(TOKEN.shape, TOKEN.dtype)
        body(*refs[:used], *refs[used + len(after) : last], *refs[last + 1 :])

    held = [math.prod(x.shape) * jnp.dtype(x.dtype).itemsize for x in scratch]
    return pl.pallas_call(
        with_token,
        in_specs=[IN_SMEM] + [IN_VMEM] * (len(operands) + len(after)),
        out_specs=[IN_VMEM] * (len(outs) + 1),
        scratch_shapes=scratch,
        out_shape=[*outs, TOKEN],
        compiler_params=pltpu.CompilerParams(vmem_limit_bytes=max(VMEM_BYTES, 4 * sum(held))),
        cost_estimate=pl.CostEstimate(
            flops=cost, bytes_accessed=cost // 200, transcendentals=0
        ),
        name=name,
    )(sel, *operands, *after)


def bf16(*shape):
    return jax.ShapeDtypeStruct(shape, jnp.bfloat16)


def tiles(hidden):
    tile = tile_of(hidden)
    return [slice(t, t + tile) for t in range(0, hidden, tile)]


def by_section(sel_ref, section, work, own, other):
    @pl.when(sel_ref[0] == section)
    def _():
        work(*own)

    @pl.when(sel_ref[0] != section)
    def _():
        work(*other)


def share_body(group, sel_ref, weight, out):
    rows = out.shape[0]
    start = pl.multiple_of((sel_ref[3] % group) * rows, rows)
    out[...] = weight[pl.ds(start, rows), :]


def share(weight, group, sel, after):
    rows, hidden = weight.shape
    body = functools.partial(share_body, group)
    return run(body, "share", sel, [weight], [bf16(rows // group, hidden)], [], after)


def relay_body(sel_ref, value, out):
    out[...] = value[...]


def relayed(value, sel, after):
    return run(relay_body, "relay", sel, [value], [bf16(*value.shape)], [], after)


def join_body(sel_ref, *refs):
    rows = refs[0].shape[0]
    for i, piece in enumerate(refs[:-1]):
        refs[-1][i * rows : (i + 1) * rows, :] = piece[...]


def joined_rows(pieces, sel):
    out = bf16(sum(piece.shape[0] for piece in pieces), pieces[0].shape[1])
    return run(join_body, "join", sel, pieces, [out], [], (), 1)


def stack_body(sel_ref, *refs):
    for i, piece in enumerate(refs[:-1]):
        refs[-1][i] = piece[...]


def assemble_body(count, sel_ref, *refs):
    pieces, beside, out = refs[:count], refs[count], refs[count + 1]
    rows = pieces[0].shape[0]
    for i, piece in enumerate(pieces):
        for q, value in ((2 * i, piece[...]), (2 * i + 1, beside[i])):
            place = (sel_ref[3] % (2 * count)) ^ q
            out[pl.ds(pl.multiple_of(place * rows, rows), rows), :] = value


def assembled(pieces, sel, after, cost=COST):
    rows, hidden = pieces[0].shape
    count = len(pieces)
    out = bf16(count, rows, hidden)
    stacked = run(stack_body, "stack", sel, pieces, [out], [], after, cost)[0]
    beside = swapped(stacked, "dp", 1)
    body = functools.partial(assemble_body, count)
    out = bf16(2 * count * rows, hidden)
    return run(body, "assemble", sel, [*pieces, beside], [out], [], (), cost)


def partial_body(count, sel_ref, *refs):
    parts, (gain, w_in, w_out) = refs[:count], refs[count : count + 3]
    stay, leave, xn, acc = refs[count + 3 :]
    rows = parts[0].shape[0]
    late = rows // 2
    for i, part in enumerate(parts):
        xn[i * rows : (i + 1) * rows, :] = normed(part[...].astype(jnp.float32), gain[...])
    for t, tile in enumerate(tiles(w_in.shape[1])):
        act, unused = gelu_pair(dot_nn(xn[...], w_in[:, tile]))
        term = dot_nt(act.astype(jnp.bfloat16), w_out[:, tile])
        acc[...] = term if t == 0 else acc[...] + term
    for i in range(count):
        start = i * rows
        leave[i] = acc[start : start + late, :].astype(jnp.bfloat16)
        stay[i] = acc[start + late : start + rows, :].astype(jnp.bfloat16)


def block0_partials(parts, gain, w_in, w_out, sel, after):
    rows, width = parts[0].shape
    hidden, n = w_in.shape[1], len(parts)
    return run(
        functools.partial(partial_body, n),
        "block0_partial",
        sel,
        [*parts, gain, w_in, w_out],
        [bf16(n, rows // 2, width)] * 2,
        [
            pltpu.VMEM((n * rows, width), jnp.bfloat16),
            pltpu.VMEM((n * rows, width), jnp.float32),
        ],
        after,
    )


def pick_body(count, sel_ref, *refs):
    stay, crossed = refs[:2]
    arrived, outs = refs[2 : 2 + count], refs[2 + count :]
    for i, out in enumerate(outs):
        value = jnp.where(sel_ref[0] == 0, stay[i], crossed[i])
        if count and i == 0:
            value = value.astype(jnp.float32)
            for part in arrived:
                value = value + part[...].astype(jnp.float32)
        out[...] = value


def picked(stay, crossed, arrived, sel):
    count, rows, width = stay.shape
    outs = [bf16(rows, width)] * count
    if arrived:
        outs[0] = jax.ShapeDtypeStruct((rows, width), jnp.float32)
    body = functools.partial(pick_body, len(arrived))
    *chosen, token = run(body, "pick", sel, [stay, crossed, *arrived], outs, [])
    return chosen, token


def denoise_body(tokens, count, sel_ref, *refs):
    latents, sigma, alpha = refs[:3]
    sums, out = refs[3 : 3 + count], refs[3 + count]
    late = out.shape[0]
    base = latents[pl.ds(pl.multiple_of((1 - sel_ref[0]) * late, late), late), :]
    base = base.astype(jnp.float32)
    eps = base
    for part in sums:
        eps = eps + part[...].astype(jnp.float32)
    out[...] = ((base - sigma[...] * eps) / alpha[...]).astype(jnp.bfloat16)


def denoised(latents, sigma, alpha, sums, tokens, sel, after):
    return run(
        functools.partial(denoise_body, tokens, len(sums)),
        "denoise",
        sel,
        [latents, sigma, alpha, *sums],
        [bf16(latents.shape[0] // 2, latents.shape[1])],
        [],
        after,
    )[:2]


def crossing(count):
    near = [k for k in range(1, count) if 2 * k != count]
    return [0] + near + [k for k in range(1, count) if 2 * k == count]


def state_body(count, sel_ref, *refs):
    parts = refs[:count]
    gain, own, other, act, slope, xn_cols, xn = refs[count:]
    rows = parts[0].shape[0]
    late = rows // 2
    share = xn_cols.shape[0]
    mine = pl.multiple_of((1 - sel_ref[0]) * late, late)
    theirs = pl.multiple_of(sel_ref[0] * late, late)
    at = 0
    for start, order in ((mine, range(len(parts))), (theirs, crossing(len(parts)))):
        for k in order:
            rows_k = parts[k][pl.ds(start, late), :].astype(jnp.float32)
            xn[at : at + late, :] = normed(rows_k, gain[...])
            at += late
    cols = xn[:, pl.ds(pl.multiple_of(sel_ref[0] * share, share), share)]
    xn_cols[...] = cols.T

    def work(weight):
        for tile in tiles(weight.shape[1]):
            value, grad = gelu_pair(dot_nn(xn[...], weight[:, tile]))
            act[:, tile] = value.astype(jnp.bfloat16)
            slope[:, tile] = grad.astype(jnp.bfloat16)

    by_section(sel_ref, 0, work, (own,), (other,))


def block0_state(parts, gain, own, other, sel, after):
    total, width = sum(part.shape[0] for part in parts), parts[0].shape[1]
    hidden = own.shape[1]
    return run(
        functools.partial(state_body, len(parts)),
        "block0_state",
        sel,
        [*parts, gain, own, other],
        [bf16(total, hidden), bf16(total, hidden), bf16(width // 2, total)],
        [pltpu.VMEM((total, width), jnp.bfloat16)],
        after,
    )


def reward_body(count, tokens, sel_ref, *refs):
    parts, (gain, text) = refs[:count], refs[count : count + 2]
    own_in, own_out, other_in, other_out = refs[count + 2 : count + 6]
    slopes, (pool, xn) = refs[count + 6 : 2 * count + 6], refs[2 * count + 6 :]
    rows = parts[0].shape[0]
    half = rows // tokens
    row = lax.broadcasted_iota(jnp.int32, pool.shape, 0)
    start = jnp.zeros(pool.shape, jnp.float32)
    for image in range(half):
        own_rows = parts[0][image * tokens : (image + 1) * tokens, :].astype(jnp.float32)
        start = jnp.where(row == image, jnp.mean(own_rows, axis=0, keepdims=True), start)
        start = jnp.where(row == count * half + image, text[image : image + 1, :], start)
    pool[...] = start
    for i, part in enumerate(parts):
        xn[i * rows : (i + 1) * rows, :] = normed(part[...].astype(jnp.float32), gain[...])

    def work(w_in, w_out):
        for tile in tiles(w_in.shape[1]):
            act, grad = gelu_pair(dot_nn(xn[...], w_in[:, tile]))
            for i in range(count):
                slopes[i][:, tile] = grad[i * rows : (i + 1) * rows, :].astype(jnp.bfloat16)
            means = [
                jnp.mean(act[at : at + tokens, :], axis=0, keepdims=True)
                for at in range(0, count * rows, tokens)
            ]
            place = lax.broadcasted_iota(jnp.int32, (pool.shape[0], act.shape[1]), 0)
            stacked = jnp.zeros(place.shape, jnp.float32)
            for i, mean in enumerate(means):
                stacked = jnp.where(place == i, mean, stacked)
            pool[...] += dot_nt(stacked.astype(jnp.bfloat16), w_out[:, tile])

    by_section(sel_ref, 1, work, (own_in, own_out), (other_in, other_out))


def reward_forward(parts, tokens, gain, text, own, other, sel, after):
    rows, width = parts[0].shape
    hidden, n = own[0].shape[1], len(parts)
    images = (n + 1) * rows // tokens
    outs = run(
        functools.partial(reward_body, n, tokens),
        "reward_forward",
        sel,
        [*parts, gain, text, *own, *other],
        [bf16(rows, hidden)] * n
        + [jax.ShapeDtypeStruct((-(-images // 8) * 8, width), jnp.float32)],
        [pltpu.VMEM((n * rows, width), jnp.bfloat16)],
        after,
    )
    return outs[:n], outs[n]


def score_gradient(pooled, text):
    unit = text * lax.rsqrt(jnp.mean(text * text, axis=-1, keepdims=True) + EPS)
    scale = lax.rsqrt(jnp.mean(pooled * pooled, axis=-1, keepdims=True) + EPS)
    along = jnp.mean(pooled * unit, axis=-1, keepdims=True)
    return (-100.0 / pooled.shape[-1]) * (scale * unit - pooled * scale**3 * along)


def back_body(count, tokens, sel_ref, *refs):
    pools, slopes = refs[:count], refs[count : 2 * count]
    own_in, own_out, other_in, other_out = refs[2 * count : 2 * count + 4]
    outs = refs[2 * count + 4 : 3 * count + 4]
    g_mean, acc = refs[3 * count + 4 :]
    rows = slopes[0].shape[0]
    half = rows // tokens
    images = count * half
    pooled, texts = [], []
    for j in range(images):
        at = [(j - k * half) % images for k in range(count)]
        pooled.append(sum(pools[k][at[k] : at[k] + 1, :] for k in range(count)))
        text = images + j % half
        texts.append(pools[j // half][text : text + 1, :])
    padded = -(-images // 16) * 16
    row = lax.broadcasted_iota(jnp.int32, (padded, acc.shape[1]), 0)
    stacked, spoken = jnp.zeros(row.shape, jnp.float32), jnp.zeros(row.shape, jnp.float32)
    for j in range(images):
        stacked = jnp.where(row == j, pooled[j], stacked)
        spoken = jnp.where(row == j, texts[j], spoken)
    g_all = score_gradient(stacked, spoken) * (1.0 / tokens)
    g_mean[...] = g_all[: g_mean.shape[0], :]
    g_tok = g_all.astype(jnp.bfloat16)

    def work(w_in, w_out):
        for t, tile in enumerate(tiles(w_in.shape[1])):
            g_h = dot_nn(g_tok, w_out[:, tile])
            terms = []
            for i in range(count):
                for image in range(half):
                    at = i * half + image
                    slope = slopes[i][image * tokens : (image + 1) * tokens, tile]
                    terms.append(
                        (slope.astype(jnp.float32) * g_h[at : at + 1, :]).astype(jnp.bfloat16)
                    )
            term = dot_nt(jnp.concatenate(terms, axis=0), w_in[:, tile])
            acc[...] = term if t == 0 else acc[...] + term

    by_section(sel_ref, 1, work, (own_in, own_out), (other_in, other_out))
    for i, out in enumerate(outs):
        out[...] = acc[i * rows : (i + 1) * rows, :].astype(jnp.bfloat16)


def reward_back(pools, slopes, tokens, own, other, sel):
    rows, hidden = slopes[0].shape
    width, n = own[0].shape[0], len(slopes)
    outs = run(
        functools.partial(back_body, n, tokens),
        "reward_back",
        sel,
        [*pools, *slopes, *own, *other],
        [bf16(rows, width)] * n + [jax.ShapeDtypeStruct((8, width), jnp.float32)],
        [pltpu.VMEM((n * rows, width), jnp.float32)],
    )
    return outs[:n], outs[n]


def eps_gradient_body(tokens, count, sel_ref, *refs):
    seen_ref, g_mean, gain, ratio = refs[:4]
    sums, out = refs[4 : 4 + count], refs[4 + count]
    g_xn = sums[0][...].astype(jnp.float32)
    for part in sums[1:]:
        g_xn = g_xn + part[...].astype(jnp.float32)
    seen = seen_ref[...].astype(jnp.float32)
    scale = lax.rsqrt(jnp.mean(seen * seen, axis=-1, keepdims=True) + EPS)
    weighted = gain[...] * g_xn
    along = jnp.mean(seen * weighted, axis=-1, keepdims=True)
    g_norm = scale * weighted - seen * scale**3 * along
    for image in range(out.shape[0] // tokens):
        at = slice(image * tokens, (image + 1) * tokens)
        g_images = (g_mean[image : image + 1, :] + g_norm[at, :]).astype(jnp.bfloat16)
        out[at, :] = (ratio[at, :] * g_images.astype(jnp.float32)).astype(jnp.bfloat16)


def eps_gradient(seen, g_mean, gain, ratio, sums, tokens, sel, after):
    return run(
        functools.partial(eps_gradient_body, tokens, len(sums)),
        "eps_gradient",
        sel,
        [seen, g_mean, gain, ratio, *sums],
        [bf16(*seen.shape)],
        [],
        after,
    )


def put_rows(result, core, keep, away, tile):
    groups, rows, unused = keep.shape
    for g in range(groups):
        even = result[2 * g * rows : (2 * g + 1) * rows, :]
        odd = result[(2 * g + 1) * rows : (2 * g + 2) * rows, :]
        keep[g, :, tile] = jnp.where(core == 0, even, odd).astype(jnp.bfloat16)
        away[g, :, tile] = jnp.where(core == 0, odd, even).astype(jnp.bfloat16)


def gradient_body(count, sel_ref, *refs):
    pieces = refs[:count]
    act, slope, xn_cols, own, other = refs[count : count + 5]
    out_keep, out_away, in_keep, in_away, g_all, turned = refs[count + 5 :]
    share = turned.shape[0]
    core = sel_ref[1]
    at = 0
    for piece in pieces:
        g_all[at : at + piece.shape[0], :] = piece[...]
        at += piece.shape[0]
    cols = g_all[:, pl.ds(pl.multiple_of(sel_ref[0] * share, share), share)]
    turned[...] = cols.T

    def work(weight):
        for tile in tiles(weight.shape[1]):
            put_rows(dot_nn(turned[...], act[:, tile]), core, out_keep, out_away, tile)
            g_h = dot_nn(g_all[...], weight[:, tile])
            g_hidden = (g_h * slope[:, tile].astype(jnp.float32)).astype(jnp.bfloat16)
            put_rows(dot_nn(xn_cols[...], g_hidden), core, in_keep, in_away, tile)

    by_section(sel_ref, 0, work, (own,), (other,))


def gradients(pieces, states, own, other, sel):
    total, width = sum(piece.shape[0] for piece in pieces), pieces[0].shape[1]
    hidden = own.shape[1]
    groups = lax.axis_size("dp") // 2
    outs = run(
        functools.partial(gradient_body, len(pieces)),
        "gradients",
        sel,
        [*pieces, *states, own, other],
        [bf16(groups, width // 2 // (2 * groups), hidden)] * 4,
        [
            pltpu.VMEM((total, width), jnp.bfloat16),
            pltpu.VMEM((width // 2, total), jnp.bfloat16),
        ],
    )
    return outs[:2], outs[2:4]


def chip_body(sel_ref, keep, arrived, mine, others):
    groups = keep.shape[0]
    for k in range(groups):
        at = (sel_ref[2] + k) % groups
        total = keep[at].astype(jnp.float32) + arrived[at].astype(jnp.float32)
        if k == 0:
            mine[...] = total
        else:
            others[k - 1] = total.astype(jnp.bfloat16)


def sum_over_dp(keep, away, sel):
    groups, rows, hidden = keep.shape
    total, others, unused = run(
        chip_body,
        "chip_sum",
        sel,
        [keep, swapped(away, "dp", 1)],
        [jax.ShapeDtypeStruct((rows, hidden), jnp.float32), bf16(groups - 1, rows, hidden)],
        [],
    )
    for k in range(1, groups):
        total = total + rotated(others[k - 1], "dp", 2 * k).astype(jnp.float32)
    return total


def on_device(latents, timesteps, prompt_ids, prompt_table, gains, w_in, w_out):
    count, tokens, width = latents.shape
    half = count // 2
    n_tp = lax.axis_size("tp")
    segment = lax.axis_index("sec")
    first = segment == 0
    dp = lax.axis_index("dp")
    sel = jnp.stack([segment, dp % 2, dp // 2, dp % 4]).astype(jnp.int32)
    own = (w_in[0], w_out[0])

    def my_half(value):
        return jnp.where(first, value[half:], value[:half])

    theta = math.pi / 2.0 * (my_half(timesteps).astype(jnp.float32) + 1.0) / (STEPS + 1.0)
    theta = jnp.repeat(theta, tokens)[:, None]
    alpha, sigma = jnp.cos(theta), jnp.sin(theta)

    flat = latents.reshape(count * tokens, width)
    near = [k for k in range(1, n_tp) if 2 * k != n_tp]
    rest = [0] + [k for k in range(1, n_tp) if 2 * k == n_tp]
    lat_parts = [flat] + [None] * (n_tp - 1)
    for k in near:
        lat_parts[k] = rotated(flat, "tp", k)
    again, near_token = relayed(flat, sel, [lat_parts[k] for k in near])
    for k in rest[1:]:
        lat_parts[k] = rotated(again, "tp", k)
    got_in = swapped(share(own[0], 4, sel, ())[0], "sec", 1)
    got_again, in_token = relayed(got_in, sel, [near_token])
    across_in = swapped(got_again, "dp", 2)
    out_share, out_token = share(own[1], 2, sel, [near_token])
    got_out = lax.ppermute(out_share, "sec", [(1, 0)])

    onehot = (
        my_half(prompt_ids)[:, None] == jnp.arange(prompt_table.shape[0], dtype=jnp.int32)[None, :]
    ).astype(jnp.bfloat16)
    text_mine = dot_nn(onehot, prompt_table)

    sums, before = [], [in_token]
    for ks in (near, rest):
        if ks:
            stay, leave, partial_token = block0_partials(
                [lat_parts[k] for k in ks], gains[:1], *own, sel, before
            )
            crossed = lax.ppermute(leave, "sec", [(0, 1)])
            chosen, picked_token = picked(stay, crossed, sums if ks is rest else [], sel)
            if ks is rest:
                sums = [chosen[0]] + [rotated(part, "tp", -k) for k, part in zip(ks[1:], chosen[1:])]
            else:
                sums = [rotated(part, "tp", -k) for k, part in zip(ks, chosen)]
                before = [partial_token, out_token]
    other_in, in_token = assembled([got_in, across_in], sel, [partial_token])
    mine_rows, unused = denoised(flat, sigma, alpha, sums, tokens, sel, [in_token])

    seen_parts = gather_parts(mine_rows)
    near_seen = [seen_parts[k] for k in near]
    other_out, joined_token = assembled([got_out], sel, near_seen)
    other = (other_in, other_out)
    late_share, late_token = share(own[1], 2, sel, [joined_token])
    got_late = lax.ppermute(late_share, "sec", [(0, 1)])
    slopes1, pool = reward_forward(
        seen_parts, tokens, gains[1:], text_mine, own, other, sel, [late_token]
    )
    pools = gather_parts(pool)
    g_parts, g_mean = reward_back(pools, slopes1, tokens, own, other, sel)

    *states, state_token = block0_state(
        lat_parts, gains[:1], own[0], other[0], sel, g_parts[:1]
    )

    g_sums = [g_parts[0]] + [rotated(g_parts[k], "tp", -k) for k in range(1, n_tp)]
    ratio = -(sigma / alpha)
    g_eps, eps_token = eps_gradient(
        mine_rows, g_mean, gains[1:], ratio, g_sums, tokens, sel, [state_token]
    )


    g_mine = gather_parts(g_eps)
    pieces = g_mine + [swapped(g_eps, "sec", 1)]
    arrived = [pieces[-1]]
    for ks in (near, rest[1:]):
        if ks:
            joined, token = joined_rows([g_mine[k] for k in ks], sel)
            pieces.append(swapped(joined, "sec", 1))
            arrived += [pieces[-1]] if ks is near else [token]
    late_out = assembled([got_late], sel, arrived, 1)[0]
    out_parts, in_parts = gradients(pieces, states, own[1], late_out, sel)
    grad_out, grad_in = sum_over_dp(*out_parts, sel), sum_over_dp(*in_parts, sel)
    return (grad_in, grad_out)


def solution(mesh):
    in_specs = (
        P(("dp", "tp"), None, None),
        P(("dp", "tp")),
        P(("dp", "tp")),
        P(),
        P(),
        P("sec", None, "tp"),
        P("sec", None, "tp"),
    )
    out_specs = (P(("sec", "dp"), "tp"), P(("sec", "dp"), "tp"))
    return jax.shard_map(
        on_device, mesh=mesh, in_specs=in_specs, out_specs=out_specs, check_vma=False
    )
```
